32 devices in a mesh: cls: 4 (over x, core), ori: 8 (over z, y).
Axes of the slice: x: 2, y: 2, z: 4, core: 2. Of those that a mesh axis runs over, the one named last changes fastest.
Arguments:
- images: bfloat16 [512, 20480], P('ori'), may hold values from -6 to 6
- projections: bfloat16 [4, 1152, 20480], P('cls', 'ori'), may hold values from -0.0390625 to 0.0390625
- log_prior: float32 [4, 1152], P('cls', 'ori'), may hold values from -4 to 300
- significant: int32 [512, 4], P('ori'), may hold values from 0 to 7, all different within a row; in each aligned block of 64 rows (0 to 63, 64 to 127, ...) at most 48 rows name the same one
- shell_index: int32 [20480], replicated, may hold values from 0 to 99
- noise_inv: float32 [100], replicated, may hold values from 0.5 to 4
Outputs:
- class_sums: bfloat16 [4, 1152, 20480], P('cls', None, 'ori')
- log_evidence: float32 [512], P('ori')
The draws below stay inside these ranges and needn't reach their ends.
Inputs may be any that keep to these rules, and one draw needn't show every extreme that they name: `significant`: each row names 4 different blocks. Among the rows of one index of ori no block is named more than 48 times, and some block is named exactly 48 times.
All inputs are finite; a program needn't handle non-finite values.
Results may differ from the reference program's by a relative error of at most 0.0076.
Values may be sent and summed in bfloat16 or wider, within the bound.
No kernel may reach another device: no remote copies, remote signals or barrier semaphores. Data moves between devices by JAX's collectives and lax.ppermute only.
A program may use at most 128 MiB of HBM per device.

```python
import math
import jax
import jax.numpy as jnp
import numpy as np
from jax import lax

FREQS = 20480
SHELLS = 100
LISTED = 4
ORI_DEV = 144
IMG_DEV = 64
CAPACITY = 48
CLASSES = 4
ORIENTS = 1152
IMAGES = 512
N_ORI = 8


def draw_log_prior(key, part):
    base_key = jax.random.fold_in(jax.random.fold_in(key, 11), 0)
    baseline = jnp.clip(jax.random.normal(base_key, (CLASSES, ORIENTS), jnp.float32), -4.0, 4.0)
    return baseline


def set_ends(entries, key, low, largest):
    longest = entries.shape.index(max(entries.shape))
    spots = []
    for shift in (0, 1):
        where = [jax.random.randint(jax.random.fold_in(key, axis), (), 0, length) for axis, length in enumerate(entries.shape)]
        where[longest] = (where[longest] + shift) % entries.shape[longest]
        spots.append(tuple(where))
    return entries.at[spots[0]].set(low).at[spots[1]].set(largest)


def steps_of(key, extent, pieces, least, high):
    def one(position, shards_of):
        heights = jax.random.uniform(jax.random.fold_in(jax.random.fold_in(key, 6), position), (shards_of,), jnp.float32, least / len(pieces), high / len(pieces))
        return jnp.repeat(jnp.exp(heights), extent[position] // shards_of).reshape((-1,) + (1,) * (len(extent) - position - 1))

    level = one(*pieces[0])
    for cut in pieces[1:]:
        level = level * one(*cut)
    return level


def shared_out(rng, own, number, rows, count, top, limit, lean):
    order = jax.random.permutation(rng, count)
    crowded, common = portions_of(count, rows * top, limit, lean, True), portions_of(count, rows * top, limit, lean, False)
    places = jnp.arange(count)

    def named(sizes, offset_by):
        used = int((sizes > 0).sum())
        fixed = max(1, used // 4)
        moved = fixed + (places - fixed + offset_by * (used - fixed)) % max(1, count - fixed)
        return jnp.zeros((count,), jnp.int32).at[order[jnp.where(places < fixed, places, moved)]].set(jnp.asarray(sizes, jnp.int32))

    sizes = jnp.where(number % 4 == 0, named(crowded, number // 4), named(common, number - number // 4 - 1))
    mixed = jax.random.permutation(jax.random.fold_in(own, 3), count)
    donor, sink = mixed[0:count // 2 * 2:2], mixed[1:count // 2 * 2:2]
    margin = jnp.minimum(sizes[donor] - 1, limit - sizes[sink]) // 2
    margin = jnp.where((donor == order[0]) | (sink == order[0]) | (sizes[sink] == 0), 0, jnp.maximum(margin, 0))
    moved = jax.random.randint(jax.random.fold_in(own, 4), (count // 2,), 0, 1 << 20) % (margin + 1)
    sizes = sizes.at[donor].add(-moved).at[sink].add(moved)
    items = jnp.searchsorted(jnp.cumsum(sizes), jnp.arange(rows * top), side="right").astype(jnp.int32)
    table = items.reshape(top, rows).T
    table = table[jax.random.permutation(jax.random.fold_in(own, 1), rows)]
    offset_by = jax.random.randint(jax.random.fold_in(own, 2), (rows, 1), 0, top)
    return jnp.take_along_axis(table, (jnp.arange(top)[None, :] + offset_by) % top, axis=1)


def portions_of(number_of, total, most, slope, full):
    portions = [(1 << 20) // math.isqrt(rank ** slope) + 1 for rank in range(1, number_of + 1)]
    largest = most if full else min(most, max(-(-total // number_of), total * portions[0] // sum(portions)))
    least = 1 if total - largest >= number_of - 1 else 0
    counts, spare = [largest] + [least] * (number_of - 1), total - largest - least * (number_of - 1)
    while spare > 0:
        movable = [i for i in range(1, number_of) if counts[i] < largest] or [i for i in range(1, number_of) if counts[i] < most]
        pool, left = sum([portions[i] for i in movable]), spare
        for i in movable:
            addition = min(most - counts[i], max(1, left * portions[i] // pool), spare)
            counts[i] = counts[i] + addition
            spare = spare - addition
    return np.array(counts)


def bell_draw(rng, extent, width, limit, shards=(), kind=jnp.bfloat16):
    drawn = jax.random.normal(rng, extent, jnp.float32) * width
    if len(shards) > 0:
        drawn = steps_of(rng, extent, shards, -0.22, 0.18) * drawn
    return jnp.clip(drawn, min=-limit, max=limit).astype(kind)


def setup_inputs(seed: int = 0) -> dict:
    arg_keys = jax.random.split(jax.random.key(seed), 7)
    images = bell_draw(arg_keys[0], (IMAGES, FREQS), 1.0, 6.0, ((0, 8),))
    projections = bell_draw(arg_keys[1], (CLASSES, ORIENTS, FREQS), FREQS ** -0.5, 0.0390625, ((0, 4), (1, 8)))
    log_prior = draw_log_prior(jax.random.fold_in(arg_keys[6], 71), 0)
    significant_keys = jax.random.split(jax.random.fold_in(arg_keys[3], 1), IMAGES // IMG_DEV)
    significant_turns = jax.random.permutation(jax.random.fold_in(arg_keys[3], 3), IMAGES // IMG_DEV)
    significant = jax.vmap(lambda own, number: shared_out(jax.random.fold_in(arg_keys[3], 2), own, number, IMG_DEV, N_ORI, LISTED, CAPACITY, 2))(significant_keys, significant_turns).reshape((IMAGES, LISTED))
    shell_index = set_ends(jax.random.randint(arg_keys[4], (FREQS,), 0, SHELLS), jax.random.fold_in(arg_keys[4], 1), 0, SHELLS - 1).astype(jnp.int32)
    noise_inv = jnp.clip(jnp.exp(jax.random.uniform(arg_keys[5], (SHELLS,), jnp.float32, math.log(0.5), math.log(4.0))), 0.5, 4.0)
    return {"images": images, "projections": projections, "log_prior": log_prior, "significant": significant, "shell_index": shell_index, "noise_inv": noise_inv}


SENTINEL = -1e30


def shell_weights(noise_inv, shell_index):
    levels = jnp.arange(noise_inv.shape[0], dtype=jnp.int32)
    table = (shell_index[:, None] == levels[None, :]).astype(jnp.float32)
    return jnp.sum(table * noise_inv[None, :].astype(jnp.float32), axis=1)


def reference(images, projections, log_prior, significant, shell_index, noise_inv):
    weight = shell_weights(noise_inv, shell_index)
    weighted = (images.astype(jnp.float32) * weight[None, :]).astype(jnp.bfloat16)
    weighted_wide = weighted.astype(jnp.float32)
    blocks = jnp.arange(N_ORI, dtype=jnp.int32)
    listed_mask = jnp.any(significant[:, :, None] == blocks[None, None, :], axis=1)
    column_mask = jnp.repeat(listed_mask, ORI_DEV, axis=1)

    def class_scores(inputs):
        projection, prior_row = inputs
        wide = projection.astype(jnp.float32)
        half_norm = 0.5 * jnp.sum(wide * wide * weight[None, :], axis=1)
        scores = jnp.dot(weighted_wide, wide.T, preferred_element_type=jnp.float32)
        scores = scores - half_norm[None, :] + prior_row[None, :]
        return jnp.where(column_mask, scores, SENTINEL)

    scores = lax.map(class_scores, (projections, log_prior))
    highest = jnp.max(jnp.max(scores, axis=2), axis=0)
    shifted = jnp.where(column_mask[None], jnp.exp(scores - highest[None, :, None]), 0.0)
    totals = jnp.sum(jnp.sum(shifted, axis=2), axis=0)
    log_evidence = highest + jnp.log(totals)

    def sums_of_class(class_scores_one):
        posterior = jnp.where(column_mask, jnp.exp(class_scores_one - highest[:, None]) / totals[:, None], 0.0)
        posterior = posterior.astype(jnp.bfloat16).astype(jnp.float32)
        return jnp.dot(posterior.T, weighted_wide, preferred_element_type=jnp.float32).astype(jnp.bfloat16)

    class_sums = lax.map(sums_of_class, scores)
    return class_sums, log_evidence
```

```python
import functools
import math

import jax
import jax.numpy as jnp
from jax import lax
from jax.experimental import pallas as pl
from jax.experimental.pallas import tpu as pltpu
from jax.sharding import PartitionSpec as P

BF16 = jnp.bfloat16
F32 = jnp.float32
MASKED = -1e30
LANES = 128
MIB = 1 << 20


def cycle_of(count):
    deep = math.isqrt(count // 2)
    tall = count // deep
    walk = [(z, 0) for z in range(tall)]
    for z in range(tall - 1, -1, -1):
        cols = list(range(1, deep))
        walk += [(z, y) for y in (cols if (tall - 1 - z) % 2 == 0 else cols[::-1])]
    return [z * deep + y for z, y in walk]


def weight_table(index, noise):
    levels = noise.shape[1]
    row = jnp.concatenate([noise, jnp.zeros((1, LANES - levels), F32)], axis=1)
    table = jnp.broadcast_to(row, index.shape)
    return jnp.take_along_axis(table, index, axis=1, mode="promise_in_bounds")


def at(start, size):
    return pl.ds(pl.multiple_of(start, LANES), size)


def image_kernel(n, wo, ws, img_ref, index_ref, noise_ref, sig_ref, own_ref, oth_ref, sh_ref, w_ref):
    cls = lax.axis_index("cls")
    core, side = cls % 2, (cls // 2) % 2
    half = 2 * wo + ws
    w_ref[...] = weight_table(index_ref[...], noise_ref[...])
    for i in range(n):
        base = (2 * i + core) * half
        for ref, start, count, spot in (
            (own_ref, base + side * wo, wo, i * wo),
            (oth_ref, base + (1 - side) * wo, wo, i * wo),
            (sh_ref, base + 2 * wo, ws, i * ws),
        ):
            for j in range(0, count, LANES):
                weight = w_ref[pl.ds(start // LANES + j // LANES, 1), :]
                wide = img_ref[:, at(start + j, LANES)].astype(F32) * weight
                ref[:, spot + j : spot + j + LANES] = wide.astype(BF16)
    rows = img_ref.shape[0]
    block = lax.broadcasted_iota(jnp.int32, (LANES, rows), 0)
    listed = block < 0
    for j in range(sig_ref.shape[0]):
        listed = listed | (sig_ref[j : j + 1, :] == block)
    unlisted = jnp.where(listed, 0.0, 1.0).astype(BF16)
    same = lax.broadcasted_iota(jnp.int32, (rows, rows), 0) == lax.broadcasted_iota(jnp.int32, (rows, rows), 1)
    eye = jnp.where(same, 1.0, 0.0).astype(BF16)
    turned = lax.dot_general(eye, unlisted, (((1,), (1,)), ((), ())), preferred_element_type=F32)
    own_ref[:, n * wo :] = turned.astype(BF16)


def prep_images(images, weight_of, significant, core, side, wo, ws, n):
    rows = images.shape[0]
    half = 2 * wo + ws
    if wo % LANES == 0:
        index, noise = weight_of
        out = [
            jax.ShapeDtypeStruct((rows, n * wo + LANES), BF16),
            jax.ShapeDtypeStruct((rows, n * wo), BF16),
            jax.ShapeDtypeStruct((rows, n * ws), BF16),
        ]
        vmem = pl.BlockSpec(memory_space=pltpu.VMEM)
        return pl.pallas_call(
            functools.partial(image_kernel, n, wo, ws),
            in_specs=[vmem] * 4,
            out_specs=[vmem] * 3,
            out_shape=out,
            scratch_shapes=[pltpu.VMEM(index.shape, F32)],
            compiler_params=pltpu.CompilerParams(vmem_limit_bytes=32 * MIB),
            name="prep_images",
        )(images, index, noise, significant.T)
    weight = full_weights(weight_of)
    weighted = (images.astype(F32) * weight).astype(BF16).reshape(rows, n, 2, half)
    mine = lax.dynamic_index_in_dim(weighted, core, 2, keepdims=False)
    own, oth, shared = cut(mine, side, wo)
    lane = jnp.arange(LANES, dtype=jnp.int32)
    listed = jnp.any(significant[:, :, None] == lane[None, None, :], axis=1)
    return jnp.concatenate([own, jnp.where(listed, 0.0, 1.0).astype(BF16)], axis=1), oth, shared


def full_weights(weight_of):
    index, noise = weight_of
    levels = jnp.arange(noise.shape[1], dtype=jnp.int32)
    return jnp.sum(jnp.where(index.reshape(-1, 1) == levels[None, :], noise, 0.0), axis=1)[None, :]


def cut(mine, side, wo):
    rows, n, _ = mine.shape
    own = lax.dynamic_slice_in_dim(mine, side * wo, wo, 2).reshape(rows, n * wo)
    oth = lax.dynamic_slice_in_dim(mine, (1 - side) * wo, wo, 2).reshape(rows, n * wo)
    return own, oth, mine[:, :, 2 * wo :].reshape(rows, -1)


def projection_kernel(wo, ws, n, proj_ref, index_ref, noise_ref, prior_ref, keep_ref, send_ref, bias_ref, acc, w_ref):
    step = pl.program_id(0)
    half = 2 * wo + ws
    cls, owner = lax.axis_index("cls"), lax.axis_index("ori")
    core, side = cls % 2, (cls // 2) % 2

    @pl.when(step == 0)
    def _():
        acc[...] = jnp.zeros_like(acc)
        w_ref[...] = weight_table(index_ref[...], noise_ref[...])
        lane = lax.broadcasted_iota(jnp.int32, (proj_ref.shape[0], LANES), 1)
        gate = jnp.where(lane == owner, MASKED, 0.0).astype(BF16)
        keep_ref[:, n * wo : n * wo + LANES] = gate
        send_ref[:, n * wo : n * wo + LANES] = gate

    total = acc[...]
    for j in range(2 * half // LANES):
        weight = w_ref[pl.ds(step * (2 * half // LANES) + j, 1), :]
        wide = proj_ref[:, j * LANES : (j + 1) * LANES].astype(F32)
        total = total + wide * wide * weight
    acc[...] = total
    for ref, which in ((keep_ref, core), (send_ref, 1 - core)):
        base = which * half
        ref[:, at(step * wo, wo)] = proj_ref[:, at(base + side * wo, wo)]
        ref[:, at(n * wo + LANES + step * wo, wo)] = proj_ref[:, at(base + (1 - side) * wo, wo)]
        ref[:, at(2 * n * wo + LANES + step * ws, ws)] = proj_ref[:, at(base + 2 * wo, ws)]

    @pl.when(step == pl.num_programs(0) - 1)
    def _():
        half_norm = 0.5 * jnp.sum(acc[...], axis=1, keepdims=True)
        bias_ref[...] = jnp.broadcast_to(prior_ref[...] - half_norm, bias_ref.shape)


def prep_projections(projection, weight_of, prior, core, side, owner, wo, ws, n):
    rows = projection.shape[0]
    half = 2 * wo + ws
    width = n * half + LANES
    if wo % LANES == 0:
        index, noise = weight_of
        out = [
            jax.ShapeDtypeStruct((rows, width), BF16),
            jax.ShapeDtypeStruct((rows, width), BF16),
            jax.ShapeDtypeStruct((rows, LANES), F32),
        ]
        fixed = lambda i: (0, 0)
        return pl.pallas_call(
            functools.partial(projection_kernel, wo, ws, n),
            grid=(n,),
            in_specs=[
                pl.BlockSpec((rows, 2 * half), lambda i: (0, i)),
                pl.BlockSpec(index.shape, fixed),
                pl.BlockSpec(noise.shape, fixed),
                pl.BlockSpec(prior.shape, fixed),
            ],
            out_specs=[pl.BlockSpec(o.shape, fixed) for o in out],
            out_shape=out,
            scratch_shapes=[pltpu.VMEM((rows, LANES), F32), pltpu.VMEM(index.shape, F32)],
            compiler_params=pltpu.CompilerParams(vmem_limit_bytes=32 * MIB),
            name="prep_projections",
        )(projection, index, noise, prior)
    weight = full_weights(weight_of)
    half_norm = 0.5 * jnp.sum(jnp.square(projection.astype(F32)) * weight, axis=1, keepdims=True)
    bias = jnp.broadcast_to(prior - half_norm, (rows, LANES))
    lane = jnp.arange(LANES, dtype=jnp.int32)
    gate = jnp.broadcast_to(jnp.where(lane == owner, MASKED, 0.0).astype(BF16)[None, :], (rows, LANES))
    split = projection.reshape(rows, n, 2, half)
    both = []
    for which in (core, 1 - core):
        own, oth, shared = cut(lax.dynamic_index_in_dim(split, which, 2, keepdims=False), side, wo)
        both.append(jnp.concatenate([own, gate, oth, shared], axis=1))
    return both[0], both[1], bias


def pack_kernel(cols, *refs):
    row = 0
    for ref in refs[:-1]:
        refs[-1][row : row + ref.shape[0], :] = ref[:, :cols]
        row += ref.shape[0]


def pack(pieces, cols):
    vmem = pl.BlockSpec(memory_space=pltpu.VMEM)
    return pl.pallas_call(
        functools.partial(pack_kernel, cols),
        in_specs=[vmem] * len(pieces),
        out_specs=vmem,
        out_shape=jax.ShapeDtypeStruct((sum(p.shape[0] for p in pieces), cols), BF16),
        compiler_params=pltpu.CompilerParams(vmem_limit_bytes=16 * MIB),
        name="pack",
    )(*pieces)


def score_kernel(wo, ws, counts, aligned, where_ref, own_ref, mate_ref, bias_ref, *refs):
    kinds, at_ref = [], 0
    for count in counts:
        kinds.append(refs[at_ref : at_ref + count])
        at_ref += count
    part_ref = refs[at_ref]
    rows = own_ref.shape[0]
    acc = None
    base = 0
    for pieces in kinds:
        width = pieces[0].shape[1]
        for start in range(0, width, 1024):
            size = min(1024, width - start)
            x = jnp.concatenate([p[:, start : start + size] for p in pieces], axis=0)
            cols = slice(base + start, base + start + size)
            p = jnp.concatenate([own_ref[:, cols], mate_ref[:, cols]], axis=0)
            term = lax.dot_general(p, x, (((1,), (1,)), ((), ())), preferred_element_type=F32)
            acc = term if acc is None else acc + term
        base += width
    part_ref[:rows, :] = acc[:rows] + bias_ref[...]
    part_ref[rows:, :] = acc[rows:]
    if aligned:
        side, owner = where_ref[1], where_ref[2]
        slice_ref = refs[at_ref + 1]
        spots = ((side * wo, wo), ((1 - side) * wo, wo), (2 * wo, ws))
        for pieces, (spot, size) in zip(kinds, spots, strict=True):
            row = 0
            for p in pieces:
                slice_ref[row : row + p.shape[0], at(spot, size)] = p[:, at(owner * size, size)]
                row += p.shape[0]


def group_scores(where, own, mate, bias, kinds, wo, ws):
    aligned = wo % LANES == 0
    rows = own.shape[0]
    count = sum(p.shape[0] for p in kinds[0])
    half = 2 * wo + ws
    out = [jax.ShapeDtypeStruct((2 * rows, count), F32)]
    if aligned:
        out.append(jax.ShapeDtypeStruct((count, half), BF16))
    flat = [p for pieces in kinds for p in pieces]
    vmem = pl.BlockSpec(memory_space=pltpu.VMEM)
    got = pl.pallas_call(
        functools.partial(score_kernel, wo, ws, [len(k) for k in kinds], aligned),
        in_specs=[pl.BlockSpec(memory_space=pltpu.SMEM)] + [vmem] * (3 + len(flat)),
        out_specs=[vmem] * len(out),
        out_shape=out,
        compiler_params=pltpu.CompilerParams(vmem_limit_bytes=40 * MIB),
        cost_estimate=pl.CostEstimate(
            flops=4 * rows * count * own.shape[1], bytes_accessed=4 * own.size + 2 * count * own.shape[1], transcendentals=0
        ),
        name="group_scores",
    )(where, own, mate, bias, *flat)
    if aligned:
        return got
    side, owner = where[1], where[2]
    own_o, oth_o, shared = (jnp.concatenate(k, axis=0) for k in kinds)
    a = lax.dynamic_slice_in_dim(own_o, owner * wo, wo, 1)
    b = lax.dynamic_slice_in_dim(oth_o, owner * wo, wo, 1)
    c = lax.dynamic_slice_in_dim(shared, owner * ws, ws, 1)
    first, second = jnp.where(side == 0, a, b), jnp.where(side == 0, b, a)
    return got[0], jnp.concatenate([first, second, c], axis=1)


def stats_kernel(groups, *refs):
    parts, recvs = refs[:groups], refs[groups : 2 * groups]
    score_ref, stat_ref = refs[2 * groups :]
    rows = score_ref.shape[0]
    for g in range(groups):
        count = parts[g].shape[1]
        cols = slice(g * count, (g + 1) * count)
        mine = parts[g][:rows, :] + recvs[g][rows:, :]
        other = parts[g][rows:, :] + recvs[g][:rows, :]
        best = jnp.maximum(jnp.max(mine, axis=0, keepdims=True), jnp.max(other, axis=0, keepdims=True))
        total = jnp.sum(jnp.exp(mine - best), axis=0, keepdims=True) + jnp.sum(jnp.exp(other - best), axis=0, keepdims=True)
        score_ref[:, cols] = mine
        stat_ref[0:1, cols] = best
        stat_ref[1:2, cols] = total
        stat_ref[2:8, cols] = jnp.zeros((6, count), F32)


def ring_order(n):
    return [(0, n // 2)] + [(d, n - d) for d in range(1, n // 2)]


def payload_kernel(n, turns, where_ref, score_ref, *refs):
    stats, out_ref = refs[:turns], refs[turns]
    rows, width = score_ref.shape
    per = width // n
    plane = where_ref[3]
    best = functools.reduce(jnp.maximum, [s[0:1, :] for s in stats])
    terms = [s[1:2, :] * jnp.exp(s[0:1, :] - best) for s in stats]
    total = None
    for a in range(turns):
        back = lax.rem(plane - a + turns, turns)
        term = sum(jnp.where(back == j, terms[j], 0.0) for j in range(turns))
        total = term if total is None else total + term
    out_ref[:rows, :] = jnp.exp(score_ref[...] - best).astype(BF16)
    tops, sums = [None] * n, [None] * n
    for g, pair in enumerate(ring_order(n)):
        for h, r in enumerate(pair):
            cols = slice((2 * g + h) * per, (2 * g + h + 1) * per)
            tops[r], sums[r] = best[:, cols], total[:, cols]
    both = jnp.concatenate([jnp.concatenate(tops, axis=0), jnp.concatenate(sums, axis=0)], axis=1)
    tail = out_ref.shape[0] - rows
    if tail > n:
        both = jnp.concatenate([both, jnp.zeros((tail - n, 2 * per), F32)], axis=0)
    left = both
    for j in range(3):
        piece = left.astype(BF16)
        out_ref[rows:, j * 2 * per : (j + 1) * 2 * per] = piece
        left = left - piece.astype(F32)
    out_ref[rows:, 6 * per :] = jnp.zeros((tail, width - 6 * per), BF16)


def sums_kernel(n, rows, halves, blocks_ref, *refs):
    payloads = refs[:n]
    w_own_ref, w_oth_ref = refs[n], refs[n + 1]
    out_ref, evidence_ref = refs[n + 2], refs[n + 3]
    posterior = refs[n + 4]
    step = pl.program_id(0)
    width = payloads[0].shape[1]
    per = width // n
    order = ring_order(n)

    @pl.when(step == 0)
    def _():
        tops, sums = [], []
        for d in range(n):
            raw = [payloads[d][rows:, j * 2 * per : (j + 1) * 2 * per].astype(F32)[:n] for j in range(3)]
            both = raw[0] + raw[1] + raw[2]
            both = jnp.concatenate([both[n - d :], both[: n - d]], axis=0) if d else both
            tops.append(both[:, :per])
            sums.append(both[:, per:])
        best = functools.reduce(jnp.maximum, tops)
        grow = [jnp.exp(t - best) for t in tops]
        total = functools.reduce(lambda a, b: a + b, [s * g for s, g in zip(sums, grow, strict=True)])
        evidence_ref[...] = best + jnp.log(total)
        for d in range(n):
            scale = grow[d] / total
            wide = jnp.concatenate([scale, scale], axis=1)
            held = payloads[d][:rows, :]
            chunks = [None] * n
            for g, pair in enumerate(order):
                for h, r in enumerate(pair):
                    c = (2 * g + h) * per
                    s = (d + r) % n
                    tile = held[:, c : c + per].astype(F32)
                    chunks[s] = (tile * wide[s : s + 1, :per]).astype(BF16)
            row = pl.multiple_of(blocks_ref[d] * rows, 16)
            for g, (a, b) in enumerate(order):
                posterior[pl.ds(row, rows), 2 * g * per : 2 * (g + 1) * per] = jnp.concatenate([chunks[a], chunks[b]], axis=1)

    if halves:
        w = jnp.where(step < pl.num_programs(0) // 2, w_own_ref[...], w_oth_ref[...])
        left = posterior[...]
    else:
        w = w_own_ref[...]
        left = posterior[pl.ds(pl.multiple_of(step * out_ref.shape[0], 16), out_ref.shape[0]), :]
    out_ref[...] = jnp.dot(left, w, preferred_element_type=F32).astype(BF16)


def body(images, projections, log_prior, significant, shell_index, noise_inv):
    n = lax.axis_size("ori")
    n_cls = lax.axis_size("cls")
    turns = n_cls // 2
    owner = lax.axis_index("ori")
    cls = lax.axis_index("cls")
    core, plane = cls % 2, cls // 2
    side = plane % 2
    rows, freqs = images.shape
    ori_rows = projections.shape[1]
    half = freqs // n // 2
    wo = 3 * half // 10
    ws = half - 2 * wo
    cycle = cycle_of(n)
    spot_of = [cycle.index(o) for o in range(n)]

    def ring(x, d):
        return lax.ppermute(x, "ori", [(cycle[i], cycle[(i + d) % n]) for i in range(n)])

    def swap(x):
        return lax.ppermute(x, "cls", [(i, i ^ 1) for i in range(n_cls)])

    def cross(x):
        return lax.ppermute(x, "cls", [(i, i ^ 2) for i in range(n_cls)])

    weight_of = (shell_index.reshape(freqs // LANES, LANES), noise_inv.reshape(1, -1))
    where = jnp.stack([core, side, owner, plane])
    own, oth, shared = prep_images(images, weight_of, significant, core, side, wo, ws, n)
    projections, own, oth, shared = lax.optimization_barrier((projections, own, oth, shared))
    keep, send, bias = prep_projections(
        projections[0], weight_of, log_prior[0].reshape(ori_rows, 1), core, side, owner, wo, ws, n
    )
    mate = swap(send)

    groups = []
    fo, bo, fs, bs = own, own, shared, shared
    cutoff = rows // 2
    crossed = {}
    for d in range(1, n // 2 + 1):
        if d == n // 2:
            fo, bo, fs, bs = fo[:cutoff], bo[cutoff:], fs[:cutoff], bs[cutoff:]
        if d > 2:
            fo, bo, crossed[d - 2] = lax.optimization_barrier((fo, bo, crossed[d - 2]))
        fo, bo = ring(fo, 1), ring(bo, -1)
        fs, bs = ring(fs, 1), ring(bs, -1)
        fp, bp = fo, bo
        if d == 1:
            fp, bp, mate = lax.optimization_barrier((fp, bp, mate))
        crossed[d] = cross(pack([fp, bp], n * wo))
        if d < n // 2:
            groups.append([[fo, bo], [crossed[d]], [fs, bs]])
        else:
            groups.insert(0, [[own, fo, bo], [oth, crossed[d]], [shared, fs, bs]])

    parts, slices = [None] * len(groups), [None] * len(groups)
    for g in list(range(1, len(groups))) + [0]:
        parts[g], slices[g] = group_scores(where, keep, mate, bias, groups[g], wo, ws)
    recvs = [swap(p) for p in parts]
    other_slices = [swap(s) for s in slices]

    vmem = pl.BlockSpec(memory_space=pltpu.VMEM)
    smem = pl.BlockSpec(memory_space=pltpu.SMEM)
    width = n * rows
    scores, stats = pl.pallas_call(
        functools.partial(stats_kernel, len(groups)),
        in_specs=[vmem] * (2 * len(groups)),
        out_specs=[vmem, vmem],
        out_shape=[jax.ShapeDtypeStruct((ori_rows, width), F32), jax.ShapeDtypeStruct((8, width), F32)],
        compiler_params=pltpu.CompilerParams(vmem_limit_bytes=32 * MIB),
        name="local_stats",
    )(*parts, *recvs)
    all_stats = [stats] + [
        lax.ppermute(stats, "cls", [(i, (i + 2 * j) % n_cls) for i in range(n_cls)]) for j in range(1, turns)
    ]
    tail = max(16, n)
    payload = pl.pallas_call(
        functools.partial(payload_kernel, n, turns),
        in_specs=[smem] + [vmem] * (1 + turns),
        out_specs=vmem,
        out_shape=jax.ShapeDtypeStruct((ori_rows + tail, width), BF16),
        compiler_params=pltpu.CompilerParams(vmem_limit_bytes=32 * MIB),
        name="payload",
    )(where, scores, *all_stats)

    payloads = [payload] + [None] * (n - 1)
    fp = bp = payload
    for d in range(1, n // 2 + 1):
        fp = payloads[d] = ring(fp, 1)
        if d < n // 2:
            bp = payloads[n - d] = ring(bp, -1)

    spots = jnp.array(spot_of, dtype=jnp.int32)
    order = jnp.array(cycle, dtype=jnp.int32)
    blocks = order[(spots[owner] - jnp.arange(n, dtype=jnp.int32)) % n]
    w_own, w_oth = jnp.concatenate(slices, axis=0), jnp.concatenate(other_slices, axis=0)
    fixed = lambda i, b: (0, 0)
    halves = half % 256 == 0
    if halves:
        per_half = half // 256
        steps = 2 * per_half
        scalars = jnp.concatenate([blocks, core[None].astype(jnp.int32)])
        first = lambda i, b: (0, jnp.minimum(i, per_half - 1))
        second = lambda i, b: (0, jnp.maximum(i - per_half, 0))
        target = lambda i, b: (0, jnp.where(i < per_half, b[n] * per_half + i, (1 - b[n]) * per_half + i - per_half))
        w_specs = [pl.BlockSpec((width, 256), first), pl.BlockSpec((width, 256), second)]
        out_spec = pl.BlockSpec((n * ori_rows, 256), target)
    else:
        steps = max(1, n // 8)
        scalars = blocks
        low, high = jnp.where(core == 0, w_own, w_oth), jnp.where(core == 0, w_oth, w_own)
        w_own = jnp.concatenate([low, high], axis=1)
        w_specs = [pl.BlockSpec((width, 2 * half), fixed), pl.BlockSpec((16, 128), fixed)]
        out_spec = pl.BlockSpec((n * ori_rows // steps, 2 * half), lambda i, b: (i, 0))
    sums, evidence = pl.pallas_call(
        functools.partial(sums_kernel, n, ori_rows, halves),
        grid_spec=pltpu.PrefetchScalarGridSpec(
            num_scalar_prefetch=1,
            grid=(steps,),
            in_specs=[pl.BlockSpec(payload.shape, fixed, pipeline_mode=pl.Buffered(1))] * n + w_specs,
            out_specs=[out_spec, pl.BlockSpec((n, rows), fixed)],
            scratch_shapes=[pltpu.VMEM((n * ori_rows, width), BF16)],
        ),
        out_shape=[jax.ShapeDtypeStruct((n * ori_rows, 2 * half), BF16), jax.ShapeDtypeStruct((n, rows), F32)],
        compiler_params=pltpu.CompilerParams(vmem_limit_bytes=58 * MIB),
        name="class_sums",
    )(scalars, *payloads, w_own, w_oth)
    return sums[None], evidence[0]


def solution(mesh):
    in_specs = (P("ori", None), P("cls", "ori", None), P("cls", "ori"), P("ori", None), P(), P())
    out_specs = (P("cls", None, "ori"), P("ori"))
    return jax.shard_map(body, mesh=mesh, in_specs=in_specs, out_specs=out_specs, check_vma=False)
```

```python
import functools
import math

import jax
import jax.numpy as jnp
from jax import lax
from jax.experimental import pallas as pl
from jax.experimental.pallas import tpu as pltpu
from jax.sharding import PartitionSpec as P

BF16 = jnp.bfloat16
F32 = jnp.float32
MASKED = -1e30
LANES = 128
MIB = 1 << 20
TAIL = 16


def cycle_of(count):
    deep = math.isqrt(count // 2)
    tall = count // deep
    walk = [(z, 0) for z in range(tall)]
    for z in range(tall - 1, -1, -1):
        cols = list(range(1, deep))
        walk += [(z, y) for y in (cols if (tall - 1 - z) % 2 == 0 else cols[::-1])]
    return [z * deep + y for z, y in walk]


def weight_table(index, noise):
    levels = noise.shape[1]
    row = jnp.concatenate([noise, jnp.zeros((1, LANES - levels), F32)], axis=1)
    table = jnp.broadcast_to(row, index.shape)
    return jnp.take_along_axis(table, index, axis=1, mode="promise_in_bounds")


def at(start, size):
    return pl.ds(pl.multiple_of(start, LANES), size)


def image_kernel(n, wo, ws, img_hbm, index_hbm, noise_hbm, sig_hbm, own_ref, oth_ref, shared_ref, w_ref, img, index, noise, sig, sems):
    cls = lax.axis_index("cls")
    core, side = cls % 2, (cls // 2) % 2
    half = 2 * wo + ws
    loads = []
    for i in range(n):
        src = img_hbm.at[:, at((2 * i + core) * half, half)]
        loads.append(pltpu.make_async_copy(src, img.at[:, i * half : (i + 1) * half], sems.at[i]))
    small = [(index_hbm, index), (noise_hbm, noise), (sig_hbm, sig)]
    copies = [pltpu.make_async_copy(src, dst, sems.at[n + i]) for i, (src, dst) in enumerate(small)]
    for copy in copies + loads:
        copy.start()
    for copy in copies:
        copy.wait()
    w_ref[...] = weight_table(index[...], noise[...])
    rows = img.shape[0]
    block = lax.broadcasted_iota(jnp.int32, (LANES, rows), 0)
    listed = block < 0
    for j in range(sig.shape[0]):
        listed = listed | (sig[j : j + 1, :] == block)
    unlisted = jnp.where(listed, 0.0, 1.0).astype(BF16)
    same = lax.broadcasted_iota(jnp.int32, (rows, rows), 0) == lax.broadcasted_iota(jnp.int32, (rows, rows), 1)
    eye = jnp.where(same, 1.0, 0.0).astype(BF16)
    turned = lax.dot_general(eye, unlisted, (((1,), (1,)), ((), ())), preferred_element_type=F32)
    own_ref[:, n * wo :] = turned.astype(BF16)
    for i in range(n):
        loads[i].wait()
        for ref, start, count in (
            (own_ref, side * wo, wo),
            (oth_ref, (1 - side) * wo, wo),
            (shared_ref, 2 * wo, ws),
        ):
            for j in range(0, count, LANES):
                tile = ((2 * i + core) * half + start + j) // LANES
                weight = w_ref[pl.ds(tile, 1), :]
                wide = img[:, at(i * half + start + j, LANES)].astype(F32) * weight
                ref[:, i * count + j : i * count + j + LANES] = wide.astype(BF16)


def prep_images(images, weight_of, significant, core, side, wo, ws, n):
    rows = images.shape[0]
    half = 2 * wo + ws
    if wo % LANES == 0:
        index, noise = weight_of
        sig = significant.T
        out = [jax.ShapeDtypeStruct((rows, w), BF16) for w in (n * wo + LANES, n * wo, n * ws)]
        out.append(jax.ShapeDtypeStruct(index.shape, F32))
        vmem = pl.BlockSpec(memory_space=pltpu.VMEM)
        return pl.pallas_call(
            functools.partial(image_kernel, n, wo, ws),
            in_specs=[pl.BlockSpec(memory_space=pl.ANY)] * 4,
            out_specs=[vmem] * 4,
            out_shape=out,
            scratch_shapes=[
                pltpu.VMEM((rows, n * half), BF16),
                pltpu.VMEM(index.shape, index.dtype),
                pltpu.VMEM(noise.shape, F32),
                pltpu.VMEM(sig.shape, sig.dtype),
                pltpu.SemaphoreType.DMA((n + 3,)),
            ],
            compiler_params=pltpu.CompilerParams(vmem_limit_bytes=61 * MIB),
            name="prep_images",
        )(images, index, noise, sig)
    weight = full_weights(weight_of)
    weighted = (images.astype(F32) * weight).astype(BF16).reshape(rows, n, 2, half)
    mine = lax.dynamic_index_in_dim(weighted, core, 2, keepdims=False)
    own, oth, shared = cut(mine, side, wo)
    lane = jnp.arange(LANES, dtype=jnp.int32)
    listed = jnp.any(significant[:, :, None] == lane[None, None, :], axis=1)
    return jnp.concatenate([own, jnp.where(listed, 0.0, 1.0).astype(BF16)], axis=1), oth, shared, weight


def full_weights(weight_of):
    index, noise = weight_of
    levels = jnp.arange(noise.shape[1], dtype=jnp.int32)
    return jnp.sum(jnp.where(index.reshape(-1, 1) == levels[None, :], noise, 0.0), axis=1)[None, :]


def cut(mine, side, wo):
    rows, n, _ = mine.shape
    own = lax.dynamic_slice_in_dim(mine, side * wo, wo, 2).reshape(rows, n * wo)
    oth = lax.dynamic_slice_in_dim(mine, (1 - side) * wo, wo, 2).reshape(rows, n * wo)
    return own, oth, mine[:, :, 2 * wo :].reshape(rows, -1)


def split_kernel(wo, ws, n, proj_hbm, keep_ref, send_ref, sems):
    half = 2 * wo + ws
    cls, owner = lax.axis_index("cls"), lax.axis_index("ori")
    core, side = cls % 2, (cls // 2) % 2
    copies = []
    for ref, which in ((send_ref, 1 - core), (keep_ref, core)):
        for i in range(n):
            base = (2 * i + which) * half
            for start, spot, count in (
                (base + side * wo, i * wo, wo),
                (base + 2 * wo, n * wo + LANES + i * ws, ws),
                (base + (1 - side) * wo, n * (wo + ws) + LANES + i * wo, wo),
            ):
                src = proj_hbm.at[0, :, at(start, count)]
                copies.append(pltpu.make_async_copy(src, ref.at[:, spot : spot + count], sems.at[len(copies)]))
                copies[-1].start()
    lane = lax.broadcasted_iota(jnp.int32, (keep_ref.shape[0], LANES), 1)
    gate = jnp.where(lane == owner, MASKED, 0.0).astype(BF16)
    keep_ref[:, n * wo : n * wo + LANES] = gate
    send_ref[:, n * wo : n * wo + LANES] = gate
    for copy in copies:
        copy.wait()


def norm_kernel(wo, ws, n, keep_ref, send_ref, prior_ref, w_ref, bias_ref):
    half = 2 * wo + ws
    cls = lax.axis_index("cls")
    core, side = cls % 2, (cls // 2) % 2
    rows = keep_ref.shape[0]
    total = jnp.zeros((rows, LANES), F32)
    for ref, which in ((keep_ref, core), (send_ref, 1 - core)):
        for i in range(n):
            base = (2 * i + which) * half
            for start, spot, count in (
                (base + side * wo, i * wo, wo),
                (base + 2 * wo, n * wo + LANES + i * ws, ws),
                (base + (1 - side) * wo, n * (wo + ws) + LANES + i * wo, wo),
            ):
                for j in range(0, count, LANES):
                    wide = ref[:, spot + j : spot + j + LANES].astype(F32)
                    total = total + wide * wide * w_ref[pl.ds((start + j) // LANES, 1), :]
    half_norm = 0.5 * jnp.sum(total, axis=1, keepdims=True)
    prior = jnp.concatenate([prior_ref[...], jnp.zeros((1, -rows % LANES), F32)], axis=1)
    spread = (rows, prior.shape[1])
    on_line = lax.broadcasted_iota(jnp.int32, spread, 0) == lax.broadcasted_iota(jnp.int32, spread, 1)
    prior = jnp.sum(jnp.where(on_line, prior, 0.0), axis=1, keepdims=True)
    bias_ref[...] = jnp.broadcast_to(prior - half_norm, bias_ref.shape)


def prep_projections(projections, weight, log_prior, core, side, owner, wo, ws, n):
    rows = projections.shape[1]
    half = 2 * wo + ws
    width = n * half + LANES
    if wo % LANES == 0:
        vmem = pl.BlockSpec(memory_space=pltpu.VMEM)
        keep, send = pl.pallas_call(
            functools.partial(split_kernel, wo, ws, n),
            in_specs=[pl.BlockSpec(memory_space=pl.ANY)],
            out_specs=[vmem] * 2,
            out_shape=[jax.ShapeDtypeStruct((rows, width), BF16)] * 2,
            scratch_shapes=[pltpu.SemaphoreType.DMA((6 * n,))],
            compiler_params=pltpu.CompilerParams(vmem_limit_bytes=54 * MIB),
            cost_estimate=pl.CostEstimate(flops=0, bytes_accessed=4 * projections.size, transcendentals=0),
            name="split_projections",
        )(projections)
        bias = pl.pallas_call(
            functools.partial(norm_kernel, wo, ws, n),
            in_specs=[vmem] * 4,
            out_specs=vmem,
            out_shape=jax.ShapeDtypeStruct((rows, LANES), F32),
            compiler_params=pltpu.CompilerParams(vmem_limit_bytes=16 * MIB),
            cost_estimate=pl.CostEstimate(flops=3 * projections.size, bytes_accessed=2 * projections.size, transcendentals=0),
            name="half_norms",
        )(keep, send, log_prior, weight)
        return keep, send, bias
    projection, prior = projections[0], log_prior.reshape(rows, 1)
    half_norm = 0.5 * jnp.sum(jnp.square(projection.astype(F32)) * weight, axis=1, keepdims=True)
    bias = jnp.broadcast_to(prior - half_norm, (rows, LANES))
    lane = jnp.arange(LANES, dtype=jnp.int32)
    gate = jnp.broadcast_to(jnp.where(lane == owner, MASKED, 0.0).astype(BF16)[None, :], (rows, LANES))
    split = projection.reshape(rows, n, 2, half)
    both = []
    for which in (core, 1 - core):
        own, oth, shared = cut(lax.dynamic_index_in_dim(split, which, 2, keepdims=False), side, wo)
        both.append(jnp.concatenate([own, gate, shared, oth], axis=1))
    return both[0], both[1], bias


def pack_kernel(pieces, *refs):
    arrays, outs = refs[: len(refs) - len(pieces)], refs[len(refs) - len(pieces) :]
    for out, places in zip(outs, pieces, strict=True):
        for k, rows, cols, row, col in places:
            size = (rows.stop - rows.start, cols.stop - cols.start)
            out[row : row + size[0], col : col + size[1]] = arrays[k][rows, cols]


def pack(arrays, shapes, pieces):
    vmem = pl.BlockSpec(memory_space=pltpu.VMEM)
    return pl.pallas_call(
        functools.partial(pack_kernel, pieces),
        in_specs=[vmem] * len(arrays),
        out_specs=[vmem] * len(shapes),
        out_shape=[jax.ShapeDtypeStruct(shape, BF16) for shape in shapes],
        compiler_params=pltpu.CompilerParams(vmem_limit_bytes=8 * MIB),
        name="pack",
    )(*arrays)


def score_kernel(wo, ws, kinds, aligned, own_ref, mate_ref, bias_ref, *refs):
    count = 1 + max(k for _, places in kinds for k, _ in places)
    pieces, part_ref = refs[:count], refs[count]
    rows = own_ref.shape[0]
    acc = None
    base = 0
    for width, places in kinds:
        for start in range(0, width, 1024):
            size = min(1024, width - start)
            x = jnp.concatenate([pieces[k][:, c + start : c + start + size] for k, c in places], axis=0)
            cols = slice(base + start, base + start + size)
            p = jnp.concatenate([own_ref[:, cols], mate_ref[:, cols]], axis=0)
            term = lax.dot_general(p, x, (((1,), (1,)), ((), ())), preferred_element_type=F32)
            acc = term if acc is None else acc + term
        base += width
    part_ref[:rows, :] = acc[:rows] + bias_ref[...]
    part_ref[rows:, :] = acc[rows:]
    if aligned:
        side, owner = (lax.axis_index("cls") // 2) % 2, lax.axis_index("ori")
        slice_ref = refs[count + 1]
        for (_, places), spot, size in zip(kinds, (side * wo, 2 * wo, (1 - side) * wo), (wo, ws, wo), strict=True):
            row = 0
            for k, c in places:
                p = pieces[k]
                slice_ref[row : row + p.shape[0], at(spot, size)] = p[:, at(c + owner * size, size)]
                row += p.shape[0]


def group_scores(own, mate, bias, kinds, wo, ws, n):
    aligned = wo % LANES == 0
    rows = own.shape[0]
    half = 2 * wo + ws
    count = sum(p.shape[0] for p, _ in kinds[0])
    out = [jax.ShapeDtypeStruct((2 * rows, count), F32)]
    if aligned:
        out.append(jax.ShapeDtypeStruct((count, half), BF16))
    arrays, numbered = [], []
    for places, width in zip(kinds, (n * wo + LANES, n * ws, n * wo), strict=True):
        numbered.append((width, [(len(arrays) + i, c) for i, (_, c) in enumerate(places)]))
        arrays += [p for p, _ in places]
    vmem = pl.BlockSpec(memory_space=pltpu.VMEM)
    got = pl.pallas_call(
        functools.partial(score_kernel, wo, ws, numbered, aligned),
        in_specs=[vmem] * (3 + len(arrays)),
        out_specs=[vmem] * len(out),
        out_shape=out,
        compiler_params=pltpu.CompilerParams(vmem_limit_bytes=8 * MIB),
        cost_estimate=pl.CostEstimate(
            flops=4 * rows * count * own.shape[1], bytes_accessed=4 * own.size + 2 * count * own.shape[1], transcendentals=0
        ),
        name="group_scores",
    )(own, mate, bias, *arrays)
    if aligned:
        return got
    side, owner = (lax.axis_index("cls") // 2) % 2, lax.axis_index("ori")
    cols = []
    for places, size in zip(kinds, (wo, ws, wo), strict=True):
        cols.append(jnp.concatenate([lax.dynamic_slice_in_dim(p, c + owner * size, size, 1) for p, c in places], axis=0))
    a, c, b = cols
    first, second = jnp.where(side == 0, a, b), jnp.where(side == 0, b, a)
    return got[0], jnp.concatenate([first, second, c], axis=1)


def group_order(n):
    return [(0, n // 2)] + [(d, n - d) for d in range(1, n // 2)]


def stats_kernel(n, *refs):
    groups = n // 2
    parts, recvs = refs[:groups], refs[groups : 2 * groups]
    score_ref, stat_ref = refs[2 * groups :]
    rows = score_ref.shape[0]
    per = parts[0].shape[1] // 2
    for g, pair in enumerate(group_order(n)):
        mine = parts[g][:rows, :] + recvs[g][rows:, :]
        other = parts[g][rows:, :] + recvs[g][:rows, :]
        best = jnp.maximum(jnp.max(mine, axis=0, keepdims=True), jnp.max(other, axis=0, keepdims=True))
        total = jnp.sum(jnp.exp(mine - best), axis=0, keepdims=True) + jnp.sum(jnp.exp(other - best), axis=0, keepdims=True)
        for h, r in enumerate(pair):
            cols, held = slice(r * per, (r + 1) * per), slice(h * per, (h + 1) * per)
            score_ref[:, cols] = mine[:, held]
            stat_ref[0:1, cols] = best[:, held]
            stat_ref[1:2, cols] = total[:, held]
    stat_ref[2:8, :] = jnp.zeros((6, stat_ref.shape[1]), F32)


def payload_kernel(turns, score_ref, *refs):
    stats, out_ref = refs[:turns], refs[turns]
    rows = score_ref.shape[0]
    plane = lax.axis_index("cls") // 2
    best = functools.reduce(jnp.maximum, [s[0:1, :] for s in stats])
    terms = [s[1:2, :] * jnp.exp(s[0:1, :] - best) for s in stats]
    total = None
    for a in range(turns):
        back = lax.rem(plane - a + turns, turns)
        term = sum(jnp.where(back == j, terms[j], 0.0) for j in range(turns))
        total = term if total is None else total + term
    out_ref[:rows, :] = jnp.exp(score_ref[...] - best).astype(BF16)
    left = jnp.concatenate([best, total], axis=0)
    levels = []
    for _ in range(3):
        piece = left.astype(BF16).astype(F32)
        levels.append(piece)
        left = left - piece
    levels.append(jnp.zeros((TAIL - 6, best.shape[1]), F32))
    out_ref[rows:, :] = jnp.concatenate(levels, axis=0).astype(BF16)


def sums_kernel(n, rows, per_half, cycle, *refs):
    owner = lax.axis_index("ori")
    spot = sum(jnp.where(owner == o, cycle.index(o), 0) for o in range(n))
    payloads, refs = refs[:n], refs[n:]
    groups = n // 2
    w_own, w_oth = refs[:groups], refs[groups:-3]
    out_ref, evidence_ref, posterior = refs[-3:]
    step = pl.program_id(0)
    width = payloads[0].shape[1]
    per = width // n

    @pl.when(step == 0)
    def _():
        tops, sums = [], []
        for d in range(n):
            stat = payloads[d][rows:, :].astype(F32)
            stat = jnp.concatenate([stat[0:2] + stat[2:4] + stat[4:6], jnp.zeros((6, width), F32)], axis=0)
            stat = pltpu.roll(stat, per * d, 1) if d else stat
            tops.append(stat[0:1])
            sums.append(stat[1:2])
        best = functools.reduce(jnp.maximum, tops)
        grow = [jnp.exp(t - best) for t in tops]
        total = functools.reduce(lambda a, b: a + b, [s * g for s, g in zip(sums, grow, strict=True)])
        evidence_ref[...] = (best + jnp.log(total))[:, :per]
        for d in range(n):
            wide = payloads[d][:rows, :].astype(F32)
            wide = pltpu.roll(wide, per * d, 1) if d else wide
            back = lax.rem(spot + (n - d), n)
            block = sum(jnp.where(back == p, cycle[p], 0) for p in range(n))
            row = pl.multiple_of(block * rows, 16)
            posterior[pl.ds(row, rows), :] = (wide * (grow[d] / total)).astype(BF16)

    places = {r: (g, h) for g, pair in enumerate(group_order(n)) for h, r in enumerate(pair)}
    first = (step < per_half) == (lax.axis_index("cls") % 2 == 0)
    pieces = []
    for r in range(n):
        g, h = places[r]
        held = slice(h * per, (h + 1) * per)
        pieces.append(jnp.where(first, w_own[g][held, :], w_oth[g][held, :]) if per_half else w_own[g][held, :])
    left = posterior[...]
    if not per_half:
        left = posterior[pl.ds(pl.multiple_of(step * out_ref.shape[0], 16), out_ref.shape[0]), :]
    out_ref[...] = jnp.dot(left, jnp.concatenate(pieces, axis=0), preferred_element_type=F32).astype(BF16)


def tie(*values):
    return lax.optimization_barrier(values)


def body(images, projections, log_prior, significant, shell_index, noise_inv):
    n = lax.axis_size("ori")
    n_cls = lax.axis_size("cls")
    turns = n_cls // 2
    owner = lax.axis_index("ori")
    cls = lax.axis_index("cls")
    core, side = cls % 2, (cls // 2) % 2
    rows, freqs = images.shape
    ori_rows = projections.shape[1]
    half = freqs // n // 2
    wo = 3 * half // 10
    ws = half - 2 * wo
    cycle = cycle_of(n)
    far = n // 2

    def ring(x, d):
        return lax.ppermute(x, "ori", [(cycle[i], cycle[(i + d) % n]) for i in range(n)])

    def swap(x):
        return lax.ppermute(x, "cls", [(i, i ^ 1) for i in range(n_cls)])

    def cross(x):
        return lax.ppermute(x, "cls", [(i, i ^ 2) for i in range(n_cls)])

    weight_of = (shell_index.reshape(freqs // LANES, LANES), noise_inv.reshape(1, -1))
    own, oth, shared, weight = prep_images(images, weight_of, significant, core, side, wo, ws, n)
    projections, own, oth, shared = tie(projections, own, oth, shared)
    keep, send, bias = prep_projections(projections, weight, log_prior, core, side, owner, wo, ws, n)

    cut_at = rows // 2
    every, top, bottom = slice(0, rows), slice(0, cut_at), slice(cut_at, rows)
    plane_w, shared_w = n * wo + LANES, n * ws
    plane_cols, cross_cols = slice(0, plane_w), slice(0, n * wo)
    shared_cols = slice(plane_w, plane_w + shared_w)
    f, b = ring(own, 1), ring(own, -1)
    f, b, shared, send = tie(f, b, shared, send)
    whole = slice(0, shared_w)
    mates = swap(send)
    both, x_in = [None], None
    f2, b2, x_in = pack(
        [f, b, shared],
        [(rows, plane_w + shared_w)] * 2 + [(2 * rows, n * wo)],
        [[(i, every, plane_cols, 0, 0), (2, every, whole, 0, plane_w)] for i in (0, 1)]
        + [[(0, every, cross_cols, 0, 0), (1, every, cross_cols, rows, 0)]],
    )
    both = [(f2, b2)]
    parts, slices = [None] * far, [None] * far
    crossed = [None]
    for s in range(1, far - 1):
        f, b = both[-1]
        f, b, x = ring(f, 1), ring(b, -1), cross(x_in)
        if s == 1:
            f, b, x, mates = tie(f, b, x, mates)
        else:
            f, b, x, parts[s - 1], slices[s - 1] = tie(f, b, x, parts[s - 1], slices[s - 1])
        both.append((f, b))
        crossed.append(x)
        kinds = ([(p, 0) for p in both[s - 1]], [(p, plane_w) for p in both[s]], [(x, 0)])
        parts[s], slices[s] = group_scores(keep, mates, bias, kinds, wo, ws, n)
        if s < far - 2:
            (x_in,) = pack([f, b], [(2 * rows, n * wo)], [[(0, every, cross_cols, 0, 0), (1, every, cross_cols, rows, 0)]])
    x_in, fo, bo, fs, bs = pack(
        [f, b],
        [(2 * rows, n * wo)] + [(cut_at, plane_w)] * 2 + [(rows, shared_w)] * 2,
        [
            [(0, every, cross_cols, 0, 0), (1, every, cross_cols, rows, 0)],
            [(0, top, plane_cols, 0, 0)],
            [(1, bottom, plane_cols, 0, 0)],
            [(0, every, shared_cols, 0, 0)],
            [(1, every, shared_cols, 0, 0)],
        ],
    )
    fo, bo, fs, bs, x = ring(fo, 1), ring(bo, -1), ring(fs, 1), ring(bs, -1), cross(x_in)
    fo, bo, fs, bs, x, parts[far - 2], slices[far - 2] = tie(fo, bo, fs, bs, x, parts[far - 2], slices[far - 2])
    kinds = ([(p, 0) for p in both[far - 2]], [(fs, 0), (bs, 0)], [(x, 0)])
    parts[far - 1], slices[far - 1] = group_scores(keep, mates, bias, kinds, wo, ws, n)
    (x_in,) = pack([fo, bo], [(rows, n * wo)], [[(0, top, cross_cols, 0, 0), (1, top, cross_cols, cut_at, 0)]])
    fs, bs, x = ring(fs[:cut_at], 1), ring(bs[cut_at:], -1), cross(x_in)
    kinds = ([(own, 0), (fo, 0), (bo, 0)], [(shared, 0), (fs, 0), (bs, 0)], [(oth, 0), (x, 0)])
    parts[0], slices[0] = group_scores(keep, mates, bias, kinds, wo, ws, n)
    recvs = [swap(p) for p in parts]
    other_slices = [swap(x) for x in slices]

    vmem = pl.BlockSpec(memory_space=pltpu.VMEM)
    width = n * rows
    scores, stats = pl.pallas_call(
        functools.partial(stats_kernel, n),
        in_specs=[vmem] * (2 * far),
        out_specs=[vmem, vmem],
        out_shape=[jax.ShapeDtypeStruct((ori_rows, width), F32), jax.ShapeDtypeStruct((8, width), F32)],
        compiler_params=pltpu.CompilerParams(vmem_limit_bytes=16 * MIB),
        name="local_stats",
    )(*parts, *recvs)
    all_stats = [stats] + [
        lax.ppermute(stats, "cls", [(i, (i + 2 * j) % n_cls) for i in range(n_cls)]) for j in range(1, turns)
    ]
    payload = pl.pallas_call(
        functools.partial(payload_kernel, turns),
        in_specs=[vmem] * (1 + turns),
        out_specs=vmem,
        out_shape=jax.ShapeDtypeStruct((ori_rows + TAIL, width), BF16),
        compiler_params=pltpu.CompilerParams(vmem_limit_bytes=16 * MIB),
        name="payload",
    )(scores, *all_stats)
    payloads = [payload] + [None] * (n - 1)
    fp = bp = payload
    for d in range(1, far + 1):
        fp = payloads[d] = ring(fp, 1)
        if d < far:
            bp = payloads[n - d] = ring(bp, -1)

    fixed = lambda i: (0, 0)
    per_half = half // 256 if half % 256 == 0 else 0
    if per_half:
        steps = 2 * per_half
        w = slices + other_slices
        w_specs = [pl.BlockSpec((LANES, 256), lambda i: (0, lax.rem(i, per_half)))] * len(w)
        out_spec = pl.BlockSpec((n * ori_rows, 256), lambda i: (0, i))
        grant = 24
    else:
        steps = max(1, n // 2)
        w = [
            jnp.concatenate([jnp.where(core == 0, a, b), jnp.where(core == 0, b, a)], axis=1)
            for a, b in zip(slices, other_slices, strict=True)
        ]
        w_specs = [pl.BlockSpec((LANES, 2 * half), fixed, pipeline_mode=pl.Buffered(1))] * len(w)
        out_spec = pl.BlockSpec((n * ori_rows // steps, 2 * half), lambda i: (i, 0))
        grant = 62
    held_once = pl.BlockSpec(payload.shape, fixed, pipeline_mode=pl.Buffered(1))
    sums, evidence = pl.pallas_call(
        functools.partial(sums_kernel, n, ori_rows, per_half, cycle),
        grid=(steps,),
        in_specs=[held_once] * n + w_specs,
        out_specs=[out_spec, pl.BlockSpec((1, rows), fixed)],
        scratch_shapes=[pltpu.VMEM((n * ori_rows, width), BF16)],
        out_shape=[jax.ShapeDtypeStruct((n * ori_rows, 2 * half), BF16), jax.ShapeDtypeStruct((1, rows), F32)],
        compiler_params=pltpu.CompilerParams(vmem_limit_bytes=grant * MIB),
        name="class_sums",
    )(*payloads, *w)
    return sums[None], evidence.reshape(rows)


def solution(mesh):
    in_specs = (P("ori", None), P("cls", "ori", None), P("cls", "ori"), P("ori", None), P(), P())
    out_specs = (P("cls", None, "ori"), P("ori"))
    return jax.shard_map(body, mesh=mesh, in_specs=in_specs, out_specs=out_specs, check_vma=False)
```

```python
import functools
import math

import jax
import jax.numpy as jnp
from jax import lax
from jax.experimental import pallas as pl
from jax.experimental.pallas import tpu as pltpu
from jax.sharding import PartitionSpec as P

BF16 = jnp.bfloat16
F32 = jnp.float32
MASKED = -1e30
LANES = 128
MIB = 1 << 20
TAIL = 16
COLS = 1280


def cycle_of(count):
    deep = math.isqrt(count // 2)
    tall = count // deep
    walk = [(z, 0) for z in range(tall)]
    for z in range(tall - 1, -1, -1):
        cols = list(range(1, deep))
        walk += [(z, y) for y in (cols if (tall - 1 - z) % 2 == 0 else cols[::-1])]
    return [z * deep + y for z, y in walk]


def weight_table(index, noise):
    levels = noise.shape[1]
    row = jnp.concatenate([noise, jnp.zeros((1, LANES - levels), F32)], axis=1)
    table = jnp.broadcast_to(row, index.shape)
    return jnp.take_along_axis(table, index, axis=1, mode="promise_in_bounds")


def at(start, size):
    return pl.ds(pl.multiple_of(start, LANES), size)


def image_kernel(n, wo, ws, img_hbm, index_hbm, noise_hbm, sig_hbm, own_ref, oth_ref, shared_ref, w_ref, img, index, noise, sig, sems):
    cls = lax.axis_index("cls")
    core, side = cls % 2, (cls // 2) % 2
    half = 2 * wo + ws
    loads = []
    for i in range(n):
        src = img_hbm.at[:, at((2 * i + core) * half, half)]
        loads.append(pltpu.make_async_copy(src, img.at[:, i * half : (i + 1) * half], sems.at[i]))
    small = [(index_hbm, index), (noise_hbm, noise), (sig_hbm, sig)]
    copies = [pltpu.make_async_copy(src, dst, sems.at[n + i]) for i, (src, dst) in enumerate(small)]
    for copy in copies + loads:
        copy.start()
    for copy in copies:
        copy.wait()
    w_ref[...] = weight_table(index[...], noise[...])
    rows = img.shape[0]
    block = lax.broadcasted_iota(jnp.int32, (LANES, rows), 0)
    listed = block < 0
    for j in range(sig.shape[0]):
        listed = listed | (sig[j : j + 1, :] == block)
    unlisted = jnp.where(listed, 0.0, 1.0).astype(BF16)
    same = lax.broadcasted_iota(jnp.int32, (rows, rows), 0) == lax.broadcasted_iota(jnp.int32, (rows, rows), 1)
    eye = jnp.where(same, 1.0, 0.0).astype(BF16)
    turned = lax.dot_general(eye, unlisted, (((1,), (1,)), ((), ())), preferred_element_type=F32)
    own_ref[:, n * wo :] = turned.astype(BF16)
    for i in range(n):
        loads[i].wait()
        for ref, start, count in (
            (own_ref, side * wo, wo),
            (oth_ref, (1 - side) * wo, wo),
            (shared_ref, 2 * wo, ws),
        ):
            for j in range(0, count, LANES):
                tile = ((2 * i + core) * half + start + j) // LANES
                weight = w_ref[pl.ds(tile, 1), :]
                wide = img[:, at(i * half + start + j, LANES)].astype(F32) * weight
                ref[:, i * count + j : i * count + j + LANES] = wide.astype(BF16)


def prep_images(images, weight_of, significant, core, side, wo, ws, n):
    rows = images.shape[0]
    half = 2 * wo + ws
    if wo % LANES == 0:
        index, noise = weight_of
        sig = significant.T
        out = [jax.ShapeDtypeStruct((rows, w), BF16) for w in (n * wo + LANES, n * wo, n * ws)]
        out.append(jax.ShapeDtypeStruct(index.shape, F32))
        vmem = pl.BlockSpec(memory_space=pltpu.VMEM)
        return pl.pallas_call(
            functools.partial(image_kernel, n, wo, ws),
            in_specs=[pl.BlockSpec(memory_space=pl.ANY)] * 4,
            out_specs=[vmem] * 4,
            out_shape=out,
            scratch_shapes=[
                pltpu.VMEM((rows, n * half), BF16),
                pltpu.VMEM(index.shape, index.dtype),
                pltpu.VMEM(noise.shape, F32),
                pltpu.VMEM(sig.shape, sig.dtype),
                pltpu.SemaphoreType.DMA((n + 3,)),
            ],
            compiler_params=pltpu.CompilerParams(vmem_limit_bytes=61 * MIB),
            name="prep_images",
        )(images, index, noise, sig)
    weight = full_weights(weight_of)
    weighted = (images.astype(F32) * weight).astype(BF16).reshape(rows, n, 2, half)
    mine = lax.dynamic_index_in_dim(weighted, core, 2, keepdims=False)
    own, oth, shared = cut(mine, side, wo)
    lane = jnp.arange(LANES, dtype=jnp.int32)
    listed = jnp.any(significant[:, :, None] == lane[None, None, :], axis=1)
    return jnp.concatenate([own, jnp.where(listed, 0.0, 1.0).astype(BF16)], axis=1), oth, shared, weight


def full_weights(weight_of):
    index, noise = weight_of
    levels = jnp.arange(noise.shape[1], dtype=jnp.int32)
    return jnp.sum(jnp.where(index.reshape(-1, 1) == levels[None, :], noise, 0.0), axis=1)[None, :]


def cut(mine, side, wo):
    rows, n, _ = mine.shape
    own = lax.dynamic_slice_in_dim(mine, side * wo, wo, 2).reshape(rows, n * wo)
    oth = lax.dynamic_slice_in_dim(mine, (1 - side) * wo, wo, 2).reshape(rows, n * wo)
    return own, oth, mine[:, :, 2 * wo :].reshape(rows, -1)


def split_kernel(wo, ws, n, proj_hbm, keep_ref, send_ref, sems):
    half = 2 * wo + ws
    cls, owner = lax.axis_index("cls"), lax.axis_index("ori")
    core, side = cls % 2, (cls // 2) % 2
    copies = []
    for ref, which in ((send_ref, 1 - core), (keep_ref, core)):
        for i in range(n):
            base = (2 * i + which) * half
            for start, spot, count in (
                (base + side * wo, i * wo, wo),
                (base + 2 * wo, n * wo + LANES + i * ws, ws),
                (base + (1 - side) * wo, n * (wo + ws) + LANES + i * wo, wo),
            ):
                src = proj_hbm.at[0, :, at(start, count)]
                copies.append(pltpu.make_async_copy(src, ref.at[:, spot : spot + count], sems.at[len(copies)]))
                copies[-1].start()
    lane = lax.broadcasted_iota(jnp.int32, (keep_ref.shape[0], LANES), 1)
    gate = jnp.where(lane == owner, MASKED, 0.0).astype(BF16)
    keep_ref[:, n * wo : n * wo + LANES] = gate
    send_ref[:, n * wo : n * wo + LANES] = gate
    for copy in copies:
        copy.wait()


def norm_kernel(wo, ws, n, keep_ref, send_ref, prior_ref, w_ref, bias_ref):
    half = 2 * wo + ws
    cls = lax.axis_index("cls")
    core, side = cls % 2, (cls // 2) % 2
    rows = keep_ref.shape[0]
    total = jnp.zeros((rows, LANES), F32)
    for ref, which in ((keep_ref, core), (send_ref, 1 - core)):
        for i in range(n):
            base = (2 * i + which) * half
            for start, spot, count in (
                (base + side * wo, i * wo, wo),
                (base + 2 * wo, n * wo + LANES + i * ws, ws),
                (base + (1 - side) * wo, n * (wo + ws) + LANES + i * wo, wo),
            ):
                for j in range(0, count, LANES):
                    wide = ref[:, spot + j : spot + j + LANES].astype(F32)
                    total = total + wide * wide * w_ref[pl.ds((start + j) // LANES, 1), :]
    half_norm = 0.5 * jnp.sum(total, axis=1, keepdims=True)
    prior = jnp.concatenate([prior_ref[...], jnp.zeros((1, -rows % LANES), F32)], axis=1)
    spread = (rows, prior.shape[1])
    on_line = lax.broadcasted_iota(jnp.int32, spread, 0) == lax.broadcasted_iota(jnp.int32, spread, 1)
    prior = jnp.sum(jnp.where(on_line, prior, 0.0), axis=1, keepdims=True)
    bias_ref[...] = jnp.broadcast_to(prior - half_norm, bias_ref.shape)


def prep_projections(projections, weight, log_prior, core, side, owner, wo, ws, n):
    rows = projections.shape[1]
    half = 2 * wo + ws
    width = n * half + LANES
    if wo % LANES == 0:
        vmem = pl.BlockSpec(memory_space=pltpu.VMEM)
        keep, send = pl.pallas_call(
            functools.partial(split_kernel, wo, ws, n),
            in_specs=[pl.BlockSpec(memory_space=pl.ANY)],
            out_specs=[vmem] * 2,
            out_shape=[jax.ShapeDtypeStruct((rows, width), BF16)] * 2,
            scratch_shapes=[pltpu.SemaphoreType.DMA((6 * n,))],
            compiler_params=pltpu.CompilerParams(vmem_limit_bytes=54 * MIB),
            cost_estimate=pl.CostEstimate(flops=0, bytes_accessed=4 * projections.size, transcendentals=0),
            name="split_projections",
        )(projections)
        bias = pl.pallas_call(
            functools.partial(norm_kernel, wo, ws, n),
            in_specs=[vmem] * 4,
            out_specs=vmem,
            out_shape=jax.ShapeDtypeStruct((rows, LANES), F32),
            compiler_params=pltpu.CompilerParams(vmem_limit_bytes=16 * MIB),
            cost_estimate=pl.CostEstimate(flops=3 * projections.size, bytes_accessed=2 * projections.size, transcendentals=0),
            name="half_norms",
        )(keep, send, log_prior, weight)
        return keep, send, bias
    projection, prior = projections[0], log_prior.reshape(rows, 1)
    half_norm = 0.5 * jnp.sum(jnp.square(projection.astype(F32)) * weight, axis=1, keepdims=True)
    bias = jnp.broadcast_to(prior - half_norm, (rows, LANES))
    lane = jnp.arange(LANES, dtype=jnp.int32)
    gate = jnp.broadcast_to(jnp.where(lane == owner, MASKED, 0.0).astype(BF16)[None, :], (rows, LANES))
    split = projection.reshape(rows, n, 2, half)
    both = []
    for which in (core, 1 - core):
        own, oth, shared = cut(lax.dynamic_index_in_dim(split, which, 2, keepdims=False), side, wo)
        both.append(jnp.concatenate([own, gate, shared, oth], axis=1))
    return both[0], both[1], bias


def pack_kernel(pieces, *refs):
    arrays, outs = refs[: len(refs) - len(pieces)], refs[len(refs) - len(pieces) :]
    for out, places in zip(outs, pieces, strict=True):
        for k, rows, cols, row, col in places:
            size = (rows.stop - rows.start, cols.stop - cols.start)
            out[row : row + size[0], col : col + size[1]] = arrays[k][rows, cols]


def pack(arrays, shapes, pieces):
    vmem = pl.BlockSpec(memory_space=pltpu.VMEM)
    return pl.pallas_call(
        functools.partial(pack_kernel, pieces),
        in_specs=[vmem] * len(arrays),
        out_specs=[vmem] * len(shapes),
        out_shape=[jax.ShapeDtypeStruct(shape, BF16) for shape in shapes],
        compiler_params=pltpu.CompilerParams(vmem_limit_bytes=8 * MIB),
        name="pack",
    )(*arrays)


def score_kernel(wo, ws, kinds, aligned, own_ref, mate_ref, bias_ref, *refs):
    count = 1 + max(k for _, places in kinds for k, _ in places)
    pieces, part_ref = refs[:count], refs[count]
    rows = own_ref.shape[0]
    acc = None
    base = 0
    for width, places in kinds:
        for start in range(0, width, 1024):
            size = min(1024, width - start)
            x = jnp.concatenate([pieces[k][:, c + start : c + start + size] for k, c in places], axis=0)
            cols = slice(base + start, base + start + size)
            p = jnp.concatenate([own_ref[:, cols], mate_ref[:, cols]], axis=0)
            term = lax.dot_general(p, x, (((1,), (1,)), ((), ())), preferred_element_type=F32)
            acc = term if acc is None else acc + term
        base += width
    part_ref[:rows, :] = acc[:rows] + bias_ref[...]
    part_ref[rows:, :] = acc[rows:]
    if aligned:
        side, owner = (lax.axis_index("cls") // 2) % 2, lax.axis_index("ori")
        slice_ref = refs[count + 1]
        for (_, places), spot, size in zip(kinds, (side * wo, 2 * wo, (1 - side) * wo), (wo, ws, wo), strict=True):
            row = 0
            for k, c in places:
                p = pieces[k]
                slice_ref[row : row + p.shape[0], at(spot, size)] = p[:, at(c + owner * size, size)]
                row += p.shape[0]


def group_scores(own, mate, bias, kinds, wo, ws, n):
    aligned = wo % LANES == 0
    rows = own.shape[0]
    half = 2 * wo + ws
    count = sum(p.shape[0] for p, _ in kinds[0])
    out = [jax.ShapeDtypeStruct((2 * rows, count), F32)]
    if aligned:
        out.append(jax.ShapeDtypeStruct((count, half), BF16))
    arrays, numbered = [], []
    for places, width in zip(kinds, (n * wo + LANES, n * ws, n * wo), strict=True):
        numbered.append((width, [(len(arrays) + i, c) for i, (_, c) in enumerate(places)]))
        arrays += [p for p, _ in places]
    vmem = pl.BlockSpec(memory_space=pltpu.VMEM)
    got = pl.pallas_call(
        functools.partial(score_kernel, wo, ws, numbered, aligned),
        in_specs=[vmem] * (3 + len(arrays)),
        out_specs=[vmem] * len(out),
        out_shape=out,
        compiler_params=pltpu.CompilerParams(vmem_limit_bytes=8 * MIB),
        cost_estimate=pl.CostEstimate(
            flops=4 * rows * count * own.shape[1], bytes_accessed=4 * own.size + 2 * count * own.shape[1], transcendentals=0
        ),
        name="group_scores",
    )(own, mate, bias, *arrays)
    if aligned:
        return got
    side, owner = (lax.axis_index("cls") // 2) % 2, lax.axis_index("ori")
    cols = []
    for places, size in zip(kinds, (wo, ws, wo), strict=True):
        cols.append(jnp.concatenate([lax.dynamic_slice_in_dim(p, c + owner * size, size, 1) for p, c in places], axis=0))
    a, c, b = cols
    first, second = jnp.where(side == 0, a, b), jnp.where(side == 0, b, a)
    return got[0], jnp.concatenate([first, second, c], axis=1)


def group_order(n):
    return [(0, n // 2)] + [(d, n - d) for d in range(1, n // 2)]


def stats_kernel(n, *refs):
    groups = n // 2
    parts, recvs = refs[:groups], refs[groups : 2 * groups]
    score_ref, stat_ref = refs[2 * groups :]
    rows = score_ref.shape[0]
    per = parts[0].shape[1] // 2
    for g, pair in enumerate(group_order(n)):
        mine = parts[g][:rows, :] + recvs[g][rows:, :]
        other = parts[g][rows:, :] + recvs[g][:rows, :]
        best = jnp.maximum(jnp.max(mine, axis=0, keepdims=True), jnp.max(other, axis=0, keepdims=True))
        total = jnp.sum(jnp.exp(mine - best), axis=0, keepdims=True) + jnp.sum(jnp.exp(other - best), axis=0, keepdims=True)
        for h, r in enumerate(pair):
            cols, held = slice(r * per, (r + 1) * per), slice(h * per, (h + 1) * per)
            score_ref[:, cols] = mine[:, held]
            stat_ref[0:1, cols] = best[:, held]
            stat_ref[1:2, cols] = total[:, held]
    stat_ref[2:8, :] = jnp.zeros((6, stat_ref.shape[1]), F32)


def payload_kernel(turns, score_ref, *refs):
    stats, out_ref = refs[:turns], refs[turns]
    rows = score_ref.shape[0]
    plane = lax.axis_index("cls") // 2
    best = functools.reduce(jnp.maximum, [s[0:1, :] for s in stats])
    terms = [s[1:2, :] * jnp.exp(s[0:1, :] - best) for s in stats]
    total = None
    for a in range(turns):
        back = lax.rem(plane - a + turns, turns)
        term = sum(jnp.where(back == j, terms[j], 0.0) for j in range(turns))
        total = term if total is None else total + term
    out_ref[:rows, :] = jnp.exp(score_ref[...] - best).astype(BF16)
    left = jnp.concatenate([best, total], axis=0)
    levels = []
    for _ in range(3):
        piece = left.astype(BF16).astype(F32)
        levels.append(piece)
        left = left - piece
    levels.append(jnp.zeros((TAIL - 6, best.shape[1]), F32))
    out_ref[rows:, :] = jnp.concatenate(levels, axis=0).astype(BF16)


def sums_kernel(n, rows, per_half, cycle, *refs):
    owner = lax.axis_index("ori")
    spot = sum(jnp.where(owner == o, cycle.index(o), 0) for o in range(n))
    payloads, refs = refs[:n], refs[n:]
    groups = n // 2
    w_own, w_oth = refs[:groups], refs[groups:-3]
    out_ref, evidence_ref, posterior = refs[-3:]
    step = pl.program_id(0)
    width = payloads[0].shape[1]
    per = width // n

    @pl.when(step == 0)
    def _():
        tops, sums = [], []
        for d in range(n):
            stat = payloads[d][rows:, :].astype(F32)
            stat = jnp.concatenate([stat[0:2] + stat[2:4] + stat[4:6], jnp.zeros((6, width), F32)], axis=0)
            stat = pltpu.roll(stat, per * d, 1) if d else stat
            tops.append(stat[0:1])
            sums.append(stat[1:2])
        best = functools.reduce(jnp.maximum, tops)
        grow = [jnp.exp(t - best) for t in tops]
        total = functools.reduce(lambda a, b: a + b, [s * g for s, g in zip(sums, grow, strict=True)])
        evidence_ref[...] = (best + jnp.log(total))[:, :per]
        for d in range(n):
            wide = payloads[d][:rows, :].astype(F32)
            wide = pltpu.roll(wide, per * d, 1) if d else wide
            back = lax.rem(spot + (n - d), n)
            block = sum(jnp.where(back == p, cycle[p], 0) for p in range(n))
            row = pl.multiple_of(block * rows, 16)
            posterior[pl.ds(row, rows), :] = (wide * (grow[d] / total)).astype(BF16)

    places = {r: (g, h) for g, pair in enumerate(group_order(n)) for h, r in enumerate(pair)}
    first = (step < per_half) == (lax.axis_index("cls") % 2 == 0)
    pieces = []
    for r in range(n):
        g, h = places[r]
        held = slice(h * per, (h + 1) * per)
        pieces.append(jnp.where(first, w_own[g][held, :], w_oth[g][held, :]) if per_half else w_own[g][held, :])
    left = posterior[...]
    if not per_half:
        left = posterior[pl.ds(pl.multiple_of(step * out_ref.shape[0], 16), out_ref.shape[0]), :]
    out_ref[...] = jnp.dot(left, jnp.concatenate(pieces, axis=0), preferred_element_type=F32).astype(BF16)


def tie(*values):
    return lax.optimization_barrier(values)


def body(images, projections, log_prior, significant, shell_index, noise_inv):
    n = lax.axis_size("ori")
    n_cls = lax.axis_size("cls")
    turns = n_cls // 2
    owner = lax.axis_index("ori")
    cls = lax.axis_index("cls")
    core, side = cls % 2, (cls // 2) % 2
    rows, freqs = images.shape
    ori_rows = projections.shape[1]
    half = freqs // n // 2
    wo = 3 * half // 10
    ws = half - 2 * wo
    cycle = cycle_of(n)
    far = n // 2

    def ring(x, d):
        return lax.ppermute(x, "ori", [(cycle[i], cycle[(i + d) % n]) for i in range(n)])

    def swap(x):
        return lax.ppermute(x, "cls", [(i, i ^ 1) for i in range(n_cls)])

    def cross(x):
        return lax.ppermute(x, "cls", [(i, i ^ 2) for i in range(n_cls)])

    weight_of = (shell_index.reshape(freqs // LANES, LANES), noise_inv.reshape(1, -1))
    own, oth, shared, weight = prep_images(images, weight_of, significant, core, side, wo, ws, n)
    projections, own, oth, shared = tie(projections, own, oth, shared)
    keep, send, bias = prep_projections(projections, weight, log_prior, core, side, owner, wo, ws, n)

    cut_at = rows // 2
    every, top, bottom = slice(0, rows), slice(0, cut_at), slice(cut_at, rows)
    plane_w, shared_w = n * wo + LANES, n * ws
    plane_cols, cross_cols = slice(0, plane_w), slice(0, n * wo)
    shared_cols = slice(plane_w, plane_w + shared_w)
    f, b = ring(own, 1), ring(own, -1)
    f, b, shared, send = tie(f, b, shared, send)
    whole = slice(0, shared_w)
    mates = swap(send)
    both, x_in = [None], None
    f2, b2, x_in = pack(
        [f, b, shared],
        [(rows, plane_w + shared_w)] * 2 + [(2 * rows, n * wo)],
        [[(i, every, plane_cols, 0, 0), (2, every, whole, 0, plane_w)] for i in (0, 1)]
        + [[(0, every, cross_cols, 0, 0), (1, every, cross_cols, rows, 0)]],
    )
    both = [(f2, b2)]
    parts, slices = [None] * far, [None] * far
    crossed = [None]
    for s in range(1, far - 1):
        f, b = both[-1]
        f, b, x = ring(f, 1), ring(b, -1), cross(x_in)
        if s == 1:
            f, b, x, mates = tie(f, b, x, mates)
        else:
            f, b, x, parts[s - 1], slices[s - 1] = tie(f, b, x, parts[s - 1], slices[s - 1])
        both.append((f, b))
        crossed.append(x)
        kinds = ([(p, 0) for p in both[s - 1]], [(p, plane_w) for p in both[s]], [(x, 0)])
        parts[s], slices[s] = group_scores(keep, mates, bias, kinds, wo, ws, n)
        if s < far - 2:
            (x_in,) = pack([f, b], [(2 * rows, n * wo)], [[(0, every, cross_cols, 0, 0), (1, every, cross_cols, rows, 0)]])
    x_in, fo, bo, fs, bs = pack(
        [f, b],
        [(2 * rows, n * wo)] + [(cut_at, plane_w)] * 2 + [(rows, shared_w)] * 2,
        [
            [(0, every, cross_cols, 0, 0), (1, every, cross_cols, rows, 0)],
            [(0, top, plane_cols, 0, 0)],
            [(1, bottom, plane_cols, 0, 0)],
            [(0, every, shared_cols, 0, 0)],
            [(1, every, shared_cols, 0, 0)],
        ],
    )
    fo, bo, fs, bs, x = ring(fo, 1), ring(bo, -1), ring(fs, 1), ring(bs, -1), cross(x_in)
    fo, bo, fs, bs, x, parts[far - 2], slices[far - 2] = tie(fo, bo, fs, bs, x, parts[far - 2], slices[far - 2])
    kinds = ([(p, 0) for p in both[far - 2]], [(fs, 0), (bs, 0)], [(x, 0)])
    parts[far - 1], slices[far - 1] = group_scores(keep, mates, bias, kinds, wo, ws, n)
    (x_in,) = pack([fo, bo], [(rows, n * wo)], [[(0, top, cross_cols, 0, 0), (1, top, cross_cols, cut_at, 0)]])
    fs, bs, x = ring(fs[:cut_at], 1), ring(bs[cut_at:], -1), cross(x_in)
    kinds = ([(own, 0), (fo, 0), (bo, 0)], [(shared, 0), (fs, 0), (bs, 0)], [(oth, 0), (x, 0)])
    parts[0], slices[0] = group_scores(keep, mates, bias, kinds, wo, ws, n)
    recvs = [swap(p) for p in parts]
    other_slices = [swap(x) for x in slices]

    vmem = pl.BlockSpec(memory_space=pltpu.VMEM)
    width = n * rows
    scores, stats = pl.pallas_call(
        functools.partial(stats_kernel, n),
        in_specs=[vmem] * (2 * far),
        out_specs=[vmem, vmem],
        out_shape=[jax.ShapeDtypeStruct((ori_rows, width), F32), jax.ShapeDtypeStruct((8, width), F32)],
        compiler_params=pltpu.CompilerParams(vmem_limit_bytes=16 * MIB),
        name="local_stats",
    )(*parts, *recvs)
    all_stats = [stats] + [
        lax.ppermute(stats, "cls", [(i, (i + 2 * j) % n_cls) for i in range(n_cls)]) for j in range(1, turns)
    ]
    payload = pl.pallas_call(
        functools.partial(payload_kernel, turns),
        in_specs=[vmem] * (1 + turns),
        out_specs=vmem,
        out_shape=jax.ShapeDtypeStruct((ori_rows + TAIL, width), BF16),
        compiler_params=pltpu.CompilerParams(vmem_limit_bytes=16 * MIB),
        name="payload",
    )(scores, *all_stats)
    payloads = [payload] + [None] * (n - 1)
    fp = bp = payload
    payloads[far] = ring(payload, far)
    for d in range(1, far):
        fp = payloads[d] = ring(fp, 1)
        bp = payloads[n - d] = ring(bp, -1)

    fixed = lambda i: (0, 0)
    per_half = half // COLS if half % COLS == 0 else 0
    if per_half:
        steps = 2 * per_half
        w = slices + other_slices
        w_specs = [pl.BlockSpec((LANES, COLS), lambda i: (0, lax.rem(i, per_half)))] * len(w)
        out_spec = pl.BlockSpec((n * ori_rows, COLS), lambda i: (0, i))
        grant = 40
    else:
        steps = max(1, n // 2)
        w = [
            jnp.concatenate([jnp.where(core == 0, a, b), jnp.where(core == 0, b, a)], axis=1)
            for a, b in zip(slices, other_slices, strict=True)
        ]
        w_specs = [pl.BlockSpec((LANES, 2 * half), fixed, pipeline_mode=pl.Buffered(1))] * len(w)
        out_spec = pl.BlockSpec((n * ori_rows // steps, 2 * half), lambda i: (i, 0))
        grant = 62
    held_once = pl.BlockSpec(payload.shape, fixed, pipeline_mode=pl.Buffered(1))
    sums, evidence = pl.pallas_call(
        functools.partial(sums_kernel, n, ori_rows, per_half, cycle),
        grid=(steps,),
        in_specs=[held_once] * n + w_specs,
        out_specs=[out_spec, pl.BlockSpec((1, rows), fixed)],
        scratch_shapes=[pltpu.VMEM((n * ori_rows, width), BF16)],
        out_shape=[jax.ShapeDtypeStruct((n * ori_rows, 2 * half), BF16), jax.ShapeDtypeStruct((1, rows), F32)],
        compiler_params=pltpu.CompilerParams(vmem_limit_bytes=grant * MIB),
        name="class_sums",
    )(*payloads, *w)
    return sums[None], evidence.reshape(rows)


def solution(mesh):
    in_specs = (P("ori", None), P("cls", "ori", None), P("cls", "ori"), P("ori", None), P(), P())
    out_specs = (P("cls", None, "ori"), P("ori"))
    return jax.shard_map(body, mesh=mesh, in_specs=in_specs, out_specs=out_specs, check_vma=False)
```

```python
import functools
import math

import jax
import jax.numpy as jnp
from jax import lax
from jax.experimental import pallas as pl
from jax.experimental.pallas import tpu as pltpu
from jax.sharding import PartitionSpec as P

BF16 = jnp.bfloat16
F32 = jnp.float32
MASKED = -1e30
LANES = 128
MIB = 1 << 20
TAIL = 16
CHUNKS = 4


def cycle_of(count):
    deep = math.isqrt(count // 2)
    tall = count // deep
    walk = [(z, 0) for z in range(tall)]
    for z in range(tall - 1, -1, -1):
        cols = list(range(1, deep))
        walk += [(z, y) for y in (cols if (tall - 1 - z) % 2 == 0 else cols[::-1])]
    return [z * deep + y for z, y in walk]


def weight_table(index, noise):
    levels = noise.shape[1]
    row = jnp.concatenate([noise, jnp.zeros((1, LANES - levels), F32)], axis=1)
    table = jnp.broadcast_to(row, index.shape)
    return jnp.take_along_axis(table, index, axis=1, mode="promise_in_bounds")


def at(start, size):
    return pl.ds(pl.multiple_of(start, LANES), size)


def weigh(n, half, pieces, img, w_ref):
    core = lax.axis_index("cls") % 2
    for i in range(n):
        yield i
        for ref, first, start, count in pieces:
            for j in range(0, count, LANES):
                weight = w_ref[pl.ds(((2 * i + core) * half + start + j) // LANES, 1), :]
                wide = img[:, at(first + i * count + j, LANES)].astype(F32) * weight
                ref[:, i * count + j : i * count + j + LANES] = wide.astype(BF16)


def own_kernel(n, wo, ws, img_hbm, index_hbm, noise_hbm, sig_hbm, own_ref, w_ref, img, index, noise, sig, sems):
    cls = lax.axis_index("cls")
    core, side = cls % 2, (cls // 2) % 2
    half = 2 * wo + ws
    small = [(index_hbm, index), (noise_hbm, noise), (sig_hbm, sig)]
    copies = [pltpu.make_async_copy(src, dst, sems.at[n + i]) for i, (src, dst) in enumerate(small)]
    loads = []
    for i in range(n):
        src = img_hbm.at[:, at((2 * i + core) * half + side * wo, wo)]
        loads.append(pltpu.make_async_copy(src, img.at[:, i * wo : (i + 1) * wo], sems.at[i]))
    for copy in copies + loads:
        copy.start()
    for copy in copies:
        copy.wait()
    w_ref[...] = weight_table(index[...], noise[...])
    rows = img.shape[0]
    block = lax.broadcasted_iota(jnp.int32, (LANES, rows), 0)
    listed = block < 0
    for j in range(sig.shape[0]):
        listed = listed | (sig[j : j + 1, :] == block)
    unlisted = jnp.where(listed, 0.0, 1.0).astype(BF16)
    same = lax.broadcasted_iota(jnp.int32, (rows, rows), 0) == lax.broadcasted_iota(jnp.int32, (rows, rows), 1)
    eye = jnp.where(same, 1.0, 0.0).astype(BF16)
    turned = lax.dot_general(eye, unlisted, (((1,), (1,)), ((), ())), preferred_element_type=F32)
    own_ref[:, n * wo :] = turned.astype(BF16)
    for i in weigh(n, half, [(own_ref, 0, side * wo, wo)], img, w_ref):
        loads[i].wait()


def rest_kernel(n, wo, ws, img_hbm, w_ref, oth_ref, shared_ref, img, sems):
    cls = lax.axis_index("cls")
    core, side = cls % 2, (cls // 2) % 2
    half = 2 * wo + ws
    loads = []
    for i in range(n):
        base = (2 * i + core) * half
        for k, start, first, count in ((0, (1 - side) * wo, i * wo, wo), (1, 2 * wo, n * wo + i * ws, ws)):
            src = img_hbm.at[:, at(base + start, count)]
            loads.append(pltpu.make_async_copy(src, img.at[:, first : first + count], sems.at[2 * i + k]))
            loads[-1].start()
    pieces = [(oth_ref, 0, (1 - side) * wo, wo), (shared_ref, n * wo, 2 * wo, ws)]
    for i in weigh(n, half, pieces, img, w_ref):
        loads[2 * i].wait()
        loads[2 * i + 1].wait()


def prep_images(images, weight_of, significant, core, side, wo, ws, n):
    rows = images.shape[0]
    half = 2 * wo + ws
    if wo % LANES == 0:
        index, noise = weight_of
        sig = significant.T
        vmem, somewhere = pl.BlockSpec(memory_space=pltpu.VMEM), pl.BlockSpec(memory_space=pl.ANY)
        own, weight = pl.pallas_call(
            functools.partial(own_kernel, n, wo, ws),
            in_specs=[somewhere] * 4,
            out_specs=[vmem] * 2,
            out_shape=[jax.ShapeDtypeStruct((rows, n * wo + LANES), BF16), jax.ShapeDtypeStruct(index.shape, F32)],
            scratch_shapes=[
                pltpu.VMEM((rows, n * wo), BF16),
                pltpu.VMEM(index.shape, index.dtype),
                pltpu.VMEM(noise.shape, F32),
                pltpu.VMEM(sig.shape, sig.dtype),
                pltpu.SemaphoreType.DMA((n + 3,)),
            ],
            compiler_params=pltpu.CompilerParams(vmem_limit_bytes=61 * MIB),
            name="prep_own_plane",
        )(images, index, noise, sig)
        oth, shared = pl.pallas_call(
            functools.partial(rest_kernel, n, wo, ws),
            in_specs=[somewhere, vmem],
            out_specs=[vmem] * 2,
            out_shape=[jax.ShapeDtypeStruct((rows, n * wo), BF16), jax.ShapeDtypeStruct((rows, n * ws), BF16)],
            scratch_shapes=[pltpu.VMEM((rows, n * (wo + ws)), BF16), pltpu.SemaphoreType.DMA((2 * n,))],
            compiler_params=pltpu.CompilerParams(vmem_limit_bytes=58 * MIB),
            name="prep_rest",
        )(images, weight)
        return own, oth, shared, weight
    weight = full_weights(weight_of)
    weighted = (images.astype(F32) * weight).astype(BF16).reshape(rows, n, 2, half)
    mine = lax.dynamic_index_in_dim(weighted, core, 2, keepdims=False)
    own, oth, shared = cut(mine, side, wo)
    lane = jnp.arange(LANES, dtype=jnp.int32)
    listed = jnp.any(significant[:, :, None] == lane[None, None, :], axis=1)
    return jnp.concatenate([own, jnp.where(listed, 0.0, 1.0).astype(BF16)], axis=1), oth, shared, weight


def full_weights(weight_of):
    index, noise = weight_of
    levels = jnp.arange(noise.shape[1], dtype=jnp.int32)
    return jnp.sum(jnp.where(index.reshape(-1, 1) == levels[None, :], noise, 0.0), axis=1)[None, :]


def cut(mine, side, wo):
    rows, n, _ = mine.shape
    own = lax.dynamic_slice_in_dim(mine, side * wo, wo, 2).reshape(rows, n * wo)
    oth = lax.dynamic_slice_in_dim(mine, (1 - side) * wo, wo, 2).reshape(rows, n * wo)
    return own, oth, mine[:, :, 2 * wo :].reshape(rows, -1)


def split_kernel(wo, ws, n, proj_hbm, keep_ref, send_ref, sems):
    half = 2 * wo + ws
    cls, owner = lax.axis_index("cls"), lax.axis_index("ori")
    core, side = cls % 2, (cls // 2) % 2
    copies = []
    for ref, which in ((send_ref, 1 - core), (keep_ref, core)):
        for i in range(n):
            base = (2 * i + which) * half
            for start, spot, count in (
                (base + side * wo, i * wo, wo),
                (base + 2 * wo, n * wo + LANES + i * ws, ws),
                (base + (1 - side) * wo, n * (wo + ws) + LANES + i * wo, wo),
            ):
                src = proj_hbm.at[0, :, at(start, count)]
                copies.append(pltpu.make_async_copy(src, ref.at[:, spot : spot + count], sems.at[len(copies)]))
                copies[-1].start()
    lane = lax.broadcasted_iota(jnp.int32, (keep_ref.shape[0], LANES), 1)
    gate = jnp.where(lane == owner, MASKED, 0.0).astype(BF16)
    keep_ref[:, n * wo : n * wo + LANES] = gate
    send_ref[:, n * wo : n * wo + LANES] = gate
    for copy in copies:
        copy.wait()


def norm_kernel(wo, ws, n, keep_ref, send_ref, prior_ref, w_ref, bias_ref):
    half = 2 * wo + ws
    cls = lax.axis_index("cls")
    core, side = cls % 2, (cls // 2) % 2
    rows = keep_ref.shape[0]
    total = jnp.zeros((rows, LANES), F32)
    for ref, which in ((keep_ref, core), (send_ref, 1 - core)):
        for i in range(n):
            base = (2 * i + which) * half
            for start, spot, count in (
                (base + side * wo, i * wo, wo),
                (base + 2 * wo, n * wo + LANES + i * ws, ws),
                (base + (1 - side) * wo, n * (wo + ws) + LANES + i * wo, wo),
            ):
                for j in range(0, count, LANES):
                    wide = ref[:, spot + j : spot + j + LANES].astype(F32)
                    total = total + wide * wide * w_ref[pl.ds((start + j) // LANES, 1), :]
    half_norm = 0.5 * jnp.sum(total, axis=1, keepdims=True)
    prior = jnp.concatenate([prior_ref[...], jnp.zeros((1, -rows % LANES), F32)], axis=1)
    spread = (rows, prior.shape[1])
    on_line = lax.broadcasted_iota(jnp.int32, spread, 0) == lax.broadcasted_iota(jnp.int32, spread, 1)
    prior = jnp.sum(jnp.where(on_line, prior, 0.0), axis=1, keepdims=True)
    bias_ref[...] = jnp.broadcast_to(prior - half_norm, bias_ref.shape)


def prep_projections(projections, weight, log_prior, core, side, owner, wo, ws, n):
    rows = projections.shape[1]
    half = 2 * wo + ws
    width = n * half + LANES
    if wo % LANES == 0:
        vmem = pl.BlockSpec(memory_space=pltpu.VMEM)
        keep, send = pl.pallas_call(
            functools.partial(split_kernel, wo, ws, n),
            in_specs=[pl.BlockSpec(memory_space=pl.ANY)],
            out_specs=[vmem] * 2,
            out_shape=[jax.ShapeDtypeStruct((rows, width), BF16)] * 2,
            scratch_shapes=[pltpu.SemaphoreType.DMA((6 * n,))],
            compiler_params=pltpu.CompilerParams(vmem_limit_bytes=54 * MIB),
            cost_estimate=pl.CostEstimate(flops=0, bytes_accessed=4 * projections.size, transcendentals=0),
            name="split_projections",
        )(projections)
        bias = pl.pallas_call(
            functools.partial(norm_kernel, wo, ws, n),
            in_specs=[vmem] * 4,
            out_specs=vmem,
            out_shape=jax.ShapeDtypeStruct((rows, LANES), F32),
            compiler_params=pltpu.CompilerParams(vmem_limit_bytes=16 * MIB),
            cost_estimate=pl.CostEstimate(flops=3 * projections.size, bytes_accessed=2 * projections.size, transcendentals=0),
            name="half_norms",
        )(keep, send, log_prior, weight)
        return keep, send, bias
    projection, prior = projections[0], log_prior.reshape(rows, 1)
    half_norm = 0.5 * jnp.sum(jnp.square(projection.astype(F32)) * weight, axis=1, keepdims=True)
    bias = jnp.broadcast_to(prior - half_norm, (rows, LANES))
    lane = jnp.arange(LANES, dtype=jnp.int32)
    gate = jnp.broadcast_to(jnp.where(lane == owner, MASKED, 0.0).astype(BF16)[None, :], (rows, LANES))
    split = projection.reshape(rows, n, 2, half)
    both = []
    for which in (core, 1 - core):
        own, oth, shared = cut(lax.dynamic_index_in_dim(split, which, 2, keepdims=False), side, wo)
        both.append(jnp.concatenate([own, gate, shared, oth], axis=1))
    return both[0], both[1], bias


def pack_kernel(pieces, *refs):
    arrays, outs = refs[: len(refs) - len(pieces)], refs[len(refs) - len(pieces) :]
    for out, places in zip(outs, pieces, strict=True):
        for k, rows, cols, row, col in places:
            size = (rows.stop - rows.start, cols.stop - cols.start)
            out[row : row + size[0], col : col + size[1]] = arrays[k][rows, cols]


def pack(arrays, shapes, pieces):
    vmem = pl.BlockSpec(memory_space=pltpu.VMEM)
    return pl.pallas_call(
        functools.partial(pack_kernel, pieces),
        in_specs=[vmem] * len(arrays),
        out_specs=[vmem] * len(shapes),
        out_shape=[jax.ShapeDtypeStruct(shape, BF16) for shape in shapes],
        compiler_params=pltpu.CompilerParams(vmem_limit_bytes=8 * MIB),
        name="pack",
    )(*arrays)


def score_kernel(wo, ws, kinds, aligned, own_ref, mate_ref, bias_ref, *refs):
    count = 1 + max(k for _, places in kinds for k, _ in places)
    pieces, part_ref = refs[:count], refs[count]
    rows = own_ref.shape[0]
    acc = None
    base = 0
    for width, places in kinds:
        for start in range(0, width, 1024):
            size = min(1024, width - start)
            x = jnp.concatenate([pieces[k][:, c + start : c + start + size] for k, c in places], axis=0)
            cols = slice(base + start, base + start + size)
            p = jnp.concatenate([own_ref[:, cols], mate_ref[:, cols]], axis=0)
            term = lax.dot_general(p, x, (((1,), (1,)), ((), ())), preferred_element_type=F32)
            acc = term if acc is None else acc + term
        base += width
    part_ref[:rows, :] = acc[:rows] + bias_ref[...]
    part_ref[rows:, :] = acc[rows:]
    if aligned:
        side, owner = (lax.axis_index("cls") // 2) % 2, lax.axis_index("ori")
        slice_ref = refs[count + 1]
        for (_, places), spot, size in zip(kinds, (side * wo, 2 * wo, (1 - side) * wo), (wo, ws, wo), strict=True):
            row = 0
            for k, c in places:
                p = pieces[k]
                slice_ref[row : row + p.shape[0], at(spot, size)] = p[:, at(c + owner * size, size)]
                row += p.shape[0]


def group_scores(own, mate, bias, kinds, wo, ws, n):
    aligned = wo % LANES == 0
    rows = own.shape[0]
    half = 2 * wo + ws
    count = sum(p.shape[0] for p, _ in kinds[0])
    out = [jax.ShapeDtypeStruct((2 * rows, count), F32)]
    if aligned:
        out.append(jax.ShapeDtypeStruct((count, half), BF16))
    arrays, numbered = [], []
    for places, width in zip(kinds, (n * wo + LANES, n * ws, n * wo), strict=True):
        numbered.append((width, [(len(arrays) + i, c) for i, (_, c) in enumerate(places)]))
        arrays += [p for p, _ in places]
    vmem = pl.BlockSpec(memory_space=pltpu.VMEM)
    got = pl.pallas_call(
        functools.partial(score_kernel, wo, ws, numbered, aligned),
        in_specs=[vmem] * (3 + len(arrays)),
        out_specs=[vmem] * len(out),
        out_shape=out,
        compiler_params=pltpu.CompilerParams(vmem_limit_bytes=8 * MIB),
        cost_estimate=pl.CostEstimate(
            flops=4 * rows * count * own.shape[1], bytes_accessed=4 * own.size + 2 * count * own.shape[1], transcendentals=0
        ),
        name="group_scores",
    )(own, mate, bias, *arrays)
    if aligned:
        return got
    side, owner = (lax.axis_index("cls") // 2) % 2, lax.axis_index("ori")
    cols = []
    for places, size in zip(kinds, (wo, ws, wo), strict=True):
        cols.append(jnp.concatenate([lax.dynamic_slice_in_dim(p, c + owner * size, size, 1) for p, c in places], axis=0))
    a, c, b = cols
    first, second = jnp.where(side == 0, a, b), jnp.where(side == 0, b, a)
    return got[0], jnp.concatenate([first, second, c], axis=1)


def group_order(n):
    return [(0, n // 2)] + [(d, n - d) for d in range(1, n // 2)]


def stats_kernel(n, *refs):
    groups = n // 2
    parts, recvs = refs[:groups], refs[groups : 2 * groups]
    score_ref, stat_ref = refs[2 * groups :]
    rows = score_ref.shape[0]
    per = parts[0].shape[1] // 2
    for g, pair in enumerate(group_order(n)):
        mine = parts[g][:rows, :] + recvs[g][rows:, :]
        other = parts[g][rows:, :] + recvs[g][:rows, :]
        best = jnp.maximum(jnp.max(mine, axis=0, keepdims=True), jnp.max(other, axis=0, keepdims=True))
        total = jnp.sum(jnp.exp(mine - best), axis=0, keepdims=True) + jnp.sum(jnp.exp(other - best), axis=0, keepdims=True)
        for h, r in enumerate(pair):
            cols, held = slice(r * per, (r + 1) * per), slice(h * per, (h + 1) * per)
            score_ref[:, cols] = mine[:, held]
            stat_ref[0:1, cols] = best[:, held]
            stat_ref[1:2, cols] = total[:, held]
    stat_ref[2:8, :] = jnp.zeros((6, stat_ref.shape[1]), F32)


def payload_kernel(turns, score_ref, *refs):
    stats, out_ref = refs[:turns], refs[turns]
    rows = score_ref.shape[0]
    plane = lax.axis_index("cls") // 2
    best = functools.reduce(jnp.maximum, [s[0:1, :] for s in stats])
    terms = [s[1:2, :] * jnp.exp(s[0:1, :] - best) for s in stats]
    total = None
    for a in range(turns):
        back = lax.rem(plane - a + turns, turns)
        term = sum(jnp.where(back == j, terms[j], 0.0) for j in range(turns))
        total = term if total is None else total + term
    out_ref[:rows, :] = jnp.exp(score_ref[...] - best).astype(BF16)
    left = jnp.concatenate([best, total], axis=0)
    levels = []
    for _ in range(3):
        piece = left.astype(BF16).astype(F32)
        levels.append(piece)
        left = left - piece
    levels.append(jnp.zeros((TAIL - 6, best.shape[1]), F32))
    out_ref[rows:, :] = jnp.concatenate(levels, axis=0).astype(BF16)


def scale_posteriors(n, rows, cycle, payloads, posterior, evidence_ref):
    owner = lax.axis_index("ori")
    spot = sum(jnp.where(owner == o, cycle.index(o), 0) for o in range(n))
    width = payloads[0].shape[1]
    per = width // n
    tops, sums = [], []
    for d in range(n):
        stat = payloads[d][rows:, :].astype(F32)
        stat = jnp.concatenate([stat[0:2] + stat[2:4] + stat[4:6], jnp.zeros((6, width), F32)], axis=0)
        stat = pltpu.roll(stat, per * d, 1) if d else stat
        tops.append(stat[0:1])
        sums.append(stat[1:2])
    best = functools.reduce(jnp.maximum, tops)
    grow = [jnp.exp(t - best) for t in tops]
    total = functools.reduce(lambda a, b: a + b, [s * g for s, g in zip(sums, grow, strict=True)])
    evidence_ref[...] = (best + jnp.log(total))[:, :per]
    for d in range(n):
        wide = payloads[d][:rows, :].astype(F32)
        wide = pltpu.roll(wide, per * d, 1) if d else wide
        back = lax.rem(spot + (n - d), n)
        block = sum(jnp.where(back == p, cycle[p], 0) for p in range(n))
        row = pl.multiple_of(block * rows, 16)
        posterior[pl.ds(row, rows), :] = (wide * (grow[d] / total)).astype(BF16)


def images_in_order(n, w):
    per = w[0].shape[0] // 2
    places = {r: (g, h) for g, pair in enumerate(group_order(n)) for h, r in enumerate(pair)}
    return jnp.concatenate([w[places[r][0]][places[r][1] * per : (places[r][1] + 1) * per, :] for r in range(n)], axis=0)


def stream_kernel(n, rows, cycle, *refs):
    payloads, refs = refs[:n], refs[n:]
    groups = n // 2
    halves = (refs[:groups], refs[groups : 2 * groups])
    out_hbm, evidence_ref, posterior, held, sems = refs[2 * groups :]
    scale_posteriors(n, rows, cycle, payloads, posterior, evidence_ref)
    core = lax.axis_index("cls") % 2
    half = held.shape[1] // 2
    tall = held.shape[0] // CHUNKS
    copies = []
    for h, w in enumerate(halves):
        which = core if h == 0 else 1 - core
        right = images_in_order(n, w)
        for c in range(CHUNKS):
            part, cols = slice(c * tall, (c + 1) * tall), slice(h * half, (h + 1) * half)
            held[part, cols] = jnp.dot(posterior[part, :], right, preferred_element_type=F32).astype(BF16)
            target = out_hbm.at[part, at(which * half, half)]
            copies.append(pltpu.make_async_copy(held.at[part, cols], target, sems.at[len(copies)]))
            copies[-1].start()
    for copy in copies:
        copy.wait()


def sums_kernel(n, rows, cycle, *refs):
    payloads, refs = refs[:n], refs[n:]
    w, (out_ref, evidence_ref, posterior) = refs[:-3], refs[-3:]
    step = pl.program_id(0)

    @pl.when(step == 0)
    def _():
        scale_posteriors(n, rows, cycle, payloads, posterior, evidence_ref)

    left = posterior[pl.ds(pl.multiple_of(step * out_ref.shape[0], 16), out_ref.shape[0]), :]
    out_ref[...] = jnp.dot(left, images_in_order(n, w), preferred_element_type=F32).astype(BF16)


def tie(*values):
    return lax.optimization_barrier(values)


def body(images, projections, log_prior, significant, shell_index, noise_inv):
    n = lax.axis_size("ori")
    n_cls = lax.axis_size("cls")
    turns = n_cls // 2
    owner = lax.axis_index("ori")
    cls = lax.axis_index("cls")
    core, side = cls % 2, (cls // 2) % 2
    rows, freqs = images.shape
    ori_rows = projections.shape[1]
    half = freqs // n // 2
    wo = 3 * half // 10
    ws = half - 2 * wo
    cycle = cycle_of(n)
    far = n // 2

    def ring(x, d):
        return lax.ppermute(x, "ori", [(cycle[i], cycle[(i + d) % n]) for i in range(n)])

    def swap(x):
        return lax.ppermute(x, "cls", [(i, i ^ 1) for i in range(n_cls)])

    def cross(x):
        return lax.ppermute(x, "cls", [(i, i ^ 2) for i in range(n_cls)])

    weight_of = (shell_index.reshape(freqs // LANES, LANES), noise_inv.reshape(1, -1))
    own, oth, shared, weight = prep_images(images, weight_of, significant, core, side, wo, ws, n)
    projections, own = tie(projections, own)
    keep, send, bias = prep_projections(projections, weight, log_prior, core, side, owner, wo, ws, n)

    cut_at = rows // 2
    every, top, bottom = slice(0, rows), slice(0, cut_at), slice(cut_at, rows)
    plane_w, shared_w = n * wo + LANES, n * ws
    plane_cols, cross_cols = slice(0, plane_w), slice(0, n * wo)
    shared_cols = slice(plane_w, plane_w + shared_w)
    f, b = ring(own, 1), ring(own, -1)
    f, b, shared, send = tie(f, b, shared, send)
    whole = slice(0, shared_w)
    mates = swap(send)
    both, x_in = [None], None
    f2, b2, x_in = pack(
        [f, b, shared],
        [(rows, plane_w + shared_w)] * 2 + [(2 * rows, n * wo)],
        [[(i, every, plane_cols, 0, 0), (2, every, whole, 0, plane_w)] for i in (0, 1)]
        + [[(0, every, cross_cols, 0, 0), (1, every, cross_cols, rows, 0)]],
    )
    both = [(f2, b2)]
    parts, slices = [None] * far, [None] * far
    crossed = [None]
    for s in range(1, far - 1):
        f, b = both[-1]
        f, b, x = ring(f, 1), ring(b, -1), cross(x_in)
        if s == 1:
            f, b, x, mates = tie(f, b, x, mates)
        else:
            f, b, x, parts[s - 1], slices[s - 1] = tie(f, b, x, parts[s - 1], slices[s - 1])
        both.append((f, b))
        crossed.append(x)
        kinds = ([(p, 0) for p in both[s - 1]], [(p, plane_w) for p in both[s]], [(x, 0)])
        parts[s], slices[s] = group_scores(keep, mates, bias, kinds, wo, ws, n)
        if s < far - 2:
            (x_in,) = pack([f, b], [(2 * rows, n * wo)], [[(0, every, cross_cols, 0, 0), (1, every, cross_cols, rows, 0)]])
    x_in, fo, bo, fs, bs = pack(
        [f, b],
        [(2 * rows, n * wo)] + [(cut_at, plane_w)] * 2 + [(rows, shared_w)] * 2,
        [
            [(0, every, cross_cols, 0, 0), (1, every, cross_cols, rows, 0)],
            [(0, top, plane_cols, 0, 0)],
            [(1, bottom, plane_cols, 0, 0)],
            [(0, every, shared_cols, 0, 0)],
            [(1, every, shared_cols, 0, 0)],
        ],
    )
    fo, bo, fs, bs, x = ring(fo, 1), ring(bo, -1), ring(fs, 1), ring(bs, -1), cross(x_in)
    fo, bo, fs, bs, x, parts[far - 2], slices[far - 2] = tie(fo, bo, fs, bs, x, parts[far - 2], slices[far - 2])
    kinds = ([(p, 0) for p in both[far - 2]], [(fs, 0), (bs, 0)], [(x, 0)])
    parts[far - 1], slices[far - 1] = group_scores(keep, mates, bias, kinds, wo, ws, n)
    (x_in,) = pack([fo, bo], [(rows, n * wo)], [[(0, top, cross_cols, 0, 0), (1, top, cross_cols, cut_at, 0)]])
    fs, bs, x = ring(fs[:cut_at], 1), ring(bs[cut_at:], -1), cross(x_in)
    kinds = ([(own, 0), (fo, 0), (bo, 0)], [(shared, 0), (fs, 0), (bs, 0)], [(oth, 0), (x, 0)])
    parts[0], slices[0] = group_scores(keep, mates, bias, kinds, wo, ws, n)
    recvs = [swap(p) for p in parts]
    other_slices = [swap(x) for x in slices]

    vmem = pl.BlockSpec(memory_space=pltpu.VMEM)
    width = n * rows
    scores, stats = pl.pallas_call(
        functools.partial(stats_kernel, n),
        in_specs=[vmem] * (2 * far),
        out_specs=[vmem, vmem],
        out_shape=[jax.ShapeDtypeStruct((ori_rows, width), F32), jax.ShapeDtypeStruct((8, width), F32)],
        compiler_params=pltpu.CompilerParams(vmem_limit_bytes=16 * MIB),
        name="local_stats",
    )(*parts, *recvs)
    all_stats = [stats] + [
        lax.ppermute(stats, "cls", [(i, (i + 2 * j) % n_cls) for i in range(n_cls)]) for j in range(1, turns)
    ]
    payload = pl.pallas_call(
        functools.partial(payload_kernel, turns),
        in_specs=[vmem] * (1 + turns),
        out_specs=vmem,
        out_shape=jax.ShapeDtypeStruct((ori_rows + TAIL, width), BF16),
        compiler_params=pltpu.CompilerParams(vmem_limit_bytes=16 * MIB),
        name="payload",
    )(scores, *all_stats)
    payloads = [payload] + [None] * (n - 1)
    fp = bp = payload
    payloads[far] = ring(payload, far)
    for d in range(1, far):
        fp = payloads[d] = ring(fp, 1)
        bp = payloads[n - d] = ring(bp, -1)

    out_shape = [jax.ShapeDtypeStruct((n * ori_rows, 2 * half), BF16), jax.ShapeDtypeStruct((1, rows), F32)]
    posterior = pltpu.VMEM((n * ori_rows, width), BF16)
    if half % LANES == 0:
        w = slices + other_slices
        sums, evidence = pl.pallas_call(
            functools.partial(stream_kernel, n, ori_rows, cycle),
            in_specs=[vmem] * (n + len(w)),
            out_specs=[pl.BlockSpec(memory_space=pl.ANY), vmem],
            out_shape=out_shape,
            scratch_shapes=[posterior, pltpu.VMEM(out_shape[0].shape, BF16), pltpu.SemaphoreType.DMA((2 * CHUNKS,))],
            compiler_params=pltpu.CompilerParams(vmem_limit_bytes=32 * MIB),
            name="class_sums",
        )(*payloads, *w)
        return sums[None], evidence.reshape(rows)
    fixed = lambda i: (0, 0)
    steps = max(1, n // 2)
    w = [
        jnp.concatenate([jnp.where(core == 0, a, b), jnp.where(core == 0, b, a)], axis=1)
        for a, b in zip(slices, other_slices, strict=True)
    ]
    once = lambda x: pl.BlockSpec(x.shape, fixed, pipeline_mode=pl.Buffered(1))
    sums, evidence = pl.pallas_call(
        functools.partial(sums_kernel, n, ori_rows, cycle),
        grid=(steps,),
        in_specs=[once(x) for x in payloads + w],
        out_specs=[pl.BlockSpec((n * ori_rows // steps, 2 * half), lambda i: (i, 0)), pl.BlockSpec((1, rows), fixed)],
        out_shape=out_shape,
        scratch_shapes=[posterior],
        compiler_params=pltpu.CompilerParams(vmem_limit_bytes=62 * MIB),
        name="class_sums",
    )(*payloads, *w)
    return sums[None], evidence.reshape(rows)


def solution(mesh):
    in_specs = (P("ori", None), P("cls", "ori", None), P("cls", "ori"), P("ori", None), P(), P())
    out_specs = (P("cls", None, "ori"), P("ori"))
    return jax.shard_map(body, mesh=mesh, in_specs=in_specs, out_specs=out_specs, check_vma=False)
```

```python
import functools
import math

import jax
import jax.numpy as jnp
from jax import lax
from jax.experimental import pallas as pl
from jax.experimental.pallas import tpu as pltpu
from jax.sharding import PartitionSpec as P

BF16 = jnp.bfloat16
F32 = jnp.float32
MASKED = -1e30
LANES = 128
MIB = 1 << 20
TAIL = 16
CHUNKS = 4


def cycle_of(count):
    deep = math.isqrt(count // 2)
    tall = count // deep
    walk = [(z, 0) for z in range(tall)]
    for z in range(tall - 1, -1, -1):
        cols = list(range(1, deep))
        walk += [(z, y) for y in (cols if (tall - 1 - z) % 2 == 0 else cols[::-1])]
    return [z * deep + y for z, y in walk]


def weight_table(index, noise):
    levels = noise.shape[1]
    row = jnp.concatenate([noise, jnp.zeros((1, LANES - levels), F32)], axis=1)
    table = jnp.broadcast_to(row, index.shape)
    return jnp.take_along_axis(table, index, axis=1, mode="promise_in_bounds")


def at(start, size):
    return pl.ds(pl.multiple_of(start, LANES), size)


def weigh(n, half, pieces, img, w_ref):
    core = lax.axis_index("cls") % 2
    for i in range(n):
        yield i
        for ref, first, start, count in pieces:
            for j in range(0, count, LANES):
                weight = w_ref[pl.ds(((2 * i + core) * half + start + j) // LANES, 1), :]
                wide = img[:, at(first + i * count + j, LANES)].astype(F32) * weight
                ref[:, i * count + j : i * count + j + LANES] = wide.astype(BF16)


def own_kernel(n, wo, ws, img_hbm, index_hbm, noise_hbm, sig_hbm, own_ref, w_ref, img, index, noise, sig, sems):
    cls = lax.axis_index("cls")
    core, side = cls % 2, (cls // 2) % 2
    half = 2 * wo + ws
    small = [(index_hbm, index), (noise_hbm, noise), (sig_hbm, sig)]
    copies = [pltpu.make_async_copy(src, dst, sems.at[n + i]) for i, (src, dst) in enumerate(small)]
    loads = []
    for i in range(n):
        src = img_hbm.at[:, at((2 * i + core) * half + side * wo, wo)]
        loads.append(pltpu.make_async_copy(src, img.at[:, i * wo : (i + 1) * wo], sems.at[i]))
    for copy in copies + loads:
        copy.start()
    for copy in copies:
        copy.wait()
    w_ref[...] = weight_table(index[...], noise[...])
    rows = img.shape[0]
    block = lax.broadcasted_iota(jnp.int32, (LANES, rows), 0)
    listed = block < 0
    for j in range(sig.shape[0]):
        listed = listed | (sig[j : j + 1, :] == block)
    unlisted = jnp.where(listed, 0.0, 1.0).astype(BF16)
    same = lax.broadcasted_iota(jnp.int32, (rows, rows), 0) == lax.broadcasted_iota(jnp.int32, (rows, rows), 1)
    eye = jnp.where(same, 1.0, 0.0).astype(BF16)
    turned = lax.dot_general(eye, unlisted, (((1,), (1,)), ((), ())), preferred_element_type=F32)
    own_ref[:, n * wo :] = turned.astype(BF16)
    for i in weigh(n, half, [(own_ref, 0, side * wo, wo)], img, w_ref):
        loads[i].wait()


def rest_kernel(n, wo, ws, img_hbm, w_ref, oth_ref, shared_ref, img, sems):
    cls = lax.axis_index("cls")
    core, side = cls % 2, (cls // 2) % 2
    half = 2 * wo + ws
    loads = []
    for i in range(n):
        base = (2 * i + core) * half
        for k, start, first, count in ((0, (1 - side) * wo, i * wo, wo), (1, 2 * wo, n * wo + i * ws, ws)):
            src = img_hbm.at[:, at(base + start, count)]
            loads.append(pltpu.make_async_copy(src, img.at[:, first : first + count], sems.at[2 * i + k]))
            loads[-1].start()
    pieces = [(oth_ref, 0, (1 - side) * wo, wo), (shared_ref, n * wo, 2 * wo, ws)]
    for i in weigh(n, half, pieces, img, w_ref):
        loads[2 * i].wait()
        loads[2 * i + 1].wait()


def prep_images(images, weight_of, significant, core, side, wo, ws, n):
    rows = images.shape[0]
    half = 2 * wo + ws
    if wo % LANES == 0:
        index, noise = weight_of
        sig = significant.T
        vmem, somewhere = pl.BlockSpec(memory_space=pltpu.VMEM), pl.BlockSpec(memory_space=pl.ANY)
        own, weight = pl.pallas_call(
            functools.partial(own_kernel, n, wo, ws),
            in_specs=[somewhere] * 4,
            out_specs=[vmem] * 2,
            out_shape=[jax.ShapeDtypeStruct((rows, n * wo + LANES), BF16), jax.ShapeDtypeStruct(index.shape, F32)],
            scratch_shapes=[
                pltpu.VMEM((rows, n * wo), BF16),
                pltpu.VMEM(index.shape, index.dtype),
                pltpu.VMEM(noise.shape, F32),
                pltpu.VMEM(sig.shape, sig.dtype),
                pltpu.SemaphoreType.DMA((n + 3,)),
            ],
            compiler_params=pltpu.CompilerParams(vmem_limit_bytes=61 * MIB),
            name="prep_own_plane",
        )(images, index, noise, sig)
        oth, shared = pl.pallas_call(
            functools.partial(rest_kernel, n, wo, ws),
            in_specs=[somewhere, vmem],
            out_specs=[vmem] * 2,
            out_shape=[jax.ShapeDtypeStruct((rows, n * wo), BF16), jax.ShapeDtypeStruct((rows, n * ws), BF16)],
            scratch_shapes=[pltpu.VMEM((rows, n * (wo + ws)), BF16), pltpu.SemaphoreType.DMA((2 * n,))],
            compiler_params=pltpu.CompilerParams(vmem_limit_bytes=58 * MIB),
            name="prep_rest",
        )(images, weight)
        return own, oth, shared, weight
    weight = full_weights(weight_of)
    weighted = (images.astype(F32) * weight).astype(BF16).reshape(rows, n, 2, half)
    mine = lax.dynamic_index_in_dim(weighted, core, 2, keepdims=False)
    own, oth, shared = cut(mine, side, wo)
    lane = jnp.arange(LANES, dtype=jnp.int32)
    listed = jnp.any(significant[:, :, None] == lane[None, None, :], axis=1)
    return jnp.concatenate([own, jnp.where(listed, 0.0, 1.0).astype(BF16)], axis=1), oth, shared, weight


def full_weights(weight_of):
    index, noise = weight_of
    levels = jnp.arange(noise.shape[1], dtype=jnp.int32)
    return jnp.sum(jnp.where(index.reshape(-1, 1) == levels[None, :], noise, 0.0), axis=1)[None, :]


def cut(mine, side, wo):
    rows, n, _ = mine.shape
    own = lax.dynamic_slice_in_dim(mine, side * wo, wo, 2).reshape(rows, n * wo)
    oth = lax.dynamic_slice_in_dim(mine, (1 - side) * wo, wo, 2).reshape(rows, n * wo)
    return own, oth, mine[:, :, 2 * wo :].reshape(rows, -1)


def split_kernel(wo, ws, n, proj_hbm, keep_ref, send_ref, sems):
    half = 2 * wo + ws
    cls, owner = lax.axis_index("cls"), lax.axis_index("ori")
    core, side = cls % 2, (cls // 2) % 2
    copies = []
    for ref, which in ((send_ref, 1 - core), (keep_ref, core)):
        for i in range(n):
            base = (2 * i + which) * half
            for start, spot, count in (
                (base + side * wo, i * wo, wo),
                (base + 2 * wo, n * wo + LANES + i * ws, ws),
                (base + (1 - side) * wo, n * (wo + ws) + LANES + i * wo, wo),
            ):
                src = proj_hbm.at[0, :, at(start, count)]
                copies.append(pltpu.make_async_copy(src, ref.at[:, spot : spot + count], sems.at[len(copies)]))
                copies[-1].start()
    lane = lax.broadcasted_iota(jnp.int32, (keep_ref.shape[0], LANES), 1)
    gate = jnp.where(lane == owner, MASKED, 0.0).astype(BF16)
    keep_ref[:, n * wo : n * wo + LANES] = gate
    send_ref[:, n * wo : n * wo + LANES] = gate
    for copy in copies:
        copy.wait()


def norm_kernel(wo, ws, n, keep_ref, send_ref, prior_ref, w_ref, bias_ref):
    half = 2 * wo + ws
    cls = lax.axis_index("cls")
    core, side = cls % 2, (cls // 2) % 2
    rows = keep_ref.shape[0]
    total = jnp.zeros((rows, LANES), F32)
    for ref, which in ((keep_ref, core), (send_ref, 1 - core)):
        for i in range(n):
            base = (2 * i + which) * half
            for start, spot, count in (
                (base + side * wo, i * wo, wo),
                (base + 2 * wo, n * wo + LANES + i * ws, ws),
                (base + (1 - side) * wo, n * (wo + ws) + LANES + i * wo, wo),
            ):
                for j in range(0, count, LANES):
                    wide = ref[:, spot + j : spot + j + LANES].astype(F32)
                    total = total + wide * wide * w_ref[pl.ds((start + j) // LANES, 1), :]
    half_norm = 0.5 * jnp.sum(total, axis=1, keepdims=True)
    prior = jnp.concatenate([prior_ref[...], jnp.zeros((1, -rows % LANES), F32)], axis=1)
    spread = (rows, prior.shape[1])
    on_line = lax.broadcasted_iota(jnp.int32, spread, 0) == lax.broadcasted_iota(jnp.int32, spread, 1)
    prior = jnp.sum(jnp.where(on_line, prior, 0.0), axis=1, keepdims=True)
    bias_ref[...] = jnp.broadcast_to(prior - half_norm, bias_ref.shape)


def prep_projections(projections, weight, log_prior, core, side, owner, wo, ws, n):
    rows = projections.shape[1]
    half = 2 * wo + ws
    width = n * half + LANES
    if wo % LANES == 0:
        vmem = pl.BlockSpec(memory_space=pltpu.VMEM)
        keep, send = pl.pallas_call(
            functools.partial(split_kernel, wo, ws, n),
            in_specs=[pl.BlockSpec(memory_space=pl.ANY)],
            out_specs=[vmem] * 2,
            out_shape=[jax.ShapeDtypeStruct((rows, width), BF16)] * 2,
            scratch_shapes=[pltpu.SemaphoreType.DMA((6 * n,))],
            compiler_params=pltpu.CompilerParams(vmem_limit_bytes=54 * MIB),
            cost_estimate=pl.CostEstimate(flops=0, bytes_accessed=4 * projections.size, transcendentals=0),
            name="split_projections",
        )(projections)
        bias = pl.pallas_call(
            functools.partial(norm_kernel, wo, ws, n),
            in_specs=[vmem] * 4,
            out_specs=vmem,
            out_shape=jax.ShapeDtypeStruct((rows, LANES), F32),
            compiler_params=pltpu.CompilerParams(vmem_limit_bytes=16 * MIB),
            cost_estimate=pl.CostEstimate(flops=3 * projections.size, bytes_accessed=2 * projections.size, transcendentals=0),
            name="half_norms",
        )(keep, send, log_prior, weight)
        return keep, send, bias
    projection, prior = projections[0], log_prior.reshape(rows, 1)
    half_norm = 0.5 * jnp.sum(jnp.square(projection.astype(F32)) * weight, axis=1, keepdims=True)
    bias = jnp.broadcast_to(prior - half_norm, (rows, LANES))
    lane = jnp.arange(LANES, dtype=jnp.int32)
    gate = jnp.broadcast_to(jnp.where(lane == owner, MASKED, 0.0).astype(BF16)[None, :], (rows, LANES))
    split = projection.reshape(rows, n, 2, half)
    both = []
    for which in (core, 1 - core):
        own, oth, shared = cut(lax.dynamic_index_in_dim(split, which, 2, keepdims=False), side, wo)
        both.append(jnp.concatenate([own, gate, shared, oth], axis=1))
    return both[0], both[1], bias


def pack_kernel(pieces, *refs):
    arrays, outs = refs[: len(refs) - len(pieces)], refs[len(refs) - len(pieces) :]
    for out, places in zip(outs, pieces, strict=True):
        for k, rows, cols, row, col in places:
            size = (rows.stop - rows.start, cols.stop - cols.start)
            out[row : row + size[0], col : col + size[1]] = arrays[k][rows, cols]


def pack(arrays, shapes, pieces):
    vmem = pl.BlockSpec(memory_space=pltpu.VMEM)
    return pl.pallas_call(
        functools.partial(pack_kernel, pieces),
        in_specs=[vmem] * len(arrays),
        out_specs=[vmem] * len(shapes),
        out_shape=[jax.ShapeDtypeStruct(shape, BF16) for shape in shapes],
        compiler_params=pltpu.CompilerParams(vmem_limit_bytes=8 * MIB),
        name="pack",
    )(*arrays)


def plane_kernel(own_ref, mate_ref, bias_ref, *refs):
    part_ref = refs[-1]
    rows = own_ref.shape[0]
    acc = None
    for start in range(0, refs[0].shape[1], 1024):
        cols = slice(start, min(start + 1024, refs[0].shape[1]))
        x = jnp.concatenate([p[:, cols] for p in refs[:-1]], axis=0)
        p = jnp.concatenate([own_ref[:, cols], mate_ref[:, cols]], axis=0)
        term = lax.dot_general(p, x, (((1,), (1,)), ((), ())), preferred_element_type=F32)
        acc = term if acc is None else acc + term
    part_ref[:rows, :] = acc[:rows] + bias_ref[...]
    part_ref[rows:, :] = acc[rows:]


def plane_scores(own, mate, bias, pieces):
    vmem = pl.BlockSpec(memory_space=pltpu.VMEM)
    rows, count, depth = own.shape[0], sum(p.shape[0] for p in pieces), pieces[0].shape[1]
    return pl.pallas_call(
        plane_kernel,
        in_specs=[vmem] * (3 + len(pieces)),
        out_specs=vmem,
        out_shape=jax.ShapeDtypeStruct((2 * rows, count), F32),
        compiler_params=pltpu.CompilerParams(vmem_limit_bytes=8 * MIB),
        cost_estimate=pl.CostEstimate(flops=4 * rows * count * depth, bytes_accessed=4 * rows * depth, transcendentals=0),
        name="plane_scores",
    )(own, mate, bias, *pieces)


def score_kernel(wo, ws, kinds, aligned, begun, own_ref, mate_ref, bias_ref, *refs):
    count = 1 + max(k for kind in kinds for _, places in kind for k, _ in places)
    pieces, part_ref = refs[:count], refs[count]
    rows = own_ref.shape[0]
    acc = bias_ref[...] if begun else None
    base = sum(width for width, _ in kinds[0]) if begun else 0
    for width, places in [segment for kind in kinds[int(begun) :] for segment in kind]:
        for start in range(0, width, 1024):
            size = min(1024, width - start)
            x = jnp.concatenate([pieces[k][:, c + start : c + start + size] for k, c in places], axis=0)
            cols = slice(base + start, base + start + size)
            p = jnp.concatenate([own_ref[:, cols], mate_ref[:, cols]], axis=0)
            term = lax.dot_general(p, x, (((1,), (1,)), ((), ())), preferred_element_type=F32)
            acc = term if acc is None else acc + term
        base += width
    part_ref[:rows, :] = acc[:rows] if begun else acc[:rows] + bias_ref[...]
    part_ref[rows:, :] = acc[rows:]
    if aligned:
        side, owner = (lax.axis_index("cls") // 2) % 2, lax.axis_index("ori")
        slice_ref = refs[count + 1]
        for kind, spot, size in zip(kinds, (side * wo, 2 * wo, (1 - side) * wo), (wo, ws, wo), strict=True):
            row = 0
            for i in range(len(kind[0][1])):
                k, c = kind[0][1][i]
                high = pieces[k].shape[0]
                own_part = kind[0][0] // size
                if len(kind) == 1 or kind[1][1][i][0] == k:
                    tile = pieces[k][:, at(c + owner * size, size)]
                else:
                    k2, c2 = kind[1][1][i]
                    first = pieces[k][:, at(c + jnp.minimum(owner, own_part - 1) * size, size)]
                    second = pieces[k2][:, at(c2 + jnp.maximum(owner - own_part, 0) * size, size)]
                    tile = jnp.where(owner < own_part, first, second)
                slice_ref[row : row + high, at(spot, size)] = tile
                row += high


def group_scores(own, mate, bias, kinds, wo, ws, begun=False):
    aligned = wo % LANES == 0
    rows = own.shape[0]
    half = 2 * wo + ws
    count = sum(p.shape[0] for p, _ in kinds[0][0][1])
    out = [jax.ShapeDtypeStruct((2 * rows, count), F32)]
    if aligned:
        out.append(jax.ShapeDtypeStruct((count, half), BF16))
    arrays, numbered = [], []
    for kind in kinds:
        numbered.append([])
        for width, places in kind:
            named = []
            for p, c in places:
                if not any(p is q for q in arrays):
                    arrays.append(p)
                named.append(([p is q for q in arrays].index(True), c))
            numbered[-1].append((width, named))
    vmem = pl.BlockSpec(memory_space=pltpu.VMEM)
    got = pl.pallas_call(
        functools.partial(score_kernel, wo, ws, numbered, aligned, begun),
        in_specs=[vmem] * (3 + len(arrays)),
        out_specs=[vmem] * len(out),
        out_shape=out,
        compiler_params=pltpu.CompilerParams(vmem_limit_bytes=8 * MIB),
        cost_estimate=pl.CostEstimate(
            flops=4 * rows * count * own.shape[1], bytes_accessed=4 * own.size + 2 * count * own.shape[1], transcendentals=0
        ),
        name="group_scores",
    )(own, mate, bias, *arrays)
    if aligned:
        return got
    side, owner = (lax.axis_index("cls") // 2) % 2, lax.axis_index("ori")
    cols = []
    for kind, size in zip(kinds, (wo, ws, wo), strict=True):
        sources = zip(*[[p[:, c : c + width] for p, c in places] for width, places in kind], strict=True)
        rows_of = [jnp.concatenate(parts, axis=1) for parts in sources]
        cols.append(jnp.concatenate([lax.dynamic_slice_in_dim(p, owner * size, size, 1) for p in rows_of], axis=0))
    a, c, b = cols
    first, second = jnp.where(side == 0, a, b), jnp.where(side == 0, b, a)
    return got[0], jnp.concatenate([first, second, c], axis=1)


def group_order(n):
    return [(0, n // 2)] + [(d, n - d) for d in range(1, n // 2)]


def stats_kernel(n, *refs):
    groups = n // 2
    parts, recvs = refs[:groups], refs[groups : 2 * groups]
    score_ref, stat_ref = refs[2 * groups :]
    rows = score_ref.shape[0]
    per = parts[0].shape[1] // 2
    for g, pair in enumerate(group_order(n)):
        mine = parts[g][:rows, :] + recvs[g][rows:, :]
        other = parts[g][rows:, :] + recvs[g][:rows, :]
        best = jnp.maximum(jnp.max(mine, axis=0, keepdims=True), jnp.max(other, axis=0, keepdims=True))
        total = jnp.sum(jnp.exp(mine - best), axis=0, keepdims=True) + jnp.sum(jnp.exp(other - best), axis=0, keepdims=True)
        for h, r in enumerate(pair):
            cols, held = slice(r * per, (r + 1) * per), slice(h * per, (h + 1) * per)
            score_ref[:, cols] = mine[:, held]
            stat_ref[0:1, cols] = best[:, held]
            stat_ref[1:2, cols] = total[:, held]
    stat_ref[2:8, :] = jnp.zeros((6, stat_ref.shape[1]), F32)


def payload_kernel(turns, score_ref, *refs):
    stats, out_ref = refs[:turns], refs[turns]
    rows = score_ref.shape[0]
    plane = lax.axis_index("cls") // 2
    best = functools.reduce(jnp.maximum, [s[0:1, :] for s in stats])
    terms = [s[1:2, :] * jnp.exp(s[0:1, :] - best) for s in stats]
    total = None
    for a in range(turns):
        back = lax.rem(plane - a + turns, turns)
        term = sum(jnp.where(back == j, terms[j], 0.0) for j in range(turns))
        total = term if total is None else total + term
    out_ref[:rows, :] = jnp.exp(score_ref[...] - best).astype(BF16)
    left = jnp.concatenate([best, total], axis=0)
    levels = []
    for _ in range(3):
        piece = left.astype(BF16).astype(F32)
        levels.append(piece)
        left = left - piece
    levels.append(jnp.zeros((TAIL - 6, best.shape[1]), F32))
    out_ref[rows:, :] = jnp.concatenate(levels, axis=0).astype(BF16)


def scale_posteriors(n, rows, cycle, payloads, posterior, evidence_ref):
    owner = lax.axis_index("ori")
    spot = sum(jnp.where(owner == o, cycle.index(o), 0) for o in range(n))
    width = payloads[0].shape[1]
    per = width // n
    tops, sums = [], []
    for d in range(n):
        stat = payloads[d][rows:, :].astype(F32)
        stat = jnp.concatenate([stat[0:2] + stat[2:4] + stat[4:6], jnp.zeros((6, width), F32)], axis=0)
        stat = pltpu.roll(stat, per * d, 1) if d else stat
        tops.append(stat[0:1])
        sums.append(stat[1:2])
    best = functools.reduce(jnp.maximum, tops)
    grow = [jnp.exp(t - best) for t in tops]
    total = functools.reduce(lambda a, b: a + b, [s * g for s, g in zip(sums, grow, strict=True)])
    evidence_ref[...] = (best + jnp.log(total))[:, :per]
    for d in range(n):
        wide = payloads[d][:rows, :].astype(F32)
        wide = pltpu.roll(wide, per * d, 1) if d else wide
        back = lax.rem(spot + (n - d), n)
        block = sum(jnp.where(back == p, cycle[p], 0) for p in range(n))
        row = pl.multiple_of(block * rows, 16)
        posterior[pl.ds(row, rows), :] = (wide * (grow[d] / total)).astype(BF16)


def images_in_order(n, w):
    per = w[0].shape[0] // 2
    places = {r: (g, h) for g, pair in enumerate(group_order(n)) for h, r in enumerate(pair)}
    return jnp.concatenate([w[places[r][0]][places[r][1] * per : (places[r][1] + 1) * per, :] for r in range(n)], axis=0)


def stream_kernel(n, rows, cycle, *refs):
    payloads, refs = refs[:n], refs[n:]
    groups = n // 2
    halves = (refs[:groups], refs[groups : 2 * groups])
    out_hbm, evidence_ref, posterior, held, sems = refs[2 * groups :]
    scale_posteriors(n, rows, cycle, payloads, posterior, evidence_ref)
    core = lax.axis_index("cls") % 2
    half = held.shape[1] // 2
    tall = held.shape[0] // CHUNKS
    copies = []
    for h, w in enumerate(halves):
        which = core if h == 0 else 1 - core
        right = images_in_order(n, w)
        for c in range(CHUNKS):
            part, cols = slice(c * tall, (c + 1) * tall), slice(h * half, (h + 1) * half)
            held[part, cols] = jnp.dot(posterior[part, :], right, preferred_element_type=F32).astype(BF16)
            target = out_hbm.at[part, at(which * half, half)]
            copies.append(pltpu.make_async_copy(held.at[part, cols], target, sems.at[len(copies)]))
            copies[-1].start()
    for copy in copies:
        copy.wait()


def sums_kernel(n, rows, cycle, *refs):
    payloads, refs = refs[:n], refs[n:]
    w, (out_ref, evidence_ref, posterior) = refs[:-3], refs[-3:]
    step = pl.program_id(0)

    @pl.when(step == 0)
    def _():
        scale_posteriors(n, rows, cycle, payloads, posterior, evidence_ref)

    left = posterior[pl.ds(pl.multiple_of(step * out_ref.shape[0], 16), out_ref.shape[0]), :]
    out_ref[...] = jnp.dot(left, images_in_order(n, w), preferred_element_type=F32).astype(BF16)


def tie(*values):
    return lax.optimization_barrier(values)


def body(images, projections, log_prior, significant, shell_index, noise_inv):
    n = lax.axis_size("ori")
    n_cls = lax.axis_size("cls")
    turns = n_cls // 2
    owner = lax.axis_index("ori")
    cls = lax.axis_index("cls")
    core, side = cls % 2, (cls // 2) % 2
    rows, freqs = images.shape
    ori_rows = projections.shape[1]
    half = freqs // n // 2
    wo = 3 * half // 10
    ws = half - 2 * wo
    cycle = cycle_of(n)
    far = n // 2

    def ring(x, d):
        return lax.ppermute(x, "ori", [(cycle[i], cycle[(i + d) % n]) for i in range(n)])

    def swap(x):
        return lax.ppermute(x, "cls", [(i, i ^ 1) for i in range(n_cls)])

    def cross(x):
        return lax.ppermute(x, "cls", [(i, i ^ 2) for i in range(n_cls)])

    weight_of = (shell_index.reshape(freqs // LANES, LANES), noise_inv.reshape(1, -1))
    own, oth, shared, weight = prep_images(images, weight_of, significant, core, side, wo, ws, n)
    projections, own = tie(projections, own)
    keep, send, bias = prep_projections(projections, weight, log_prior, core, side, owner, wo, ws, n)

    every = slice(0, rows)
    plane_w, shared_w = n * wo + LANES, n * ws
    plane_cols, cross_cols = slice(0, plane_w), slice(0, n * wo)
    shared_cols = slice(plane_w, plane_w + shared_w)
    f, b = ring(own, 1), ring(own, -1)
    f, b, shared, send = tie(f, b, shared, send)
    whole = slice(0, shared_w)
    mates = swap(send)
    both, x_in = [None], None
    f2, b2, x_in = pack(
        [f, b, shared],
        [(rows, plane_w + shared_w)] * 2 + [(2 * rows, n * wo)],
        [[(i, every, plane_cols, 0, 0), (2, every, whole, 0, plane_w)] for i in (0, 1)]
        + [[(0, every, cross_cols, 0, 0), (1, every, cross_cols, rows, 0)]],
    )
    both = [(f2, b2)]
    parts, slices = [None] * far, [None] * far
    crossed = [None]
    for s in range(1, far - 1):
        f, b = both[-1]
        f, b, x = ring(f, 1), ring(b, -1), cross(x_in)
        if s == 1:
            f, b, x, mates = tie(f, b, x, mates)
        else:
            f, b, x, parts[s - 1], slices[s - 1] = tie(f, b, x, parts[s - 1], slices[s - 1])
        both.append((f, b))
        crossed.append(x)
        kinds = (
            [(plane_w, [(p, 0) for p in both[s - 1]])],
            [(shared_w, [(p, plane_w) for p in both[s]])],
            [(n * wo, [(x, 0)])],
        )
        parts[s], slices[s] = group_scores(keep, mates, bias, kinds, wo, ws)
        if s < far - 2:
            (x_in,) = pack([f, b], [(2 * rows, n * wo)], [[(0, every, cross_cols, 0, 0), (1, every, cross_cols, rows, 0)]])
    half_o, half_s = n // 2 * wo, n // 2 * ws
    rest_o = plane_w - half_o
    x_in, f, b = pack(
        [f, b],
        [(2 * rows, n * wo), (rows, half_o + shared_w), (rows, rest_o + shared_w)],
        [
            [(0, every, cross_cols, 0, 0), (1, every, cross_cols, rows, 0)],
            [(0, every, slice(0, half_o), 0, 0), (0, every, shared_cols, 0, half_o)],
            [(1, every, slice(half_o, plane_w), 0, 0), (1, every, shared_cols, 0, rest_o)],
        ],
    )
    f, b, x = ring(f, 1), ring(b, -1), cross(x_in)
    f, b, x, parts[far - 2], slices[far - 2] = tie(f, b, x, parts[far - 2], slices[far - 2])
    kinds = (
        [(plane_w, [(p, 0) for p in both[far - 2]])],
        [(shared_w, [(f, half_o), (b, rest_o)])],
        [(n * wo, [(x, 0)])],
    )
    parts[far - 1], slices[far - 1] = group_scores(keep, mates, bias, kinds, wo, ws)
    x_in, last, f, b = pack(
        [f, b],
        [(rows, n * wo), (rows, plane_w), (rows, half_s), (rows, half_s)],
        [
            [(0, every, slice(0, half_o), 0, 0), (1, every, slice(0, n * wo - half_o), 0, half_o)],
            [(0, every, slice(0, half_o), 0, 0), (1, every, slice(0, rest_o), 0, half_o)],
            [(0, every, slice(half_o, half_o + half_s), 0, 0)],
            [(1, every, slice(rest_o + half_s, rest_o + shared_w), 0, 0)],
        ],
    )
    f, b, x = ring(f, 1), ring(b, -1), cross(x_in)
    begun = plane_scores(keep, mates, bias, [own, last])
    f, b, x, begun = tie(f, b, x, begun)
    kinds = (
        [(plane_w, [(own, 0), (last, 0)])],
        [(half_s, [(shared, 0), (f, 0)]), (half_s, [(shared, half_s), (b, 0)])],
        [(n * wo, [(oth, 0), (x, 0)])],
    )
    parts[0], slices[0] = group_scores(keep, mates, begun, kinds, wo, ws, True)
    recvs = [swap(p) for p in parts]
    other_slices = [swap(x) for x in slices]

    vmem = pl.BlockSpec(memory_space=pltpu.VMEM)
    width = n * rows
    scores, stats = pl.pallas_call(
        functools.partial(stats_kernel, n),
        in_specs=[vmem] * (2 * far),
        out_specs=[vmem, vmem],
        out_shape=[jax.ShapeDtypeStruct((ori_rows, width), F32), jax.ShapeDtypeStruct((8, width), F32)],
        compiler_params=pltpu.CompilerParams(vmem_limit_bytes=16 * MIB),
        name="local_stats",
    )(*parts, *recvs)
    all_stats = [stats] + [
        lax.ppermute(stats, "cls", [(i, (i + 2 * j) % n_cls) for i in range(n_cls)]) for j in range(1, turns)
    ]
    payload = pl.pallas_call(
        functools.partial(payload_kernel, turns),
        in_specs=[vmem] * (1 + turns),
        out_specs=vmem,
        out_shape=jax.ShapeDtypeStruct((ori_rows + TAIL, width), BF16),
        compiler_params=pltpu.CompilerParams(vmem_limit_bytes=16 * MIB),
        name="payload",
    )(scores, *all_stats)
    payloads = [payload] + [None] * (n - 1)
    fp = bp = payload
    payloads[far] = ring(payload, far)
    for d in range(1, far):
        fp = payloads[d] = ring(fp, 1)
        bp = payloads[n - d] = ring(bp, -1)

    out_shape = [jax.ShapeDtypeStruct((n * ori_rows, 2 * half), BF16), jax.ShapeDtypeStruct((1, rows), F32)]
    posterior = pltpu.VMEM((n * ori_rows, width), BF16)
    if half % LANES == 0:
        w = slices + other_slices
        sums, evidence = pl.pallas_call(
            functools.partial(stream_kernel, n, ori_rows, cycle),
            in_specs=[vmem] * (n + len(w)),
            out_specs=[pl.BlockSpec(memory_space=pl.ANY), vmem],
            out_shape=out_shape,
            scratch_shapes=[posterior, pltpu.VMEM(out_shape[0].shape, BF16), pltpu.SemaphoreType.DMA((2 * CHUNKS,))],
            compiler_params=pltpu.CompilerParams(vmem_limit_bytes=32 * MIB),
            name="class_sums",
        )(*payloads, *w)
        return sums[None], evidence.reshape(rows)
    fixed = lambda i: (0, 0)
    steps = max(1, n // 2)
    w = [
        jnp.concatenate([jnp.where(core == 0, a, b), jnp.where(core == 0, b, a)], axis=1)
        for a, b in zip(slices, other_slices, strict=True)
    ]
    once = lambda x: pl.BlockSpec(x.shape, fixed, pipeline_mode=pl.Buffered(1))
    sums, evidence = pl.pallas_call(
        functools.partial(sums_kernel, n, ori_rows, cycle),
        grid=(steps,),
        in_specs=[once(x) for x in payloads + w],
        out_specs=[pl.BlockSpec((n * ori_rows // steps, 2 * half), lambda i: (i, 0)), pl.BlockSpec((1, rows), fixed)],
        out_shape=out_shape,
        scratch_shapes=[posterior],
        compiler_params=pltpu.CompilerParams(vmem_limit_bytes=62 * MIB),
        name="class_sums",
    )(*payloads, *w)
    return sums[None], evidence.reshape(rows)


def solution(mesh):
    in_specs = (P("ori", None), P("cls", "ori", None), P("cls", "ori"), P("ori", None), P(), P())
    out_specs = (P("cls", None, "ori"), P("ori"))
    return jax.shard_map(body, mesh=mesh, in_specs=in_specs, out_specs=out_specs, check_vma=False)
```

```python
import functools
import math

import jax
import jax.numpy as jnp
from jax import lax
from jax.experimental import pallas as pl
from jax.experimental.pallas import tpu as pltpu
from jax.sharding import PartitionSpec as P

BF16 = jnp.bfloat16
F32 = jnp.float32
MASKED = -1e30
LANES = 128
MIB = 1 << 20
TAIL = 16
CHUNKS = 4


def cycle_of(count):
    deep = math.isqrt(count // 2)
    tall = count // deep
    walk = [(z, 0) for z in range(tall)]
    for z in range(tall - 1, -1, -1):
        cols = list(range(1, deep))
        walk += [(z, y) for y in (cols if (tall - 1 - z) % 2 == 0 else cols[::-1])]
    return [z * deep + y for z, y in walk]


def weight_table(index, noise):
    levels = noise.shape[1]
    row = jnp.concatenate([noise, jnp.zeros((1, LANES - levels), F32)], axis=1)
    table = jnp.broadcast_to(row, index.shape)
    return jnp.take_along_axis(table, index, axis=1, mode="promise_in_bounds")


def at(start, size):
    return pl.ds(pl.multiple_of(start, LANES), size)


def weigh(n, half, pieces, img, w_ref):
    core = lax.axis_index("cls") % 2
    for i in range(n):
        yield i
        for ref, first, start, count in pieces:
            for j in range(0, count, LANES):
                weight = w_ref[pl.ds(((2 * i + core) * half + start + j) // LANES, 1), :]
                wide = img[:, at(first + i * count + j, LANES)].astype(F32) * weight
                ref[:, i * count + j : i * count + j + LANES] = wide.astype(BF16)


def own_kernel(n, wo, ws, img_hbm, index_hbm, noise_hbm, sig_hbm, own_ref, w_ref, img, index, noise, sig, sems):
    cls = lax.axis_index("cls")
    core, side = cls % 2, (cls // 2) % 2
    half = 2 * wo + ws
    small = [(index_hbm, index), (noise_hbm, noise), (sig_hbm, sig)]
    copies = [pltpu.make_async_copy(src, dst, sems.at[n + i]) for i, (src, dst) in enumerate(small)]
    loads = []
    for i in range(n):
        src = img_hbm.at[:, at((2 * i + core) * half + side * wo, wo)]
        loads.append(pltpu.make_async_copy(src, img.at[:, i * wo : (i + 1) * wo], sems.at[i]))
    for copy in copies + loads:
        copy.start()
    for copy in copies:
        copy.wait()
    w_ref[...] = weight_table(index[...], noise[...])
    rows = img.shape[0]
    block = lax.broadcasted_iota(jnp.int32, (LANES, rows), 0)
    listed = block < 0
    for j in range(sig.shape[0]):
        listed = listed | (sig[j : j + 1, :] == block)
    unlisted = jnp.where(listed, 0.0, 1.0).astype(BF16)
    same = lax.broadcasted_iota(jnp.int32, (rows, rows), 0) == lax.broadcasted_iota(jnp.int32, (rows, rows), 1)
    eye = jnp.where(same, 1.0, 0.0).astype(BF16)
    turned = lax.dot_general(eye, unlisted, (((1,), (1,)), ((), ())), preferred_element_type=F32)
    own_ref[:, n * wo :] = turned.astype(BF16)
    for i in weigh(n, half, [(own_ref, 0, side * wo, wo)], img, w_ref):
        loads[i].wait()


def rest_kernel(n, wo, ws, img_hbm, w_ref, oth_ref, shared_ref, img, sems):
    cls = lax.axis_index("cls")
    core, side = cls % 2, (cls // 2) % 2
    half = 2 * wo + ws
    loads = []
    for i in range(n):
        base = (2 * i + core) * half
        for k, start, first, count in ((0, (1 - side) * wo, i * wo, wo), (1, 2 * wo, n * wo + i * ws, ws)):
            src = img_hbm.at[:, at(base + start, count)]
            loads.append(pltpu.make_async_copy(src, img.at[:, first : first + count], sems.at[2 * i + k]))
            loads[-1].start()
    pieces = [(oth_ref, 0, (1 - side) * wo, wo), (shared_ref, n * wo, 2 * wo, ws)]
    for i in weigh(n, half, pieces, img, w_ref):
        loads[2 * i].wait()
        loads[2 * i + 1].wait()


def prep_images(images, weight_of, significant, core, side, wo, ws, n):
    rows = images.shape[0]
    half = 2 * wo + ws
    if wo % LANES == 0:
        index, noise = weight_of
        sig = significant.T
        vmem, somewhere = pl.BlockSpec(memory_space=pltpu.VMEM), pl.BlockSpec(memory_space=pl.ANY)
        own, weight = pl.pallas_call(
            functools.partial(own_kernel, n, wo, ws),
            in_specs=[somewhere] * 4,
            out_specs=[vmem] * 2,
            out_shape=[jax.ShapeDtypeStruct((rows, n * wo + LANES), BF16), jax.ShapeDtypeStruct(index.shape, F32)],
            scratch_shapes=[
                pltpu.VMEM((rows, n * wo), BF16),
                pltpu.VMEM(index.shape, index.dtype),
                pltpu.VMEM(noise.shape, F32),
                pltpu.VMEM(sig.shape, sig.dtype),
                pltpu.SemaphoreType.DMA((n + 3,)),
            ],
            compiler_params=pltpu.CompilerParams(vmem_limit_bytes=61 * MIB),
            name="prep_own_plane",
        )(images, index, noise, sig)
        oth, shared = pl.pallas_call(
            functools.partial(rest_kernel, n, wo, ws),
            in_specs=[somewhere, vmem],
            out_specs=[vmem] * 2,
            out_shape=[jax.ShapeDtypeStruct((rows, n * wo), BF16), jax.ShapeDtypeStruct((rows, n * ws), BF16)],
            scratch_shapes=[pltpu.VMEM((rows, n * (wo + ws)), BF16), pltpu.SemaphoreType.DMA((2 * n,))],
            compiler_params=pltpu.CompilerParams(vmem_limit_bytes=58 * MIB),
            name="prep_rest",
        )(images, weight)
        return own, oth, shared, weight
    weight = full_weights(weight_of)
    weighted = (images.astype(F32) * weight).astype(BF16).reshape(rows, n, 2, half)
    mine = lax.dynamic_index_in_dim(weighted, core, 2, keepdims=False)
    own, oth, shared = cut(mine, side, wo)
    lane = jnp.arange(LANES, dtype=jnp.int32)
    listed = jnp.any(significant[:, :, None] == lane[None, None, :], axis=1)
    return jnp.concatenate([own, jnp.where(listed, 0.0, 1.0).astype(BF16)], axis=1), oth, shared, weight


def full_weights(weight_of):
    index, noise = weight_of
    levels = jnp.arange(noise.shape[1], dtype=jnp.int32)
    return jnp.sum(jnp.where(index.reshape(-1, 1) == levels[None, :], noise, 0.0), axis=1)[None, :]


def cut(mine, side, wo):
    rows, n, _ = mine.shape
    own = lax.dynamic_slice_in_dim(mine, side * wo, wo, 2).reshape(rows, n * wo)
    oth = lax.dynamic_slice_in_dim(mine, (1 - side) * wo, wo, 2).reshape(rows, n * wo)
    return own, oth, mine[:, :, 2 * wo :].reshape(rows, -1)


def split_kernel(wo, ws, n, proj_hbm, keep_ref, send_ref, sems):
    half = 2 * wo + ws
    cls, owner = lax.axis_index("cls"), lax.axis_index("ori")
    core, side = cls % 2, (cls // 2) % 2
    copies = []
    for ref, which in ((send_ref, 1 - core), (keep_ref, core)):
        for i in range(n):
            base = (2 * i + which) * half
            for start, spot, count in (
                (base + side * wo, i * wo, wo),
                (base + 2 * wo, n * wo + LANES + i * ws, ws),
                (base + (1 - side) * wo, n * (wo + ws) + LANES + i * wo, wo),
            ):
                src = proj_hbm.at[0, :, at(start, count)]
                copies.append(pltpu.make_async_copy(src, ref.at[:, spot : spot + count], sems.at[len(copies)]))
                copies[-1].start()
    lane = lax.broadcasted_iota(jnp.int32, (keep_ref.shape[0], LANES), 1)
    gate = jnp.where(lane == owner, MASKED, 0.0).astype(BF16)
    keep_ref[:, n * wo : n * wo + LANES] = gate
    send_ref[:, n * wo : n * wo + LANES] = gate
    for copy in copies:
        copy.wait()


def norm_kernel(wo, ws, n, keep_ref, send_ref, prior_ref, w_ref, bias_ref):
    half = 2 * wo + ws
    cls = lax.axis_index("cls")
    core, side = cls % 2, (cls // 2) % 2
    rows = keep_ref.shape[0]
    total = jnp.zeros((rows, LANES), F32)
    for ref, which in ((keep_ref, core), (send_ref, 1 - core)):
        for i in range(n):
            base = (2 * i + which) * half
            for start, spot, count in (
                (base + side * wo, i * wo, wo),
                (base + 2 * wo, n * wo + LANES + i * ws, ws),
                (base + (1 - side) * wo, n * (wo + ws) + LANES + i * wo, wo),
            ):
                for j in range(0, count, LANES):
                    wide = ref[:, spot + j : spot + j + LANES].astype(F32)
                    total = total + wide * wide * w_ref[pl.ds((start + j) // LANES, 1), :]
    half_norm = 0.5 * jnp.sum(total, axis=1, keepdims=True)
    prior = jnp.concatenate([prior_ref[...], jnp.zeros((1, -rows % LANES), F32)], axis=1)
    spread = (rows, prior.shape[1])
    on_line = lax.broadcasted_iota(jnp.int32, spread, 0) == lax.broadcasted_iota(jnp.int32, spread, 1)
    prior = jnp.sum(jnp.where(on_line, prior, 0.0), axis=1, keepdims=True)
    bias_ref[...] = jnp.broadcast_to(prior - half_norm, bias_ref.shape)


def prep_projections(projections, weight, log_prior, core, side, owner, wo, ws, n):
    rows = projections.shape[1]
    half = 2 * wo + ws
    width = n * half + LANES
    if wo % LANES == 0:
        vmem = pl.BlockSpec(memory_space=pltpu.VMEM)
        keep, send = pl.pallas_call(
            functools.partial(split_kernel, wo, ws, n),
            in_specs=[pl.BlockSpec(memory_space=pl.ANY)],
            out_specs=[vmem] * 2,
            out_shape=[jax.ShapeDtypeStruct((rows, width), BF16)] * 2,
            scratch_shapes=[pltpu.SemaphoreType.DMA((6 * n,))],
            compiler_params=pltpu.CompilerParams(vmem_limit_bytes=54 * MIB),
            cost_estimate=pl.CostEstimate(flops=0, bytes_accessed=4 * projections.size, transcendentals=0),
            name="split_projections",
        )(projections)
        bias = pl.pallas_call(
            functools.partial(norm_kernel, wo, ws, n),
            in_specs=[vmem] * 4,
            out_specs=vmem,
            out_shape=jax.ShapeDtypeStruct((rows, LANES), F32),
            compiler_params=pltpu.CompilerParams(vmem_limit_bytes=16 * MIB),
            cost_estimate=pl.CostEstimate(flops=3 * projections.size, bytes_accessed=2 * projections.size, transcendentals=0),
            name="half_norms",
        )(keep, send, log_prior, weight)
        return keep, send, bias
    projection, prior = projections[0], log_prior.reshape(rows, 1)
    half_norm = 0.5 * jnp.sum(jnp.square(projection.astype(F32)) * weight, axis=1, keepdims=True)
    bias = jnp.broadcast_to(prior - half_norm, (rows, LANES))
    lane = jnp.arange(LANES, dtype=jnp.int32)
    gate = jnp.broadcast_to(jnp.where(lane == owner, MASKED, 0.0).astype(BF16)[None, :], (rows, LANES))
    split = projection.reshape(rows, n, 2, half)
    both = []
    for which in (core, 1 - core):
        own, oth, shared = cut(lax.dynamic_index_in_dim(split, which, 2, keepdims=False), side, wo)
        both.append(jnp.concatenate([own, gate, shared, oth], axis=1))
    return both[0], both[1], bias


def pack_kernel(pieces, *refs):
    arrays, outs = refs[: len(refs) - len(pieces)], refs[len(refs) - len(pieces) :]
    for out, places in zip(outs, pieces, strict=True):
        for k, rows, cols, row, col in places:
            size = (rows.stop - rows.start, cols.stop - cols.start)
            out[row : row + size[0], col : col + size[1]] = arrays[k][rows, cols]


def pack(arrays, shapes, pieces):
    vmem = pl.BlockSpec(memory_space=pltpu.VMEM)
    return pl.pallas_call(
        functools.partial(pack_kernel, pieces),
        in_specs=[vmem] * len(arrays),
        out_specs=[vmem] * len(shapes),
        out_shape=[jax.ShapeDtypeStruct(shape, BF16) for shape in shapes],
        compiler_params=pltpu.CompilerParams(vmem_limit_bytes=8 * MIB),
        name="pack",
    )(*arrays)


def plane_kernel(own_ref, mate_ref, bias_ref, *refs):
    part_ref = refs[-1]
    rows = own_ref.shape[0]
    acc = None
    for start in range(0, refs[0].shape[1], 1024):
        cols = slice(start, min(start + 1024, refs[0].shape[1]))
        x = jnp.concatenate([p[:, cols] for p in refs[:-1]], axis=0)
        p = jnp.concatenate([own_ref[:, cols], mate_ref[:, cols]], axis=0)
        term = lax.dot_general(p, x, (((1,), (1,)), ((), ())), preferred_element_type=F32)
        acc = term if acc is None else acc + term
    part_ref[:rows, :] = acc[:rows] + bias_ref[...]
    part_ref[rows:, :] = acc[rows:]


def plane_scores(own, mate, bias, pieces):
    vmem = pl.BlockSpec(memory_space=pltpu.VMEM)
    rows, count, depth = own.shape[0], sum(p.shape[0] for p in pieces), pieces[0].shape[1]
    return pl.pallas_call(
        plane_kernel,
        in_specs=[vmem] * (3 + len(pieces)),
        out_specs=vmem,
        out_shape=jax.ShapeDtypeStruct((2 * rows, count), F32),
        compiler_params=pltpu.CompilerParams(vmem_limit_bytes=8 * MIB),
        cost_estimate=pl.CostEstimate(flops=4 * rows * count * depth, bytes_accessed=4 * rows * depth, transcendentals=0),
        name="plane_scores",
    )(own, mate, bias, *pieces)


def score_kernel(wo, ws, kinds, aligned, begun, own_ref, mate_ref, bias_ref, *refs):
    count = 1 + max(k for kind in kinds for _, places in kind for k, _ in places)
    pieces, part_ref = refs[:count], refs[count]
    rows = own_ref.shape[0]
    acc = bias_ref[...] if begun else None
    base = sum(width for width, _ in kinds[0]) if begun else 0
    for width, places in [segment for kind in kinds[int(begun) :] for segment in kind]:
        for start in range(0, width, 1024):
            size = min(1024, width - start)
            x = jnp.concatenate([pieces[k][:, c + start : c + start + size] for k, c in places], axis=0)
            cols = slice(base + start, base + start + size)
            p = jnp.concatenate([own_ref[:, cols], mate_ref[:, cols]], axis=0)
            term = lax.dot_general(p, x, (((1,), (1,)), ((), ())), preferred_element_type=F32)
            acc = term if acc is None else acc + term
        base += width
    part_ref[:rows, :] = acc[:rows] if begun else acc[:rows] + bias_ref[...]
    part_ref[rows:, :] = acc[rows:]
    if aligned:
        side, owner = (lax.axis_index("cls") // 2) % 2, lax.axis_index("ori")
        slice_ref = refs[count + 1]
        for kind, spot, size in zip(kinds, (side * wo, 2 * wo, (1 - side) * wo), (wo, ws, wo), strict=True):
            row = 0
            for i in range(len(kind[0][1])):
                k, c = kind[0][1][i]
                high = pieces[k].shape[0]
                own_part = kind[0][0] // size
                if len(kind) == 1 or kind[1][1][i][0] == k:
                    tile = pieces[k][:, at(c + owner * size, size)]
                else:
                    k2, c2 = kind[1][1][i]
                    first = pieces[k][:, at(c + jnp.minimum(owner, own_part - 1) * size, size)]
                    second = pieces[k2][:, at(c2 + jnp.maximum(owner - own_part, 0) * size, size)]
                    tile = jnp.where(owner < own_part, first, second)
                slice_ref[row : row + high, at(spot, size)] = tile
                row += high


def group_scores(own, mate, bias, kinds, wo, ws, begun=False):
    aligned = wo % LANES == 0
    rows = own.shape[0]
    half = 2 * wo + ws
    count = sum(p.shape[0] for p, _ in kinds[0][0][1])
    out = [jax.ShapeDtypeStruct((2 * rows, count), F32)]
    if aligned:
        out.append(jax.ShapeDtypeStruct((count, half), BF16))
    arrays, numbered = [], []
    for kind in kinds:
        numbered.append([])
        for width, places in kind:
            named = []
            for p, c in places:
                if not any(p is q for q in arrays):
                    arrays.append(p)
                named.append(([p is q for q in arrays].index(True), c))
            numbered[-1].append((width, named))
    vmem = pl.BlockSpec(memory_space=pltpu.VMEM)
    got = pl.pallas_call(
        functools.partial(score_kernel, wo, ws, numbered, aligned, begun),
        in_specs=[vmem] * (3 + len(arrays)),
        out_specs=[vmem] * len(out),
        out_shape=out,
        compiler_params=pltpu.CompilerParams(vmem_limit_bytes=8 * MIB),
        cost_estimate=pl.CostEstimate(
            flops=4 * rows * count * own.shape[1], bytes_accessed=4 * own.size + 2 * count * own.shape[1], transcendentals=0
        ),
        name="group_scores",
    )(own, mate, bias, *arrays)
    if aligned:
        return got
    side, owner = (lax.axis_index("cls") // 2) % 2, lax.axis_index("ori")
    cols = []
    for kind, size in zip(kinds, (wo, ws, wo), strict=True):
        sources = zip(*[[p[:, c : c + width] for p, c in places] for width, places in kind], strict=True)
        rows_of = [jnp.concatenate(parts, axis=1) for parts in sources]
        cols.append(jnp.concatenate([lax.dynamic_slice_in_dim(p, owner * size, size, 1) for p in rows_of], axis=0))
    a, c, b = cols
    first, second = jnp.where(side == 0, a, b), jnp.where(side == 0, b, a)
    return got[0], jnp.concatenate([first, second, c], axis=1)


def group_order(n):
    return [(0, n // 2)] + [(d, n - d) for d in range(1, n // 2)]


def stats_kernel(n, *refs):
    groups = n // 2
    parts, recvs = refs[:groups], refs[groups : 2 * groups]
    score_ref, stat_ref = refs[2 * groups :]
    rows = score_ref.shape[0]
    per = parts[0].shape[1] // 2
    for g, pair in enumerate(group_order(n)):
        mine = parts[g][:rows, :] + recvs[g][rows:, :]
        other = parts[g][rows:, :] + recvs[g][:rows, :]
        best = jnp.maximum(jnp.max(mine, axis=0, keepdims=True), jnp.max(other, axis=0, keepdims=True))
        total = jnp.sum(jnp.exp(mine - best), axis=0, keepdims=True) + jnp.sum(jnp.exp(other - best), axis=0, keepdims=True)
        for h, r in enumerate(pair):
            cols, held = slice(r * per, (r + 1) * per), slice(h * per, (h + 1) * per)
            score_ref[:, cols] = mine[:, held]
            stat_ref[0:1, cols] = best[:, held]
            stat_ref[1:2, cols] = total[:, held]
    stat_ref[2:8, :] = jnp.zeros((6, stat_ref.shape[1]), F32)


def payload_kernel(turns, score_ref, *refs):
    stats, out_ref = refs[:turns], refs[turns]
    rows = score_ref.shape[0]
    plane = lax.axis_index("cls") // 2
    best = functools.reduce(jnp.maximum, [s[0:1, :] for s in stats])
    terms = [s[1:2, :] * jnp.exp(s[0:1, :] - best) for s in stats]
    total = None
    for a in range(turns):
        back = lax.rem(plane - a + turns, turns)
        term = sum(jnp.where(back == j, terms[j], 0.0) for j in range(turns))
        total = term if total is None else total + term
    out_ref[:rows, :] = jnp.exp(score_ref[...] - best).astype(BF16)
    left = jnp.concatenate([best, total], axis=0)
    levels = []
    for _ in range(3):
        piece = left.astype(BF16).astype(F32)
        levels.append(piece)
        left = left - piece
    levels.append(jnp.zeros((TAIL - 6, best.shape[1]), F32))
    out_ref[rows:, :] = jnp.concatenate(levels, axis=0).astype(BF16)


def payload_rows(n, payloads, d, held):
    if d == n // 2:
        row = jnp.concatenate([ref[held, :] for ref in payloads[n - 1 :]], axis=1)
    else:
        row = payloads[d - int(d > n // 2)][held, :]
    row = row.astype(F32)
    return pltpu.roll(row, row.shape[1] // n * d, 1) if d else row


def scale_posteriors(n, rows, cycle, payloads, posterior, evidence_ref):
    owner = lax.axis_index("ori")
    spot = sum(jnp.where(owner == o, cycle.index(o), 0) for o in range(n))
    width = payloads[0].shape[1]
    per = width // n
    tops, sums = [], []
    for d in range(n):
        stat = payload_rows(n, payloads, d, slice(rows, rows + TAIL))
        stat = stat[0:2] + stat[2:4] + stat[4:6]
        tops.append(stat[0:1])
        sums.append(stat[1:2])
    best = functools.reduce(jnp.maximum, tops)
    grow = [jnp.exp(t - best) for t in tops]
    total = functools.reduce(lambda a, b: a + b, [s * g for s, g in zip(sums, grow, strict=True)])
    evidence_ref[...] = (best + jnp.log(total))[:, :per]
    for d in range(n):
        wide = payload_rows(n, payloads, d, slice(0, rows))
        back = lax.rem(spot + (n - d), n)
        block = sum(jnp.where(back == p, cycle[p], 0) for p in range(n))
        row = pl.multiple_of(block * rows, 16)
        posterior[pl.ds(row, rows), :] = (wide * (grow[d] / total)).astype(BF16)


def images_in_order(n, w):
    per = w[0].shape[0] // 2
    places = {r: (g, h) for g, pair in enumerate(group_order(n)) for h, r in enumerate(pair)}
    return jnp.concatenate([w[places[r][0]][places[r][1] * per : (places[r][1] + 1) * per, :] for r in range(n)], axis=0)


def stream_kernel(n, rows, cycle, *refs):
    payloads, refs = refs[: n + 1], refs[n + 1 :]
    groups = n // 2
    halves = (refs[:groups], refs[groups : 2 * groups])
    out_hbm, evidence_ref, posterior, held, sems = refs[2 * groups :]
    scale_posteriors(n, rows, cycle, payloads, posterior, evidence_ref)
    core = lax.axis_index("cls") % 2
    half = held.shape[1] // 2
    tall = held.shape[0] // CHUNKS
    copies = []
    for h, w in enumerate(halves):
        which = core if h == 0 else 1 - core
        right = images_in_order(n, w)
        for c in range(CHUNKS):
            part, cols = slice(c * tall, (c + 1) * tall), slice(h * half, (h + 1) * half)
            held[part, cols] = jnp.dot(posterior[part, :], right, preferred_element_type=F32).astype(BF16)
            target = out_hbm.at[part, at(which * half, half)]
            copies.append(pltpu.make_async_copy(held.at[part, cols], target, sems.at[len(copies)]))
            copies[-1].start()
    for copy in copies:
        copy.wait()


def sums_kernel(n, rows, cycle, *refs):
    payloads, refs = refs[: n + 1], refs[n + 1 :]
    w, (out_ref, evidence_ref, posterior) = refs[:-3], refs[-3:]
    step = pl.program_id(0)

    @pl.when(step == 0)
    def _():
        scale_posteriors(n, rows, cycle, payloads, posterior, evidence_ref)

    left = posterior[pl.ds(pl.multiple_of(step * out_ref.shape[0], 16), out_ref.shape[0]), :]
    out_ref[...] = jnp.dot(left, images_in_order(n, w), preferred_element_type=F32).astype(BF16)


def tie(*values):
    return lax.optimization_barrier(values)


def body(images, projections, log_prior, significant, shell_index, noise_inv):
    n = lax.axis_size("ori")
    n_cls = lax.axis_size("cls")
    turns = n_cls // 2
    owner = lax.axis_index("ori")
    cls = lax.axis_index("cls")
    core, side = cls % 2, (cls // 2) % 2
    rows, freqs = images.shape
    ori_rows = projections.shape[1]
    half = freqs // n // 2
    wo = 3 * half // 10
    ws = half - 2 * wo
    cycle = cycle_of(n)
    far = n // 2

    def ring(x, d):
        return lax.ppermute(x, "ori", [(cycle[i], cycle[(i + d) % n]) for i in range(n)])

    def swap(x):
        return lax.ppermute(x, "cls", [(i, i ^ 1) for i in range(n_cls)])

    def cross(x):
        return lax.ppermute(x, "cls", [(i, i ^ 2) for i in range(n_cls)])

    weight_of = (shell_index.reshape(freqs // LANES, LANES), noise_inv.reshape(1, -1))
    own, oth, shared, weight = prep_images(images, weight_of, significant, core, side, wo, ws, n)
    projections, own = tie(projections, own)
    keep, send, bias = prep_projections(projections, weight, log_prior, core, side, owner, wo, ws, n)

    every = slice(0, rows)
    plane_w, shared_w = n * wo + LANES, n * ws
    plane_cols, cross_cols = slice(0, plane_w), slice(0, n * wo)
    shared_cols = slice(plane_w, plane_w + shared_w)
    f, b = ring(own, 1), ring(own, -1)
    f, b, shared, send = tie(f, b, shared, send)
    whole = slice(0, shared_w)
    mates = swap(send)
    both, x_in = [None], None
    f2, b2, x_in = pack(
        [f, b, shared],
        [(rows, plane_w + shared_w)] * 2 + [(2 * rows, n * wo)],
        [[(i, every, plane_cols, 0, 0), (2, every, whole, 0, plane_w)] for i in (0, 1)]
        + [[(0, every, cross_cols, 0, 0), (1, every, cross_cols, rows, 0)]],
    )
    both = [(f2, b2)]
    parts, slices = [None] * far, [None] * far
    crossed = [None]
    for s in range(1, far - 1):
        f, b = both[-1]
        f, b, x = ring(f, 1), ring(b, -1), cross(x_in)
        if s == 1:
            f, b, x, mates = tie(f, b, x, mates)
        else:
            f, b, x, parts[s - 1], slices[s - 1] = tie(f, b, x, parts[s - 1], slices[s - 1])
        both.append((f, b))
        crossed.append(x)
        kinds = (
            [(plane_w, [(p, 0) for p in both[s - 1]])],
            [(shared_w, [(p, plane_w) for p in both[s]])],
            [(n * wo, [(x, 0)])],
        )
        parts[s], slices[s] = group_scores(keep, mates, bias, kinds, wo, ws)
        if s < far - 2:
            (x_in,) = pack([f, b], [(2 * rows, n * wo)], [[(0, every, cross_cols, 0, 0), (1, every, cross_cols, rows, 0)]])
    half_o, half_s = (n // 2 + 2) * wo, n // 2 * ws
    rest_o = plane_w - half_o
    x_in, f, b = pack(
        [f, b],
        [(2 * rows, n * wo), (rows, half_o + shared_w), (rows, rest_o + shared_w)],
        [
            [(0, every, cross_cols, 0, 0), (1, every, cross_cols, rows, 0)],
            [(0, every, slice(0, half_o), 0, 0), (0, every, shared_cols, 0, half_o)],
            [(1, every, slice(half_o, plane_w), 0, 0), (1, every, shared_cols, 0, rest_o)],
        ],
    )
    f, b, x = ring(f, 1), ring(b, -1), cross(x_in)
    f, b, x, parts[far - 2], slices[far - 2] = tie(f, b, x, parts[far - 2], slices[far - 2])
    kinds = (
        [(plane_w, [(p, 0) for p in both[far - 2]])],
        [(shared_w, [(f, half_o), (b, rest_o)])],
        [(n * wo, [(x, 0)])],
    )
    parts[far - 1], slices[far - 1] = group_scores(keep, mates, bias, kinds, wo, ws)
    x_in, last, f, b = pack(
        [f, b],
        [(rows, n * wo), (rows, plane_w), (rows, half_s), (rows, half_s)],
        [
            [(0, every, slice(0, half_o), 0, 0), (1, every, slice(0, n * wo - half_o), 0, half_o)],
            [(0, every, slice(0, half_o), 0, 0), (1, every, slice(0, rest_o), 0, half_o)],
            [(0, every, slice(half_o, half_o + half_s), 0, 0)],
            [(1, every, slice(rest_o + half_s, rest_o + shared_w), 0, 0)],
        ],
    )
    f, b, x = ring(f, 1), ring(b, -1), cross(x_in)
    begun = plane_scores(keep, mates, bias, [own, last])
    f, b, x, begun = tie(f, b, x, begun)
    kinds = (
        [(plane_w, [(own, 0), (last, 0)])],
        [(half_s, [(shared, 0), (f, 0)]), (half_s, [(shared, half_s), (b, 0)])],
        [(n * wo, [(oth, 0), (x, 0)])],
    )
    parts[0], slices[0] = group_scores(keep, mates, begun, kinds, wo, ws, True)
    recvs = [swap(p) for p in parts]
    other_slices = [swap(x) for x in slices]

    vmem = pl.BlockSpec(memory_space=pltpu.VMEM)
    width = n * rows
    scores, stats = pl.pallas_call(
        functools.partial(stats_kernel, n),
        in_specs=[vmem] * (2 * far),
        out_specs=[vmem, vmem],
        out_shape=[jax.ShapeDtypeStruct((ori_rows, width), F32), jax.ShapeDtypeStruct((8, width), F32)],
        compiler_params=pltpu.CompilerParams(vmem_limit_bytes=16 * MIB),
        name="local_stats",
    )(*parts, *recvs)
    all_stats = [stats] + [
        lax.ppermute(stats, "cls", [(i, (i + 2 * j) % n_cls) for i in range(n_cls)]) for j in range(1, turns)
    ]
    payload = pl.pallas_call(
        functools.partial(payload_kernel, turns),
        in_specs=[vmem] * (1 + turns),
        out_specs=vmem,
        out_shape=jax.ShapeDtypeStruct((ori_rows + TAIL, width), BF16),
        compiler_params=pltpu.CompilerParams(vmem_limit_bytes=16 * MIB),
        name="payload",
    )(scores, *all_stats)
    payloads = [payload] + [None] * (n - 1)
    fp = bp = payload
    for d in range(1, far):
        fp = payloads[d] = ring(fp, 1)
        bp = payloads[n - d] = ring(bp, -1)
    tall, half_w = ori_rows + TAIL, width // 2
    every_row = slice(0, tall)
    (fp,) = pack([payloads[far - 2]], [(tall, half_w)], [[(0, every_row, slice(0, half_w), 0, 0)]])
    (bp,) = pack([payloads[far + 2]], [(tall, half_w)], [[(0, every_row, slice(half_w, width), 0, 0)]])
    payloads = payloads[:far] + payloads[far + 1 :] + [ring(fp, 2), ring(bp, -2)]

    out_shape = [jax.ShapeDtypeStruct((n * ori_rows, 2 * half), BF16), jax.ShapeDtypeStruct((1, rows), F32)]
    posterior = pltpu.VMEM((n * ori_rows, width), BF16)
    if half % LANES == 0:
        w = slices + other_slices
        sums, evidence = pl.pallas_call(
            functools.partial(stream_kernel, n, ori_rows, cycle),
            in_specs=[vmem] * (len(payloads) + len(w)),
            out_specs=[pl.BlockSpec(memory_space=pl.ANY), vmem],
            out_shape=out_shape,
            scratch_shapes=[posterior, pltpu.VMEM(out_shape[0].shape, BF16), pltpu.SemaphoreType.DMA((2 * CHUNKS,))],
            compiler_params=pltpu.CompilerParams(vmem_limit_bytes=32 * MIB),
            name="class_sums",
        )(*payloads, *w)
        return sums[None], evidence.reshape(rows)
    fixed = lambda i: (0, 0)
    steps = max(1, n // 2)
    w = [
        jnp.concatenate([jnp.where(core == 0, a, b), jnp.where(core == 0, b, a)], axis=1)
        for a, b in zip(slices, other_slices, strict=True)
    ]
    once = lambda x: pl.BlockSpec(x.shape, fixed, pipeline_mode=pl.Buffered(1))
    sums, evidence = pl.pallas_call(
        functools.partial(sums_kernel, n, ori_rows, cycle),
        grid=(steps,),
        in_specs=[once(x) for x in payloads + w],
        out_specs=[pl.BlockSpec((n * ori_rows // steps, 2 * half), lambda i: (i, 0)), pl.BlockSpec((1, rows), fixed)],
        out_shape=out_shape,
        scratch_shapes=[posterior],
        compiler_params=pltpu.CompilerParams(vmem_limit_bytes=62 * MIB),
        name="class_sums",
    )(*payloads, *w)
    return sums[None], evidence.reshape(rows)


def solution(mesh):
    in_specs = (P("ori", None), P("cls", "ori", None), P("cls", "ori"), P("ori", None), P(), P())
    out_specs = (P("cls", None, "ori"), P("ori"))
    return jax.shard_map(body, mesh=mesh, in_specs=in_specs, out_specs=out_specs, check_vma=False)
```

```python
import functools
import math

import jax
import jax.numpy as jnp
from jax import lax
from jax.experimental import pallas as pl
from jax.experimental.pallas import tpu as pltpu
from jax.sharding import PartitionSpec as P

BF16 = jnp.bfloat16
F32 = jnp.float32
MASKED = -1e30
LANES = 128
MIB = 1 << 20
TAIL = 16
CHUNKS = 4


def cycle_of(count):
    deep = math.isqrt(count // 2)
    tall = count // deep
    walk = [(z, 0) for z in range(tall)]
    for z in range(tall - 1, -1, -1):
        cols = list(range(1, deep))
        walk += [(z, y) for y in (cols if (tall - 1 - z) % 2 == 0 else cols[::-1])]
    return [z * deep + y for z, y in walk]


def weight_table(index, noise):
    levels = noise.shape[1]
    row = jnp.concatenate([noise, jnp.zeros((1, LANES - levels), F32)], axis=1)
    table = jnp.broadcast_to(row, index.shape)
    return jnp.take_along_axis(table, index, axis=1, mode="promise_in_bounds")


def at(start, size):
    return pl.ds(pl.multiple_of(start, LANES), size)


def weigh(n, half, pieces, img, w_ref):
    core = lax.axis_index("cls") % 2
    for i in range(n):
        yield i
        for ref, first, start, count in pieces:
            for j in range(0, count, LANES):
                weight = w_ref[pl.ds(((2 * i + core) * half + start + j) // LANES, 1), :]
                wide = img[:, at(first + i * count + j, LANES)].astype(F32) * weight
                ref[:, i * count + j : i * count + j + LANES] = wide.astype(BF16)


def own_kernel(n, wo, ws, img_hbm, index_hbm, noise_hbm, sig_hbm, own_ref, w_ref, img, index, noise, sig, sems):
    cls = lax.axis_index("cls")
    core, side = cls % 2, (cls // 2) % 2
    half = 2 * wo + ws
    small = [(index_hbm, index), (noise_hbm, noise), (sig_hbm, sig)]
    copies = [pltpu.make_async_copy(src, dst, sems.at[n + i]) for i, (src, dst) in enumerate(small)]
    loads = []
    for i in range(n):
        src = img_hbm.at[:, at((2 * i + core) * half + side * wo, wo)]
        loads.append(pltpu.make_async_copy(src, img.at[:, i * wo : (i + 1) * wo], sems.at[i]))
    for copy in copies + loads:
        copy.start()
    for copy in copies:
        copy.wait()
    w_ref[...] = weight_table(index[...], noise[...])
    rows = img.shape[0]
    block = lax.broadcasted_iota(jnp.int32, (LANES, rows), 0)
    listed = block < 0
    for j in range(sig.shape[0]):
        listed = listed | (sig[j : j + 1, :] == block)
    unlisted = jnp.where(listed, 0.0, 1.0).astype(BF16)
    same = lax.broadcasted_iota(jnp.int32, (rows, rows), 0) == lax.broadcasted_iota(jnp.int32, (rows, rows), 1)
    eye = jnp.where(same, 1.0, 0.0).astype(BF16)
    turned = lax.dot_general(eye, unlisted, (((1,), (1,)), ((), ())), preferred_element_type=F32)
    own_ref[:, n * wo :] = turned.astype(BF16)
    for i in weigh(n, half, [(own_ref, 0, side * wo, wo)], img, w_ref):
        loads[i].wait()


def rest_kernel(n, wo, ws, img_hbm, w_ref, oth_ref, shared_ref, img, sems):
    cls = lax.axis_index("cls")
    core, side = cls % 2, (cls // 2) % 2
    half = 2 * wo + ws
    loads = []
    for i in range(n):
        base = (2 * i + core) * half
        for k, start, first, count in ((0, (1 - side) * wo, i * wo, wo), (1, 2 * wo, n * wo + i * ws, ws)):
            src = img_hbm.at[:, at(base + start, count)]
            loads.append(pltpu.make_async_copy(src, img.at[:, first : first + count], sems.at[2 * i + k]))
            loads[-1].start()
    pieces = [(oth_ref, 0, (1 - side) * wo, wo), (shared_ref, n * wo, 2 * wo, ws)]
    for i in weigh(n, half, pieces, img, w_ref):
        loads[2 * i].wait()
        loads[2 * i + 1].wait()


def prep_images(images, weight_of, significant, core, side, wo, ws, n):
    rows = images.shape[0]
    half = 2 * wo + ws
    if wo % LANES == 0:
        index, noise = weight_of
        sig = significant.T
        vmem, somewhere = pl.BlockSpec(memory_space=pltpu.VMEM), pl.BlockSpec(memory_space=pl.ANY)
        own, weight = pl.pallas_call(
            functools.partial(own_kernel, n, wo, ws),
            in_specs=[somewhere] * 4,
            out_specs=[vmem] * 2,
            out_shape=[jax.ShapeDtypeStruct((rows, n * wo + LANES), BF16), jax.ShapeDtypeStruct(index.shape, F32)],
            scratch_shapes=[
                pltpu.VMEM((rows, n * wo), BF16),
                pltpu.VMEM(index.shape, index.dtype),
                pltpu.VMEM(noise.shape, F32),
                pltpu.VMEM(sig.shape, sig.dtype),
                pltpu.SemaphoreType.DMA((n + 3,)),
            ],
            compiler_params=pltpu.CompilerParams(vmem_limit_bytes=61 * MIB),
            name="prep_own_plane",
        )(images, index, noise, sig)
        return own, None, None, weight
    weight = full_weights(weight_of)
    weighted = (images.astype(F32) * weight).astype(BF16).reshape(rows, n, 2, half)
    mine = lax.dynamic_index_in_dim(weighted, core, 2, keepdims=False)
    own, oth, shared = cut(mine, side, wo)
    lane = jnp.arange(LANES, dtype=jnp.int32)
    listed = jnp.any(significant[:, :, None] == lane[None, None, :], axis=1)
    return jnp.concatenate([own, jnp.where(listed, 0.0, 1.0).astype(BF16)], axis=1), oth, shared, weight


def full_weights(weight_of):
    index, noise = weight_of
    levels = jnp.arange(noise.shape[1], dtype=jnp.int32)
    return jnp.sum(jnp.where(index.reshape(-1, 1) == levels[None, :], noise, 0.0), axis=1)[None, :]


def cut(mine, side, wo):
    rows, n, _ = mine.shape
    own = lax.dynamic_slice_in_dim(mine, side * wo, wo, 2).reshape(rows, n * wo)
    oth = lax.dynamic_slice_in_dim(mine, (1 - side) * wo, wo, 2).reshape(rows, n * wo)
    return own, oth, mine[:, :, 2 * wo :].reshape(rows, -1)


def split_kernel(wo, ws, n, proj_hbm, keep_ref, send_ref, sems, meanwhile):
    half = 2 * wo + ws
    cls, owner = lax.axis_index("cls"), lax.axis_index("ori")
    core, side = cls % 2, (cls // 2) % 2
    copies = []
    for ref, which in ((send_ref, 1 - core), (keep_ref, core)):
        for i in range(n):
            base = (2 * i + which) * half
            for start, spot, count in (
                (base + side * wo, i * wo, wo),
                (base + 2 * wo, n * wo + LANES + i * ws, ws),
                (base + (1 - side) * wo, n * (wo + ws) + LANES + i * wo, wo),
            ):
                src = proj_hbm.at[0, :, at(start, count)]
                copies.append(pltpu.make_async_copy(src, ref.at[:, spot : spot + count], sems.at[len(copies)]))
                copies[-1].start()
    lane = lax.broadcasted_iota(jnp.int32, (keep_ref.shape[0], LANES), 1)
    gate = jnp.where(lane == owner, MASKED, 0.0).astype(BF16)
    keep_ref[:, n * wo : n * wo + LANES] = gate
    send_ref[:, n * wo : n * wo + LANES] = gate
    meanwhile()
    for copy in copies:
        copy.wait()


def prep_kernel(n, wo, ws, img_hbm, proj_hbm, w_ref, oth_ref, shared_ref, keep_ref, send_ref, img, img_sems, sems):
    split_kernel(wo, ws, n, proj_hbm, keep_ref, send_ref, sems, lambda: rest_kernel(n, wo, ws, img_hbm, w_ref, oth_ref, shared_ref, img, img_sems))


def norm_kernel(wo, ws, n, keep_ref, send_ref, prior_ref, w_ref, bias_ref):
    half = 2 * wo + ws
    cls = lax.axis_index("cls")
    core, side = cls % 2, (cls // 2) % 2
    rows = keep_ref.shape[0]
    total = jnp.zeros((rows, LANES), F32)
    for ref, which in ((keep_ref, core), (send_ref, 1 - core)):
        for i in range(n):
            base = (2 * i + which) * half
            for start, spot, count in (
                (base + side * wo, i * wo, wo),
                (base + 2 * wo, n * wo + LANES + i * ws, ws),
                (base + (1 - side) * wo, n * (wo + ws) + LANES + i * wo, wo),
            ):
                for j in range(0, count, LANES):
                    wide = ref[:, spot + j : spot + j + LANES].astype(F32)
                    total = total + wide * wide * w_ref[pl.ds((start + j) // LANES, 1), :]
    half_norm = 0.5 * jnp.sum(total, axis=1, keepdims=True)
    prior = jnp.concatenate([prior_ref[...], jnp.zeros((1, -rows % LANES), F32)], axis=1)
    spread = (rows, prior.shape[1])
    on_line = lax.broadcasted_iota(jnp.int32, spread, 0) == lax.broadcasted_iota(jnp.int32, spread, 1)
    prior = jnp.sum(jnp.where(on_line, prior, 0.0), axis=1, keepdims=True)
    bias_ref[...] = jnp.broadcast_to(prior - half_norm, bias_ref.shape)


def prep_projections(images, projections, weight, log_prior, core, side, owner, wo, ws, n):
    rows = projections.shape[1]
    half = 2 * wo + ws
    width = n * half + LANES
    if wo % LANES == 0:
        vmem = pl.BlockSpec(memory_space=pltpu.VMEM)
        somewhere = pl.BlockSpec(memory_space=pl.ANY)
        pixels = images.shape[0]
        oth, shared, keep, send = pl.pallas_call(
            functools.partial(prep_kernel, n, wo, ws),
            in_specs=[somewhere, somewhere, vmem],
            out_specs=[vmem] * 4,
            out_shape=[jax.ShapeDtypeStruct((pixels, n * w), BF16) for w in (wo, ws)]
            + [jax.ShapeDtypeStruct((rows, width), BF16)] * 2,
            scratch_shapes=[
                pltpu.VMEM((pixels, n * (wo + ws)), BF16),
                pltpu.SemaphoreType.DMA((2 * n,)),
                pltpu.SemaphoreType.DMA((6 * n,)),
            ],
            compiler_params=pltpu.CompilerParams(vmem_limit_bytes=54 * MIB),
            cost_estimate=pl.CostEstimate(flops=0, bytes_accessed=4 * projections.size, transcendentals=0),
            name="prep_rest",
        )(images, projections, weight)
        bias = pl.pallas_call(
            functools.partial(norm_kernel, wo, ws, n),
            in_specs=[vmem] * 4,
            out_specs=vmem,
            out_shape=jax.ShapeDtypeStruct((rows, LANES), F32),
            compiler_params=pltpu.CompilerParams(vmem_limit_bytes=16 * MIB),
            cost_estimate=pl.CostEstimate(flops=3 * projections.size, bytes_accessed=2 * projections.size, transcendentals=0),
            name="half_norms",
        )(keep, send, log_prior, weight)
        return oth, shared, keep, send, bias
    projection, prior = projections[0], log_prior.reshape(rows, 1)
    half_norm = 0.5 * jnp.sum(jnp.square(projection.astype(F32)) * weight, axis=1, keepdims=True)
    bias = jnp.broadcast_to(prior - half_norm, (rows, LANES))
    lane = jnp.arange(LANES, dtype=jnp.int32)
    gate = jnp.broadcast_to(jnp.where(lane == owner, MASKED, 0.0).astype(BF16)[None, :], (rows, LANES))
    split = projection.reshape(rows, n, 2, half)
    both = []
    for which in (core, 1 - core):
        own, oth, shared = cut(lax.dynamic_index_in_dim(split, which, 2, keepdims=False), side, wo)
        both.append(jnp.concatenate([own, gate, shared, oth], axis=1))
    return None, None, both[0], both[1], bias


def pack_kernel(pieces, *refs):
    arrays, outs = refs[: len(refs) - len(pieces)], refs[len(refs) - len(pieces) :]
    for out, places in zip(outs, pieces, strict=True):
        for k, rows, cols, row, col in places:
            size = (rows.stop - rows.start, cols.stop - cols.start)
            out[row : row + size[0], col : col + size[1]] = arrays[k][rows, cols]


def pack(arrays, shapes, pieces):
    vmem = pl.BlockSpec(memory_space=pltpu.VMEM)
    return pl.pallas_call(
        functools.partial(pack_kernel, pieces),
        in_specs=[vmem] * len(arrays),
        out_specs=[vmem] * len(shapes),
        out_shape=[jax.ShapeDtypeStruct(shape, BF16) for shape in shapes],
        compiler_params=pltpu.CompilerParams(vmem_limit_bytes=8 * MIB),
        name="pack",
    )(*arrays)


def plane_kernel(own_ref, mate_ref, bias_ref, *refs):
    part_ref = refs[-1]
    rows = own_ref.shape[0]
    acc = None
    for start in range(0, refs[0].shape[1], 1024):
        cols = slice(start, min(start + 1024, refs[0].shape[1]))
        x = jnp.concatenate([p[:, cols] for p in refs[:-1]], axis=0)
        p = jnp.concatenate([own_ref[:, cols], mate_ref[:, cols]], axis=0)
        term = lax.dot_general(p, x, (((1,), (1,)), ((), ())), preferred_element_type=F32)
        acc = term if acc is None else acc + term
    part_ref[:rows, :] = acc[:rows] + bias_ref[...]
    part_ref[rows:, :] = acc[rows:]


def plane_scores(own, mate, bias, pieces):
    vmem = pl.BlockSpec(memory_space=pltpu.VMEM)
    rows, count, depth = own.shape[0], sum(p.shape[0] for p in pieces), pieces[0].shape[1]
    return pl.pallas_call(
        plane_kernel,
        in_specs=[vmem] * (3 + len(pieces)),
        out_specs=vmem,
        out_shape=jax.ShapeDtypeStruct((2 * rows, count), F32),
        compiler_params=pltpu.CompilerParams(vmem_limit_bytes=8 * MIB),
        cost_estimate=pl.CostEstimate(flops=4 * rows * count * depth, bytes_accessed=4 * rows * depth, transcendentals=0),
        name="plane_scores",
    )(own, mate, bias, *pieces)


def score_kernel(wo, ws, kinds, aligned, begun, own_ref, mate_ref, bias_ref, *refs):
    count = 1 + max(k for kind in kinds for _, places in kind for k, _ in places)
    pieces, part_ref = refs[:count], refs[count]
    rows = own_ref.shape[0]
    acc = bias_ref[...] if begun else None
    base = sum(width for width, _ in kinds[0]) if begun else 0
    for width, places in [segment for kind in kinds[int(begun) :] for segment in kind]:
        for start in range(0, width, 1024):
            size = min(1024, width - start)
            x = jnp.concatenate([pieces[k][:, c + start : c + start + size] for k, c in places], axis=0)
            cols = slice(base + start, base + start + size)
            p = jnp.concatenate([own_ref[:, cols], mate_ref[:, cols]], axis=0)
            term = lax.dot_general(p, x, (((1,), (1,)), ((), ())), preferred_element_type=F32)
            acc = term if acc is None else acc + term
        base += width
    part_ref[:rows, :] = acc[:rows] if begun else acc[:rows] + bias_ref[...]
    part_ref[rows:, :] = acc[rows:]
    if aligned:
        side, owner = (lax.axis_index("cls") // 2) % 2, lax.axis_index("ori")
        slice_ref = refs[count + 1]
        for kind, spot, size in zip(kinds, (side * wo, 2 * wo, (1 - side) * wo), (wo, ws, wo), strict=True):
            row = 0
            for i in range(len(kind[0][1])):
                k, c = kind[0][1][i]
                high = pieces[k].shape[0]
                own_part = kind[0][0] // size
                if len(kind) == 1 or kind[1][1][i][0] == k:
                    tile = pieces[k][:, at(c + owner * size, size)]
                else:
                    k2, c2 = kind[1][1][i]
                    first = pieces[k][:, at(c + jnp.minimum(owner, own_part - 1) * size, size)]
                    second = pieces[k2][:, at(c2 + jnp.maximum(owner - own_part, 0) * size, size)]
                    tile = jnp.where(owner < own_part, first, second)
                slice_ref[row : row + high, at(spot, size)] = tile
                row += high


def group_scores(own, mate, bias, kinds, wo, ws, begun=False):
    aligned = wo % LANES == 0
    rows = own.shape[0]
    half = 2 * wo + ws
    count = sum(p.shape[0] for p, _ in kinds[0][0][1])
    out = [jax.ShapeDtypeStruct((2 * rows, count), F32)]
    if aligned:
        out.append(jax.ShapeDtypeStruct((count, half), BF16))
    arrays, numbered = [], []
    for kind in kinds:
        numbered.append([])
        for width, places in kind:
            named = []
            for p, c in places:
                if not any(p is q for q in arrays):
                    arrays.append(p)
                named.append(([p is q for q in arrays].index(True), c))
            numbered[-1].append((width, named))
    vmem = pl.BlockSpec(memory_space=pltpu.VMEM)
    got = pl.pallas_call(
        functools.partial(score_kernel, wo, ws, numbered, aligned, begun),
        in_specs=[vmem] * (3 + len(arrays)),
        out_specs=[vmem] * len(out),
        out_shape=out,
        compiler_params=pltpu.CompilerParams(vmem_limit_bytes=8 * MIB),
        cost_estimate=pl.CostEstimate(
            flops=4 * rows * count * own.shape[1], bytes_accessed=4 * own.size + 2 * count * own.shape[1], transcendentals=0
        ),
        name="group_scores",
    )(own, mate, bias, *arrays)
    if aligned:
        return got
    side, owner = (lax.axis_index("cls") // 2) % 2, lax.axis_index("ori")
    cols = []
    for kind, size in zip(kinds, (wo, ws, wo), strict=True):
        sources = zip(*[[p[:, c : c + width] for p, c in places] for width, places in kind], strict=True)
        rows_of = [jnp.concatenate(parts, axis=1) for parts in sources]
        cols.append(jnp.concatenate([lax.dynamic_slice_in_dim(p, owner * size, size, 1) for p in rows_of], axis=0))
    a, c, b = cols
    first, second = jnp.where(side == 0, a, b), jnp.where(side == 0, b, a)
    return got[0], jnp.concatenate([first, second, c], axis=1)


def group_order(n):
    return [(0, n // 2)] + [(d, n - d) for d in range(1, n // 2)]


def stats_kernel(n, *refs):
    groups = n // 2
    parts, recvs = refs[:groups], refs[groups : 2 * groups]
    score_ref, stat_ref = refs[2 * groups :]
    rows = score_ref.shape[0]
    per = parts[0].shape[1] // 2
    for g, pair in enumerate(group_order(n)):
        mine = parts[g][:rows, :] + recvs[g][rows:, :]
        other = parts[g][rows:, :] + recvs[g][:rows, :]
        best = jnp.maximum(jnp.max(mine, axis=0, keepdims=True), jnp.max(other, axis=0, keepdims=True))
        total = jnp.sum(jnp.exp(mine - best), axis=0, keepdims=True) + jnp.sum(jnp.exp(other - best), axis=0, keepdims=True)
        for h, r in enumerate(pair):
            cols, held = slice(r * per, (r + 1) * per), slice(h * per, (h + 1) * per)
            score_ref[:, cols] = mine[:, held]
            stat_ref[0:1, cols] = best[:, held]
            stat_ref[1:2, cols] = total[:, held]
    stat_ref[2:8, :] = jnp.zeros((6, stat_ref.shape[1]), F32)


def payload_kernel(turns, score_ref, *refs):
    stats, out_ref = refs[:turns], refs[turns]
    rows = score_ref.shape[0]
    plane = lax.axis_index("cls") // 2
    best = functools.reduce(jnp.maximum, [s[0:1, :] for s in stats])
    terms = [s[1:2, :] * jnp.exp(s[0:1, :] - best) for s in stats]
    total = None
    for a in range(turns):
        back = lax.rem(plane - a + turns, turns)
        term = sum(jnp.where(back == j, terms[j], 0.0) for j in range(turns))
        total = term if total is None else total + term
    out_ref[:rows, :] = jnp.exp(score_ref[...] - best).astype(BF16)
    left = jnp.concatenate([best, total], axis=0)
    levels = []
    for _ in range(3):
        piece = left.astype(BF16).astype(F32)
        levels.append(piece)
        left = left - piece
    levels.append(jnp.zeros((TAIL - 6, best.shape[1]), F32))
    out_ref[rows:, :] = jnp.concatenate(levels, axis=0).astype(BF16)


def scale_posteriors(n, rows, cycle, payloads, posterior, evidence_ref):
    owner = lax.axis_index("ori")
    spot = sum(jnp.where(owner == o, cycle.index(o), 0) for o in range(n))
    width = payloads[0].shape[1]
    per = width // n
    tops, sums = [], []
    for d in range(n):
        stat = payloads[d][rows:, :].astype(F32)
        stat = jnp.concatenate([stat[0:2] + stat[2:4] + stat[4:6], jnp.zeros((6, width), F32)], axis=0)
        stat = pltpu.roll(stat, per * d, 1) if d else stat
        tops.append(stat[0:1])
        sums.append(stat[1:2])
    best = functools.reduce(jnp.maximum, tops)
    grow = [jnp.exp(t - best) for t in tops]
    total = functools.reduce(lambda a, b: a + b, [s * g for s, g in zip(sums, grow, strict=True)])
    evidence_ref[...] = (best + jnp.log(total))[:, :per]
    for d in range(n):
        wide = payloads[d][:rows, :].astype(F32)
        wide = pltpu.roll(wide, per * d, 1) if d else wide
        back = lax.rem(spot + (n - d), n)
        block = sum(jnp.where(back == p, cycle[p], 0) for p in range(n))
        row = pl.multiple_of(block * rows, 16)
        posterior[pl.ds(row, rows), :] = (wide * (grow[d] / total)).astype(BF16)


def images_in_order(n, w):
    per = w[0].shape[0] // 2
    places = {r: (g, h) for g, pair in enumerate(group_order(n)) for h, r in enumerate(pair)}
    return jnp.concatenate([w[places[r][0]][places[r][1] * per : (places[r][1] + 1) * per, :] for r in range(n)], axis=0)


def stream_kernel(n, rows, cycle, *refs):
    payloads, refs = refs[:n], refs[n:]
    groups = n // 2
    halves = (refs[:groups], refs[groups : 2 * groups])
    out_hbm, evidence_ref, posterior, held, sems = refs[2 * groups :]
    scale_posteriors(n, rows, cycle, payloads, posterior, evidence_ref)
    core = lax.axis_index("cls") % 2
    half = held.shape[1] // 2
    tall = held.shape[0] // CHUNKS
    copies = []
    for h, w in enumerate(halves):
        which = core if h == 0 else 1 - core
        right = images_in_order(n, w)
        for c in range(CHUNKS):
            part, cols = slice(c * tall, (c + 1) * tall), slice(h * half, (h + 1) * half)
            held[part, cols] = jnp.dot(posterior[part, :], right, preferred_element_type=F32).astype(BF16)
            target = out_hbm.at[part, at(which * half, half)]
            copies.append(pltpu.make_async_copy(held.at[part, cols], target, sems.at[len(copies)]))
            copies[-1].start()
    for copy in copies:
        copy.wait()


def sums_kernel(n, rows, cycle, *refs):
    payloads, refs = refs[:n], refs[n:]
    w, (out_ref, evidence_ref, posterior) = refs[:-3], refs[-3:]
    step = pl.program_id(0)

    @pl.when(step == 0)
    def _():
        scale_posteriors(n, rows, cycle, payloads, posterior, evidence_ref)

    left = posterior[pl.ds(pl.multiple_of(step * out_ref.shape[0], 16), out_ref.shape[0]), :]
    out_ref[...] = jnp.dot(left, images_in_order(n, w), preferred_element_type=F32).astype(BF16)


def tie(*values):
    return lax.optimization_barrier(values)


def body(images, projections, log_prior, significant, shell_index, noise_inv):
    n = lax.axis_size("ori")
    n_cls = lax.axis_size("cls")
    turns = n_cls // 2
    owner = lax.axis_index("ori")
    cls = lax.axis_index("cls")
    core, side = cls % 2, (cls // 2) % 2
    rows, freqs = images.shape
    ori_rows = projections.shape[1]
    half = freqs // n // 2
    wo = 3 * half // 10
    ws = half - 2 * wo
    cycle = cycle_of(n)
    far = n // 2

    def ring(x, d):
        return lax.ppermute(x, "ori", [(cycle[i], cycle[(i + d) % n]) for i in range(n)])

    def swap(x):
        return lax.ppermute(x, "cls", [(i, i ^ 1) for i in range(n_cls)])

    def cross(x):
        return lax.ppermute(x, "cls", [(i, i ^ 2) for i in range(n_cls)])

    weight_of = (shell_index.reshape(freqs // LANES, LANES), noise_inv.reshape(1, -1))
    own, oth, shared, weight = prep_images(images, weight_of, significant, core, side, wo, ws, n)
    projections, own = tie(projections, own)
    rest_o, rest_s, keep, send, bias = prep_projections(images, projections, weight, log_prior, core, side, owner, wo, ws, n)
    if oth is None:
        oth, shared = rest_o, rest_s

    every = slice(0, rows)
    plane_w, shared_w = n * wo + LANES, n * ws
    plane_cols, cross_cols = slice(0, plane_w), slice(0, n * wo)
    shared_cols = slice(plane_w, plane_w + shared_w)
    f, b = ring(own, 1), ring(own, -1)
    f, b, shared, send = tie(f, b, shared, send)
    whole = slice(0, shared_w)
    mates = swap(send)
    both, x_in = [None], None
    f2, b2, x_in = pack(
        [f, b, shared],
        [(rows, plane_w + shared_w)] * 2 + [(2 * rows, n * wo)],
        [[(i, every, plane_cols, 0, 0), (2, every, whole, 0, plane_w)] for i in (0, 1)]
        + [[(0, every, cross_cols, 0, 0), (1, every, cross_cols, rows, 0)]],
    )
    both = [(f2, b2)]
    parts, slices = [None] * far, [None] * far
    crossed = [None]
    for s in range(1, far - 1):
        f, b = both[-1]
        f, b, x = ring(f, 1), ring(b, -1), cross(x_in)
        if s == 1:
            f, b, x, mates = tie(f, b, x, mates)
        else:
            f, b, x, parts[s - 1], slices[s - 1] = tie(f, b, x, parts[s - 1], slices[s - 1])
        both.append((f, b))
        crossed.append(x)
        kinds = (
            [(plane_w, [(p, 0) for p in both[s - 1]])],
            [(shared_w, [(p, plane_w) for p in both[s]])],
            [(n * wo, [(x, 0)])],
        )
        parts[s], slices[s] = group_scores(keep, mates, bias, kinds, wo, ws)
        if s < far - 2:
            (x_in,) = pack([f, b], [(2 * rows, n * wo)], [[(0, every, cross_cols, 0, 0), (1, every, cross_cols, rows, 0)]])
    half_o, half_s = n // 2 * wo, n // 2 * ws
    rest_o = plane_w - half_o
    x_in, f, b = pack(
        [f, b],
        [(2 * rows, n * wo), (rows, half_o + shared_w), (rows, rest_o + shared_w)],
        [
            [(0, every, cross_cols, 0, 0), (1, every, cross_cols, rows, 0)],
            [(0, every, slice(0, half_o), 0, 0), (0, every, shared_cols, 0, half_o)],
            [(1, every, slice(half_o, plane_w), 0, 0), (1, every, shared_cols, 0, rest_o)],
        ],
    )
    f, b, x = ring(f, 1), ring(b, -1), cross(x_in)
    f, b, x, parts[far - 2], slices[far - 2] = tie(f, b, x, parts[far - 2], slices[far - 2])
    kinds = (
        [(plane_w, [(p, 0) for p in both[far - 2]])],
        [(shared_w, [(f, half_o), (b, rest_o)])],
        [(n * wo, [(x, 0)])],
    )
    parts[far - 1], slices[far - 1] = group_scores(keep, mates, bias, kinds, wo, ws)
    x_in, last, f, b = pack(
        [f, b],
        [(rows, n * wo), (rows, plane_w), (rows, half_s), (rows, half_s)],
        [
            [(0, every, slice(0, half_o), 0, 0), (1, every, slice(0, n * wo - half_o), 0, half_o)],
            [(0, every, slice(0, half_o), 0, 0), (1, every, slice(0, rest_o), 0, half_o)],
            [(0, every, slice(half_o, half_o + half_s), 0, 0)],
            [(1, every, slice(rest_o + half_s, rest_o + shared_w), 0, 0)],
        ],
    )
    f, b, x = ring(f, 1), ring(b, -1), cross(x_in)
    begun = plane_scores(keep, mates, bias, [own, last])
    f, b, x, begun = tie(f, b, x, begun)
    kinds = (
        [(plane_w, [(own, 0), (last, 0)])],
        [(half_s, [(shared, 0), (f, 0)]), (half_s, [(shared, half_s), (b, 0)])],
        [(n * wo, [(oth, 0), (x, 0)])],
    )
    parts[0], slices[0] = group_scores(keep, mates, begun, kinds, wo, ws, True)
    recvs = [swap(p) for p in parts]
    other_slices = [swap(x) for x in slices]

    vmem = pl.BlockSpec(memory_space=pltpu.VMEM)
    width = n * rows
    scores, stats = pl.pallas_call(
        functools.partial(stats_kernel, n),
        in_specs=[vmem] * (2 * far),
        out_specs=[vmem, vmem],
        out_shape=[jax.ShapeDtypeStruct((ori_rows, width), F32), jax.ShapeDtypeStruct((8, width), F32)],
        compiler_params=pltpu.CompilerParams(vmem_limit_bytes=16 * MIB),
        name="local_stats",
    )(*parts, *recvs)
    all_stats = [stats] + [
        lax.ppermute(stats, "cls", [(i, (i + 2 * j) % n_cls) for i in range(n_cls)]) for j in range(1, turns)
    ]
    payload = pl.pallas_call(
        functools.partial(payload_kernel, turns),
        in_specs=[vmem] * (1 + turns),
        out_specs=vmem,
        out_shape=jax.ShapeDtypeStruct((ori_rows + TAIL, width), BF16),
        compiler_params=pltpu.CompilerParams(vmem_limit_bytes=16 * MIB),
        name="payload",
    )(scores, *all_stats)
    payloads = [payload] + [None] * (n - 1)
    fp = bp = payload
    payloads[far] = ring(payload, far)
    for d in range(1, far):
        fp = payloads[d] = ring(fp, 1)
        bp = payloads[n - d] = ring(bp, -1)

    out_shape = [jax.ShapeDtypeStruct((n * ori_rows, 2 * half), BF16), jax.ShapeDtypeStruct((1, rows), F32)]
    posterior = pltpu.VMEM((n * ori_rows, width), BF16)
    if half % LANES == 0:
        w = slices + other_slices
        sums, evidence = pl.pallas_call(
            functools.partial(stream_kernel, n, ori_rows, cycle),
            in_specs=[vmem] * (n + len(w)),
            out_specs=[pl.BlockSpec(memory_space=pl.ANY), vmem],
            out_shape=out_shape,
            scratch_shapes=[posterior, pltpu.VMEM(out_shape[0].shape, BF16), pltpu.SemaphoreType.DMA((2 * CHUNKS,))],
            compiler_params=pltpu.CompilerParams(vmem_limit_bytes=32 * MIB),
            name="class_sums",
        )(*payloads, *w)
        return sums[None], evidence.reshape(rows)
    fixed = lambda i: (0, 0)
    steps = max(1, n // 2)
    w = [
        jnp.concatenate([jnp.where(core == 0, a, b), jnp.where(core == 0, b, a)], axis=1)
        for a, b in zip(slices, other_slices, strict=True)
    ]
    once = lambda x: pl.BlockSpec(x.shape, fixed, pipeline_mode=pl.Buffered(1))
    sums, evidence = pl.pallas_call(
        functools.partial(sums_kernel, n, ori_rows, cycle),
        grid=(steps,),
        in_specs=[once(x) for x in payloads + w],
        out_specs=[pl.BlockSpec((n * ori_rows // steps, 2 * half), lambda i: (i, 0)), pl.BlockSpec((1, rows), fixed)],
        out_shape=out_shape,
        scratch_shapes=[posterior],
        compiler_params=pltpu.CompilerParams(vmem_limit_bytes=62 * MIB),
        name="class_sums",
    )(*payloads, *w)
    return sums[None], evidence.reshape(rows)


def solution(mesh):
    in_specs = (P("ori", None), P("cls", "ori", None), P("cls", "ori"), P("ori", None), P(), P())
    out_specs = (P("cls", None, "ori"), P("ori"))
    return jax.shard_map(body, mesh=mesh, in_specs=in_specs, out_specs=out_specs, check_vma=False)
```
